32 devices in a mesh: dp: 8 (over z, x), head: 4 (over y, core).
Axes of the slice: x: 2, y: 2, z: 4, core: 2. Of those that a mesh axis runs over, the one named last changes fastest.
Arguments:
- images: bfloat16 [64, 32, 32, 384], P('dp', 'head'), may hold values from -6 to 6
- noise: bfloat16 [64, 32, 32, 192], P('dp', 'head'), may hold values from -6 to 6
- timesteps: int32 [64], P('dp'), may hold values from 2 to 3999
- extents: int32 [64, 2], P('dp'), may hold values from 1 to 32, as said below
- film_master: float32 [768, 768], P(('dp', 'head')), may hold values from -0.21875 to 0.21875
- conv_master: float32 [6912, 384], P(('dp', 'head')), may hold values from -0.109375 to 0.109375
- qkv_master: float32 [384, 1152], P(('dp', 'head')), may hold values from -0.3125 to 0.3125
- out_master: float32 [384, 384], P(('dp', 'head')), may hold values from -1.25 to 1.25
- gains: float32 [384, 6], P(('dp', 'head')), may hold values from -3 to 4
- film_first: float32 [768, 768], P(('dp', 'head')), may hold values from -7.1525574e-07 to 7.1525574e-07
- film_second: float32 [768, 768], P(('dp', 'head')), may hold values from 1.0427094e-15 to 4.1708377e-15
- conv_first: float32 [6912, 384], P(('dp', 'head')), may hold values from -7.1525574e-07 to 7.1525574e-07
- conv_second: float32 [6912, 384], P(('dp', 'head')), may hold values from 1.0427094e-15 to 4.1708377e-15
- qkv_first: float32 [384, 1152], P(('dp', 'head')), may hold values from -7.1525574e-07 to 7.1525574e-07
- qkv_second: float32 [384, 1152], P(('dp', 'head')), may hold values from 1.0427094e-15 to 4.1708377e-15
- out_first: float32 [384, 384], P(('dp', 'head')), may hold values from -7.1525574e-07 to 7.1525574e-07
- out_second: float32 [384, 384], P(('dp', 'head')), may hold values from 1.0427094e-15 to 4.1708377e-15
- gain_first: float32 [384, 6], P(('dp', 'head')), may hold values from -6.67572e-06 to 6.67572e-06
- gain_second: float32 [384, 6], P(('dp', 'head')), may hold values from 1.04270935e-13 to 4.1708374e-13
Outputs:
- loss_parts: float32 [2], replicated
- grad_norm: float32 [], replicated
- film_new: float32 [768, 768], P(('dp', 'head'))
- film_first_new: float32 [768, 768], P(('dp', 'head'))
- film_second_new: float32 [768, 768], P(('dp', 'head'))
- conv_new: float32 [6912, 384], P(('dp', 'head'))
- conv_first_new: float32 [6912, 384], P(('dp', 'head'))
- conv_second_new: float32 [6912, 384], P(('dp', 'head'))
- qkv_new: float32 [384, 1152], P(('dp', 'head'))
- qkv_first_new: float32 [384, 1152], P(('dp', 'head'))
- qkv_second_new: float32 [384, 1152], P(('dp', 'head'))
- out_new: float32 [384, 384], P(('dp', 'head'))
- out_first_new: float32 [384, 384], P(('dp', 'head'))
- out_second_new: float32 [384, 384], P(('dp', 'head'))
- gains_new: float32 [384, 6], P(('dp', 'head'))
- gain_first_new: float32 [384, 6], P(('dp', 'head'))
- gain_second_new: float32 [384, 6], P(('dp', 'head'))
The draws below stay inside these ranges and needn't reach their ends.
Inputs may be any that keep to these rules, and one draw needn't show every extreme that they name: extents[b] = (h, w): the valid region is the last h rows and the first w columns; samples with b >= 32 are valid everywhere.
All inputs are finite; a program needn't handle non-finite values.
Results may differ from the reference program's by a relative error of at most 0.0075.
Values may be sent and summed in bfloat16 or wider, within the bound.
No kernel may reach another device: no remote copies, remote signals or barrier semaphores. Data moves between devices by JAX's collectives and lax.ppermute only.
A program may use at most 192 MiB of HBM per device.

```python
import math
import jax
import jax.numpy as jnp
from jax import lax

C = 384
E = 768
HEADS = 4
GROUPS = 32
IMG = 32
STEP = 10
TSTEPS = 4000
DH = 96
B = 64


def draw_extents(key, part):
    half_batch = B // 2
    positions = jnp.arange(B, dtype=jnp.int32)
    height_key, width_key = jax.random.split(jax.random.fold_in(key, 11))
    base_height = 1 + IMG * 3 // 4 * positions // half_batch
    height = base_height + jax.random.randint(height_key, (B,), 0, IMG // 4)
    width = jax.random.randint(width_key, (B,), IMG // 2, IMG + 1)
    cropped = positions < half_batch
    height = jnp.where(cropped, height, IMG)
    width = jnp.where(cropped, width, IMG)
    return jnp.stack([height, width], axis=1).astype(jnp.int32)


def draw_gains(key, part):
    first_key, second_key = jax.random.split(jax.random.fold_in(key, 23))
    ramp = jnp.arange(C, dtype=jnp.float32) / (C - 1)
    low_end, high_end = (0.6, 1.8)
    rough = jnp.exp(0.1 * jnp.clip(jax.random.normal(first_key, (C, 3), jnp.float32), -3.0, 3.0))
    shifts = 0.3 * jnp.clip(jax.random.normal(second_key, (C, 3), jnp.float32), -3.0, 3.0)
    scales = (low_end + (high_end - low_end) * ramp)[:, None] * rough
    return jnp.stack([scales[:, 0], shifts[:, 0], scales[:, 1], shifts[:, 1], scales[:, 2], shifts[:, 2]], axis=1).astype(jnp.float32)


def with_ends(values, stream_key, low, top_value):
    longest = values.shape.index(max(values.shape))
    spots = []
    for shift in (0, 1):
        where = [jax.random.randint(jax.random.fold_in(stream_key, axis), (), 0, length) for axis, length in enumerate(values.shape)]
        where[longest] = (where[longest] + shift) % values.shape[longest]
        spots.append(tuple(where))
    return values.at[spots[0]].set(low).at[spots[1]].set(top_value)


def levels(stream_key, extent, shards, low, largest):
    gain, own = 1.0, jax.random.fold_in(stream_key, 6)
    for dim, shards_of in shards:
        draws = jnp.exp(jax.random.uniform(jax.random.fold_in(own, dim), (shards_of,), jnp.float32, low / len(shards), largest / len(shards)))
        gain = gain * jnp.repeat(draws, extent[dim] // shards_of).reshape([-1 if axis == dim else 1 for axis in range(len(extent))])
    return gain


def gaussian(rng, shape, scale, most, pieces=(), kind=jnp.bfloat16):
    drawn = scale * jax.random.normal(rng, shape, jnp.float32)
    if pieces:
        drawn = drawn * levels(rng, shape, pieces, -0.22, 0.18)
    return jnp.clip(drawn, -most, most).astype(kind)


def setup_inputs(seed: int = 0) -> dict:
    seeds = jax.random.split(jax.random.key(seed), 20)
    return {
        "images": gaussian(seeds[0], (B, IMG, IMG, C), 1.0, 6.0, ((0, 8), (1, 4))),
        "noise": gaussian(seeds[1], (B, IMG, IMG, C // 2), 1.0, 6.0, ((0, 8), (1, 4))),
        "timesteps": with_ends(jax.random.randint(seeds[2], (B,), 2, TSTEPS), jax.random.fold_in(seeds[2], 1), 2, TSTEPS - 1).astype(jnp.int32),
        "extents": draw_extents(jax.random.fold_in(seeds[19], 71), 0),
        "film_master": gaussian(seeds[4], (2 * C, E), E ** -0.5, 0.21875, ((0, 32),), jnp.float32),
        "conv_master": gaussian(seeds[5], (18 * C, C), (9 * C) ** -0.5, 0.109375, ((0, 32),), jnp.float32),
        "qkv_master": gaussian(seeds[6], (C, 3 * C), C ** -0.5, 0.3125, ((0, 32),), jnp.float32),
        "out_master": gaussian(seeds[7], (C, C), (C // 16) ** -0.5, 1.25, ((0, 32),), jnp.float32),
        "gains": draw_gains(jax.random.fold_in(seeds[19], 71), 0),
        "film_first": gaussian(seeds[9], (2 * C, E), (0.111 * 0.002 * (2 * C * E + 22 * C * C + 6 * C) ** -0.5), 7.152557373046875e-07, ((0, 32),), jnp.float32),
        "film_second": jnp.clip(jnp.exp(math.log(4.170837666125221e-15) - 1.3862944 * jax.random.uniform(seeds[10], (2 * C, E), jnp.float32) ** levels(seeds[10], (2 * C, E), ((0, 32),), -0.2, 0.2)), 1.0427094165313053e-15, 4.170837666125221e-15),
        "conv_first": gaussian(seeds[11], (18 * C, C), (0.111 * 0.002 * (2 * C * E + 22 * C * C + 6 * C) ** -0.5), 7.152557373046875e-07, ((0, 32),), jnp.float32),
        "conv_second": jnp.clip(jnp.exp(math.log(4.170837666125221e-15) - 1.3862944 * jax.random.uniform(seeds[12], (18 * C, C), jnp.float32) ** levels(seeds[12], (18 * C, C), ((0, 32),), -0.2, 0.2)), 1.0427094165313053e-15, 4.170837666125221e-15),
        "qkv_first": gaussian(seeds[13], (C, 3 * C), (0.111 * 0.002 * (2 * C * E + 22 * C * C + 6 * C) ** -0.5), 7.152557373046875e-07, ((0, 32),), jnp.float32),
        "qkv_second": jnp.clip(jnp.exp(math.log(4.170837666125221e-15) - 1.3862944 * jax.random.uniform(seeds[14], (C, 3 * C), jnp.float32) ** levels(seeds[14], (C, 3 * C), ((0, 32),), -0.2, 0.2)), 1.0427094165313053e-15, 4.170837666125221e-15),
        "out_first": gaussian(seeds[15], (C, C), (0.111 * 0.002 * (2 * C * E + 22 * C * C + 6 * C) ** -0.5), 7.152557373046875e-07, ((0, 32),), jnp.float32),
        "out_second": jnp.clip(jnp.exp(math.log(4.170837666125221e-15) - 1.3862944 * jax.random.uniform(seeds[16], (C, C), jnp.float32) ** levels(seeds[16], (C, C), ((0, 32),), -0.2, 0.2)), 1.0427094165313053e-15, 4.170837666125221e-15),
        "gain_first": gaussian(seeds[17], (C, 6), (1.11 * 0.002 * (2 * C * E + 22 * C * C + 6 * C) ** -0.5), 6.67572021484375e-06, ((0, 32),), jnp.float32),
        "gain_second": jnp.clip(jnp.exp(math.log(4.170837395074678e-13) - 1.3862944 * jax.random.uniform(seeds[18], (C, 6), jnp.float32) ** levels(seeds[18], (C, 6), ((0, 32),), -0.2, 0.2)), 1.0427093487686695e-13, 4.170837395074678e-13),
    }


EPS_NORM = 1e-05
VLB_WEIGHT = 0.001
BETA_ONE = 0.9
BETA_TWO = 0.999
ADAM_EPS = 1e-08
DECAY = 0.01
RATE_MATRIX = 0.05
RATE_GAIN = 0.4
THRESHOLD = 0.002
OFFSET = 0.008

@jax.custom_vjp
def low(v):
    return lax.optimization_barrier(v.astype(jnp.bfloat16)).astype(jnp.float32)

@jax.custom_vjp
def low_back(v):
    return v

def low_keep(v):
    return (low(v), None)

def low_pass(kept, grad):
    return (grad,)

def back_keep(v):
    return (v, None)

def back_low(kept, grad):
    return (low(grad),)
low.defvjp(low_keep, low_pass)
low_back.defvjp(back_keep, back_low)

def matmul_high(left, right):
    return jnp.dot(left, right, precision=lax.Precision.HIGHEST, preferred_element_type=jnp.float32)

def plan(step_ids):
    moment = step_ids.astype(jnp.float32)

    def angle(values):
        return (values / TSTEPS + OFFSET) / (1.0 + OFFSET) * (0.5 * math.pi)
    start = angle(jnp.zeros_like(moment))
    before = angle(moment - 1.0)
    later_angle = angle(moment)
    beta_now = jnp.sin(later_angle - before) * jnp.sin(later_angle + before) / jnp.cos(before) ** 2
    fade_now = jnp.sin(later_angle - start) * jnp.sin(later_angle + start) / jnp.cos(start) ** 2
    fade_prev = jnp.sin(before - start) * jnp.sin(before + start) / jnp.cos(start) ** 2
    log_beta = jnp.log(beta_now)
    log_tilde = jnp.log(beta_now * fade_prev / fade_now)
    factor = beta_now * beta_now / ((1.0 - beta_now) * fade_now)
    return (log_beta, log_tilde, factor)

def embed(step_ids, width):
    half_width = width // 2
    frequency = jnp.exp(-math.log(10000.0) * jnp.arange(half_width, dtype=jnp.float32) / half_width)
    phases = step_ids.astype(jnp.float32)[:, None] * frequency[None, :]
    return jnp.concatenate([jnp.cos(phases), jnp.sin(phases)], axis=1)

def group_norm(values, gain_row, shift_row):
    grouped_vals = values.reshape(values.shape[0], GROUPS, -1)
    group_mean = lax.optimization_barrier(jnp.mean(grouped_vals, axis=(0, 2)))
    square_mean = lax.optimization_barrier(jnp.mean(grouped_vals * grouped_vals, axis=(0, 2)))
    inverse_std = lax.rsqrt(square_mean - group_mean * group_mean + EPS_NORM)
    normed = (grouped_vals - group_mean[None, :, None]) * inverse_std[None, :, None]
    return normed.reshape(values.shape) * gain_row + shift_row

def convolve(hidden, taps):
    pixels = IMG * IMG
    padded = jnp.pad(hidden.reshape(IMG, IMG, C), ((1, 1), (1, 1), (0, 0)))
    summed = jnp.zeros((pixels, C), jnp.float32)
    for tap_index in range(9):
        offset_row, offset_col = (tap_index // 3, tap_index % 3)
        window = padded[offset_row:offset_row + IMG, offset_col:offset_col + IMG].reshape(pixels, C)
        summed = summed + matmul_high(window, taps[tap_index * C:(tap_index + 1) * C])
    return summed

def sample_forward(params, picture, embedded):
    film_w, conv_w, qkv_w, out_w, gain_all = params
    film_w, conv_w, qkv_w, out_w, gain_all = (low(film_w), low(conv_w), low(qkv_w), low(out_w), low(gain_all))
    pixels = IMG * IMG
    film_out = low_back(matmul_high(film_w, low(embedded)))
    source = picture.reshape(pixels, C)
    hidden_one = low(jax.nn.silu(group_norm(source, gain_all[:, 0], gain_all[:, 1])))
    inner = low_back(convolve(hidden_one, conv_w[:9 * C]))
    second_out = group_norm(inner, gain_all[:, 2], gain_all[:, 3])
    hidden_two = low(jax.nn.silu(second_out * (1.0 + film_out[:C]) + film_out[C:]))
    middle = source + low_back(convolve(hidden_two, conv_w[9 * C:]))
    normed = low(group_norm(middle, gain_all[:, 4], gain_all[:, 5]))
    packed = low(low_back(matmul_high(normed, qkv_w))).reshape(pixels, HEADS, 3, DH)
    queries, key_part, value_part = (packed[:, :, 0], packed[:, :, 1], packed[:, :, 2])
    scores = low_back(jnp.einsum('qhd,khd->hqk', queries, key_part, precision=lax.Precision.HIGHEST) * DH ** (-0.5))
    weights_soft = low(jax.nn.softmax(scores, axis=-1))
    mixed = low(low_back(jnp.einsum('hqk,khd->qhd', weights_soft, value_part, precision=lax.Precision.HIGHEST)))
    return middle + low_back(matmul_high(mixed.reshape(pixels, C), out_w))

def pixel_loss(result, target, valid, log_beta, log_tilde, factor, fixed_error):
    half_width = C // 2
    residue = result[:, :half_width] - target
    weight = jax.nn.sigmoid(result[:, half_width:])
    blended = weight * log_beta + (1.0 - weight) * log_tilde
    diverge = 0.5 * (-1.0 + blended - log_tilde + jnp.exp(log_tilde - blended) + factor * fixed_error * fixed_error * jnp.exp(-blended))
    return jnp.sum(valid * (lax.optimization_barrier(jnp.mean(residue * residue, axis=-1)) + VLB_WEIGHT * lax.optimization_barrier(jnp.mean(diverge, axis=-1))))

def adamw(master, gradient, first, second, step_rate, decay_rate, clip_factor):
    gradient = gradient * clip_factor
    first_new = BETA_ONE * first + (1.0 - BETA_ONE) * gradient
    second_new = BETA_TWO * second + (1.0 - BETA_TWO) * gradient * gradient
    ratio = first_new / (1.0 - BETA_ONE ** STEP) / (jnp.sqrt(second_new / (1.0 - BETA_TWO ** STEP)) + ADAM_EPS)
    return (master - step_rate * (ratio + decay_rate * master), first_new, second_new)

def reference(images, noise, timesteps, extents, film_master, conv_master, qkv_master, out_master, gains, film_first, film_second, conv_first, conv_second, qkv_first, qkv_second, out_first, out_second, gain_first, gain_second):
    params = (film_master, conv_master, qkv_master, out_master, gains)
    positions = jnp.arange(IMG, dtype=jnp.int32)
    valid_masks = ((positions[None, :, None] >= IMG - extents[:, 0][:, None, None]) & (positions[None, None, :] < extents[:, 1][:, None, None])).astype(jnp.float32)
    valid_count = jnp.sum(valid_masks)
    log_beta, log_tilde, factor = plan(timesteps)
    embedded_all = jax.nn.silu(embed(timesteps, E))

    def per_sample(carry, item_parts):
        gradients, loss_total = carry
        picture, target, valid, embedded, beta_log, tilde_log, coef = item_parts
        picture = picture.astype(jnp.float32)
        target = target.astype(jnp.float32).reshape(IMG * IMG, C // 2)
        valid = valid.reshape(IMG * IMG)
        result = sample_forward(params, picture, embedded)
        fixed_error = result[:, :C // 2] - target

        def objective(weights_all):
            return pixel_loss(sample_forward(weights_all, picture, embedded), target, valid, beta_log, tilde_log, coef, fixed_error)
        loss_value, pullback = jax.vjp(objective, params)
        gradient, = pullback(1.0 / valid_count)
        gradients = jax.tree.map(jnp.add, gradients, gradient)
        return ((gradients, loss_total + loss_value), None)
    zeros = jax.tree.map(lambda array: jnp.zeros(array.shape, jnp.float32), params)
    (gradients, loss_total), _ = lax.scan(per_sample, (zeros, jnp.zeros((), jnp.float32)), (images, noise, valid_masks, embedded_all, log_beta, log_tilde, factor))
    square_total = jnp.zeros((), jnp.float32)
    for gradient in gradients:
        square_total = square_total + jnp.sum(gradient * gradient)
    grad_norm = jnp.sqrt(square_total)
    clip_factor = jnp.minimum(1.0, THRESHOLD / (grad_norm + 1e-06))
    film_g, conv_g, qkv_g, out_g, gain_g = gradients
    film_res = adamw(film_master, film_g, film_first, film_second, RATE_MATRIX, DECAY, clip_factor)
    conv_res = adamw(conv_master, conv_g, conv_first, conv_second, RATE_MATRIX, DECAY, clip_factor)
    qkv_res = adamw(qkv_master, qkv_g, qkv_first, qkv_second, RATE_MATRIX, DECAY, clip_factor)
    out_res = adamw(out_master, out_g, out_first, out_second, RATE_MATRIX, DECAY, clip_factor)
    gain_res = adamw(gains, gain_g, gain_first, gain_second, RATE_GAIN, 0.0, clip_factor)
    loss_parts = jnp.stack([loss_total, valid_count])
    return (loss_parts, grad_norm, film_res[0], film_res[1], film_res[2], conv_res[0], conv_res[1], conv_res[2], qkv_res[0], qkv_res[1], qkv_res[2], out_res[0], out_res[1], out_res[2], gain_res[0], gain_res[1], gain_res[2])
```

```python
import math

import jax
import jax.numpy as jnp
from jax import lax
from jax.sharding import PartitionSpec as P

HEADS = 4
GROUPS = 32
STEP = 10
TSTEPS = 4000


EPS_NORM = 1e-05
VLB_WEIGHT = 0.001
BETA_ONE = 0.9
BETA_TWO = 0.999
ADAM_EPS = 1e-08
DECAY = 0.01
RATE_MATRIX = 0.05
RATE_GAIN = 0.4
THRESHOLD = 0.002
OFFSET = 0.008


def plan(step_ids):
    moment = step_ids.astype(jnp.float32)

    def angle(values):
        return (values / TSTEPS + OFFSET) / (1.0 + OFFSET) * (0.5 * math.pi)

    start = angle(jnp.zeros_like(moment))
    before = angle(moment - 1.0)
    later_angle = angle(moment)
    beta_now = jnp.sin(later_angle - before) * jnp.sin(later_angle + before) / jnp.cos(before) ** 2
    fade_now = jnp.sin(later_angle - start) * jnp.sin(later_angle + start) / jnp.cos(start) ** 2
    fade_prev = jnp.sin(before - start) * jnp.sin(before + start) / jnp.cos(start) ** 2
    log_beta = jnp.log(beta_now)
    log_tilde = jnp.log(beta_now * fade_prev / fade_now)
    factor = beta_now * beta_now / ((1.0 - beta_now) * fade_now)
    return (log_beta, log_tilde, factor)


def embed(step_ids, width):
    half_width = width // 2
    frequency = jnp.exp(-math.log(10000.0) * jnp.arange(half_width, dtype=jnp.float32) / half_width)
    phases = step_ids.astype(jnp.float32)[:, None] * frequency[None, :]
    return jnp.concatenate([jnp.cos(phases), jnp.sin(phases)], axis=1)


def silu_slope(values):
    sigmoid_vals = jax.nn.sigmoid(values)
    return sigmoid_vals * (1.0 + values * (1.0 - sigmoid_vals))


def bit_count(axis):
    size = lax.axis_size(axis)
    count = size.bit_length() - 1
    assert size == 1 << count
    return count


def flip(values, axis, bit):
    size = lax.axis_size(axis)
    return lax.ppermute(values, axis, [(i, i ^ (1 << bit)) for i in range(size)])


def my_bit(axis, bit):
    return (lax.axis_index(axis) >> bit) & 1


def all_bits():
    return [(axis, bit) for axis in ("dp", "head") for bit in reversed(range(bit_count(axis)))]


def gather_bits(block, order):
    rank = {name: place for place, name in enumerate(all_bits())}
    shape = block.shape
    held = []
    for name in order:
        other = flip(block, *name)
        place = sum(rank[have] < rank[name] for have in held)
        bit = my_bit(*name) == 0
        block = jnp.stack([jnp.where(bit, block, other), jnp.where(bit, other, block)], axis=place)
        held.append(name)
    return block.reshape((-1,) + shape)


def scatter_bits(blocks, order, wire):
    names = sorted(order, key=all_bits().index)
    total = blocks.reshape((2,) * len(names) + blocks.shape[1:])
    for name in order:
        place = names.index(name)
        bit = my_bit(*name)
        keep = lax.dynamic_index_in_dim(total, bit, place, keepdims=False)
        send = lax.dynamic_index_in_dim(total, 1 - bit, place, keepdims=False).astype(wire)
        total = keep + flip(send, *name).astype(keep.dtype)
        names.remove(name)
    return total


def sum_bits(values, order):
    for name in order:
        values = values + flip(values, *name)
    return values


def rows_to_samples(strips):
    parts = lax.axis_size("head")
    rest = strips.shape[1:]
    held = strips.reshape((1, strips.shape[0]) + rest)
    for bit in reversed(range(bit_count("head"))):
        sources, samples = held.shape[:2]
        halves = held.reshape((sources, 2, samples // 2) + rest)
        mine = my_bit("head", bit)
        keep = lax.dynamic_index_in_dim(halves, mine, 1, keepdims=False)
        got = flip(lax.dynamic_index_in_dim(halves, 1 - mine, 1, keepdims=False), "head", bit)
        low = mine == 0
        held = jnp.stack([jnp.where(low, keep, got), jnp.where(low, got, keep)], axis=1)
        held = held.reshape((sources * 2, samples // 2) + rest)
    held = jnp.moveaxis(held, 0, 1)
    return held.reshape((held.shape[0], parts * rest[0]) + rest[1:])


def group_norm(values, gain_row, shift_row):
    samples, pixels, channels = values.shape
    grouped_vals = values.reshape(samples, pixels, GROUPS, channels // GROUPS)
    group_mean = jnp.mean(grouped_vals, axis=(1, 3))
    square_mean = jnp.mean(grouped_vals * grouped_vals, axis=(1, 3))
    inverse_std = lax.rsqrt(square_mean - group_mean * group_mean + EPS_NORM)
    normed = (
        (grouped_vals - group_mean[:, None, :, None]) * inverse_std[:, None, :, None]
    ).reshape(values.shape)
    return (normed * gain_row + shift_row, normed, inverse_std)


def group_norm_back(grad_out, normed, inverse_std, gain_row):
    samples, pixels, channels = grad_out.shape
    scaled = (grad_out * gain_row).reshape(samples, pixels, GROUPS, channels // GROUPS)
    flat_normed = normed.reshape(scaled.shape)
    back_values = (
        scaled
        - jnp.mean(scaled, axis=(1, 3))[:, None, :, None]
        - flat_normed * jnp.mean(scaled * flat_normed, axis=(1, 3))[:, None, :, None]
    ) * inverse_std[:, None, :, None]
    return (
        back_values.reshape(grad_out.shape),
        jnp.sum(grad_out * normed, axis=(0, 1)),
        jnp.sum(grad_out, axis=(0, 1)),
    )


def conv(hidden, taps, flipped):
    channels = taps.shape[-1]
    kernel = taps.reshape(3, 3, channels, channels)
    if flipped:
        kernel = jnp.flip(kernel, (0, 1))
    spec = ("NHWC", "HWOI" if flipped else "HWIO", "NHWC")
    return lax.conv_general_dilated(
        hidden, kernel, (1, 1), "SAME", dimension_numbers=spec, preferred_element_type=jnp.float32
    )


def conv_weights(hidden, grad_b):
    channels = hidden.shape[-1]
    spec = ("CHWN", "IHWO", "HWNC")
    return lax.conv_general_dilated(
        hidden, grad_b, (1, 1), ((1, 1), (1, 1)), dimension_numbers=spec, preferred_element_type=jnp.float32
    ).reshape(9 * channels, channels)


def adamw(master, gradient, first, second, step_rate, decay_rate, clip_factor):
    gradient = gradient * clip_factor
    first_new = BETA_ONE * first + (1.0 - BETA_ONE) * gradient
    second_new = BETA_TWO * second + (1.0 - BETA_TWO) * gradient * gradient
    ratio = (
        first_new
        / (1.0 - BETA_ONE**STEP)
        / (jnp.sqrt(second_new / (1.0 - BETA_TWO**STEP)) + ADAM_EPS)
    )
    return (master - step_rate * (ratio + decay_rate * master), first_new, second_new)


def body(
    images,
    noise,
    timesteps,
    extents,
    film_master,
    conv_master,
    qkv_master,
    out_master,
    gains,
    film_first,
    film_second,
    conv_first,
    conv_second,
    qkv_first,
    qkv_second,
    out_first,
    out_second,
    gain_first,
    gain_second,
):
    devices = lax.axis_size("dp") * lax.axis_size("head")
    device = lax.axis_index("dp") * lax.axis_size("head") + lax.axis_index("head")
    bits = all_bits()
    high, low_bits = bits[0], bits[1:]
    channels = images.shape[-1]
    wide = film_master.shape[1]
    half_width = channels // 2
    head_size = channels // HEADS
    factor_att = head_size ** (-0.5)
    conv_rows = conv_master.shape[0]
    film_rows = film_master.shape[0]
    out_rows = out_master.shape[0]

    local_samples = timesteps.shape[0]
    small = jnp.concatenate(
        [
            gains.reshape(-1),
            extents.astype(jnp.float32).reshape(-1),
            (timesteps // 64).astype(jnp.float32),
            (timesteps % 64).astype(jnp.float32),
        ]
    )
    small = jnp.pad(small, (0, 8 * channels - small.shape[0])).reshape(8, channels)
    block = jnp.concatenate(
        [
            conv_master,
            film_master.reshape(-1, channels),
            qkv_master.reshape(-1, channels),
            out_master,
            small,
        ]
    ).astype(jnp.bfloat16)
    every = gather_bits(block, bits)
    ends = [0]
    for length in (conv_rows, film_rows * wide // channels, 3 * out_rows, out_rows, 8):
        ends.append(ends[-1] + length)
    conv_w, film_w, qkv_w, out_w, smalls = [every[:, lo:hi] for lo, hi in zip(ends, ends[1:])]
    conv_w = conv_w.reshape(-1, channels)
    film_w = film_w.reshape(-1, wide)
    qkv_w = qkv_w.reshape(channels, 3 * channels)
    out_w = out_w.reshape(channels, channels)
    smalls = smalls.reshape(devices, -1).astype(jnp.float32)
    gain_f = smalls[:, : gains.size].reshape(channels, 6)
    dp_smalls = smalls.reshape(lax.axis_size("dp"), lax.axis_size("head"), -1)[:, 0, gains.size :]
    extents_all = dp_smalls[:, : 2 * local_samples].reshape(-1, 2)
    times = dp_smalls[:, 2 * local_samples : 4 * local_samples].reshape(-1, 2, local_samples)
    times_all = (times[:, 0] * 64.0 + times[:, 1]).reshape(-1).astype(jnp.int32)
    divisor = jnp.sum(extents_all[:, 0] * extents_all[:, 1])

    pictures = rows_to_samples(images)
    target = rows_to_samples(noise)
    samples, rows, width_px, _ = pictures.shape
    pixels = rows * width_px
    first = lax.axis_index("head") * samples
    own_times = lax.dynamic_slice_in_dim(timesteps, first, samples)
    own_extents = lax.dynamic_slice_in_dim(extents, first, samples)

    taps_one = conv_w[: 9 * channels]
    taps_two = conv_w[9 * channels :]
    log_beta, log_tilde, factor = plan(own_times)
    embedded_all = jax.nn.silu(embed(times_all, wide)).astype(jnp.bfloat16)
    embedded = jax.nn.silu(embed(own_times, wide)).astype(jnp.bfloat16)
    film_out = lax.dot_general(
        embedded, film_w, (((1,), (1,)), ((), ())), preferred_element_type=jnp.float32
    )
    scale_part = film_out[:, None, :channels]
    shift_part = film_out[:, None, channels:]
    source = pictures.reshape(samples, pixels, channels).astype(jnp.float32)
    first_out, first_normed, first_std = group_norm(source, gain_f[:, 0], gain_f[:, 1])
    hidden_one = jax.nn.silu(first_out).astype(jnp.bfloat16).reshape(pictures.shape)
    inner = conv(hidden_one, taps_one, False).reshape(source.shape)
    second_out, second_normed, second_std = group_norm(inner, gain_f[:, 2], gain_f[:, 3])
    lifted = second_out * (1.0 + scale_part) + shift_part
    hidden_two = jax.nn.silu(lifted).astype(jnp.bfloat16).reshape(pictures.shape)
    middle = source + conv(hidden_two, taps_two, False).reshape(source.shape)
    third_out, third_normed, third_std = group_norm(middle, gain_f[:, 4], gain_f[:, 5])
    normed_b = third_out.astype(jnp.bfloat16)
    packed = jnp.einsum("spc,cf->spf", normed_b, qkv_w, preferred_element_type=jnp.float32)
    packed = packed.astype(jnp.bfloat16).reshape(samples, pixels, HEADS, 3 * head_size)
    packed = jnp.moveaxis(packed, 2, 1).reshape(samples * HEADS, pixels, 3 * head_size)

    def attend(block):
        queries = block[:, :head_size]
        key_part = block[:, head_size : 2 * head_size]
        value_part = block[:, 2 * head_size :]
        scores = (
            jnp.einsum("qd,kd->qk", queries, key_part, preferred_element_type=jnp.float32)
            * factor_att
        )
        row_max = jnp.max(scores, axis=-1, keepdims=True)
        log_total = jnp.log(jnp.sum(jnp.exp(scores - row_max), axis=-1, keepdims=True)) + row_max
        weights_soft = jnp.exp(scores - log_total).astype(jnp.bfloat16)
        mixed = jnp.einsum("qk,kd->qd", weights_soft, value_part, preferred_element_type=jnp.float32)
        return (mixed.astype(jnp.bfloat16), log_total)

    mixed_all, log_totals = lax.map(attend, packed)
    attn_cat = jnp.moveaxis(mixed_all.reshape(samples, HEADS, pixels, head_size), 1, 2)
    attn_cat = attn_cat.reshape(samples, pixels, channels)
    result = middle + jnp.einsum("spc,cd->spd", attn_cat, out_w, preferred_element_type=jnp.float32)
    row_ids = jnp.arange(rows, dtype=jnp.int32)
    col_ids = jnp.arange(width_px, dtype=jnp.int32)
    valid = (
        (
            (row_ids[None, :, None] >= rows - own_extents[:, 0][:, None, None])
            & (col_ids[None, None, :] < own_extents[:, 1][:, None, None])
        )
        .astype(jnp.float32)
        .reshape(samples, pixels)
    )
    residue = result[..., :half_width] - target.reshape(samples, pixels, half_width).astype(jnp.float32)
    weight = jax.nn.sigmoid(result[..., half_width:])
    beta_log = log_beta[:, None, None]
    tilde_log = log_tilde[:, None, None]
    blended = weight * beta_log + (1.0 - weight) * tilde_log
    spread = jnp.exp(tilde_log - blended)
    damped = factor[:, None, None] * residue * residue * jnp.exp(-blended)
    diverge = 0.5 * (-1.0 + blended - tilde_log + spread + damped)
    loss_local = jnp.sum(
        valid * (jnp.mean(residue * residue, axis=-1) + VLB_WEIGHT * jnp.mean(diverge, axis=-1))
    )
    grad_guess = valid[..., None] * 2.0 * residue / (half_width * divisor)
    grad_blend = (
        valid[..., None] * (VLB_WEIGHT / half_width) * 0.5 * (1.0 - spread - damped) / divisor
    )
    grad_raw = grad_blend * (beta_log - tilde_log) * weight * (1.0 - weight)
    grad_result = jnp.concatenate([grad_guess, grad_raw], axis=-1)
    down_b = grad_result.astype(jnp.bfloat16)
    out_grad = jnp.einsum("spc,spd->cd", attn_cat, down_b, preferred_element_type=jnp.float32)
    back_mixed = jnp.einsum(
        "spd,cd->spc", down_b, out_w, preferred_element_type=jnp.float32
    ).astype(jnp.bfloat16)
    back_grouped = jnp.moveaxis(back_mixed.reshape(samples, pixels, HEADS, head_size), 2, 1)
    back_grouped = back_grouped.reshape(samples * HEADS, pixels, head_size)

    def attend_back(parts):
        block, log_total, upstream = parts
        queries = block[:, :head_size]
        key_part = block[:, head_size : 2 * head_size]
        value_part = block[:, 2 * head_size :]
        scores = (
            jnp.einsum("qd,kd->qk", queries, key_part, preferred_element_type=jnp.float32)
            * factor_att
        )
        weights_soft = jnp.exp(scores - log_total)
        grad_value = jnp.einsum(
            "qk,qd->kd", weights_soft.astype(jnp.bfloat16), upstream, preferred_element_type=jnp.float32
        )
        grad_soft = jnp.einsum("qd,kd->qk", upstream, value_part, preferred_element_type=jnp.float32)
        grad_scores = (
            weights_soft * (grad_soft - jnp.sum(weights_soft * grad_soft, axis=-1, keepdims=True))
        ).astype(jnp.bfloat16)
        grad_query = (
            jnp.einsum("qk,kd->qd", grad_scores, key_part, preferred_element_type=jnp.float32)
            * factor_att
        )
        grad_key = (
            jnp.einsum("qk,qd->kd", grad_scores, queries, preferred_element_type=jnp.float32)
            * factor_att
        )
        return jnp.concatenate([grad_query, grad_key, grad_value], axis=-1).astype(jnp.bfloat16)

    grad_grouped = lax.map(attend_back, (packed, log_totals, back_grouped))
    grad_local = jnp.moveaxis(grad_grouped.reshape(samples, HEADS, pixels, 3 * head_size), 1, 2)
    grad_local = grad_local.reshape(samples, pixels, 3 * channels)
    qkv_grad = jnp.einsum("spc,spf->cf", normed_b, grad_local, preferred_element_type=jnp.float32)
    grad_normed = jnp.einsum("spf,cf->spc", grad_local, qkv_w, preferred_element_type=jnp.float32)
    back_middle, gain_three, bias_three = group_norm_back(
        grad_normed, third_normed, third_std, gain_f[:, 4]
    )
    grad_middle = grad_result + back_middle
    grad_two_b = grad_middle.astype(jnp.bfloat16).reshape(pictures.shape)
    conv_two_grad = conv_weights(hidden_two, grad_two_b)
    grad_hidden_two = conv(grad_two_b, taps_two, True).reshape(source.shape)
    grad_lifted = grad_hidden_two * silu_slope(lifted)
    grad_scale = jnp.sum(grad_lifted * second_out, axis=1)
    grad_shift = jnp.sum(grad_lifted, axis=1)
    grad_second = grad_lifted * (1.0 + scale_part)
    back_inner, gain_two, bias_two = group_norm_back(
        grad_second, second_normed, second_std, gain_f[:, 2]
    )
    grad_one_b = back_inner.astype(jnp.bfloat16).reshape(pictures.shape)
    conv_one_grad = conv_weights(hidden_one, grad_one_b)
    grad_hidden_one = conv(grad_one_b, taps_one, True).reshape(source.shape)
    grad_first = grad_hidden_one * silu_slope(first_out)
    gain_one = jnp.sum(grad_first * first_normed, axis=(0, 1))
    bias_one = jnp.sum(grad_first, axis=(0, 1))
    film_grad_b = jnp.concatenate([grad_scale, grad_shift], axis=1).astype(jnp.bfloat16)

    back_order = tuple(reversed(bits))
    early = jnp.concatenate(
        [qkv_grad.reshape(devices, -1, channels), out_grad.reshape(devices, -1, channels)], axis=1
    )
    early = scatter_bits(early, back_order, jnp.bfloat16)
    qkv_g = early[: 3 * out_rows].reshape(qkv_master.shape)
    out_g = early[3 * out_rows :]
    back_low = tuple(reversed(low_bits))
    shares = []
    for part in (conv_two_grad, conv_one_grad):
        shares.append(scatter_bits(part.reshape(-1, conv_rows, channels), back_low, jnp.bfloat16))
    size = lax.axis_size(high[0])
    top = my_bit(*high) == 1
    sent = jnp.where(top, shares[1], shares[0]).astype(jnp.bfloat16)
    conv_g = jnp.where(top, shares[0], shares[1]) + flip(sent, *high).astype(jnp.float32)

    film_all = gather_bits(film_grad_b, bits).reshape(-1, film_grad_b.shape[1])
    film_own = lax.dynamic_slice_in_dim(film_all, device * film_rows, film_rows, axis=1)
    film_g = jnp.einsum("sf,se->fe", film_own, embedded_all, preferred_element_type=jnp.float32)
    gain_grad = jnp.stack([gain_one, bias_one, gain_two, bias_two, gain_three, bias_three], axis=1)
    gain_g = sum_bits(gain_grad, bits).reshape(devices, -1, 6)
    gain_g = lax.dynamic_index_in_dim(gain_g, device, 0, keepdims=False)
    reduced = (film_g, conv_g, qkv_g, out_g, gain_g)
    squares = jnp.zeros((), jnp.float32)
    for gradient in reduced:
        squares = squares + jnp.sum(gradient * gradient)
    totals = sum_bits(jnp.stack([squares, loss_local]), bits)
    grad_norm = jnp.sqrt(totals[0])
    clip_factor = jnp.minimum(1.0, THRESHOLD / (grad_norm + 1e-06))
    film_res = adamw(film_master, film_g, film_first, film_second, RATE_MATRIX, DECAY, clip_factor)
    conv_res = adamw(conv_master, conv_g, conv_first, conv_second, RATE_MATRIX, DECAY, clip_factor)
    qkv_res = adamw(qkv_master, qkv_g, qkv_first, qkv_second, RATE_MATRIX, DECAY, clip_factor)
    out_res = adamw(out_master, out_g, out_first, out_second, RATE_MATRIX, DECAY, clip_factor)
    gain_res = adamw(gains, gain_g, gain_first, gain_second, RATE_GAIN, 0.0, clip_factor)
    loss_parts = jnp.stack([totals[1], divisor])
    return (
        loss_parts,
        grad_norm,
        film_res[0],
        film_res[1],
        film_res[2],
        conv_res[0],
        conv_res[1],
        conv_res[2],
        qkv_res[0],
        qkv_res[1],
        qkv_res[2],
        out_res[0],
        out_res[1],
        out_res[2],
        gain_res[0],
        gain_res[1],
        gain_res[2],
    )


def solution(mesh):
    in_specs = (
        P("dp", "head", None, None),
        P("dp", "head", None, None),
        P("dp"),
        P("dp", None),
        P(("dp", "head"), None),
        P(("dp", "head"), None),
        P(("dp", "head"), None),
        P(("dp", "head"), None),
        P(("dp", "head"), None),
        P(("dp", "head"), None),
        P(("dp", "head"), None),
        P(("dp", "head"), None),
        P(("dp", "head"), None),
        P(("dp", "head"), None),
        P(("dp", "head"), None),
        P(("dp", "head"), None),
        P(("dp", "head"), None),
        P(("dp", "head"), None),
        P(("dp", "head"), None),
    )
    out_specs = (
        P(),
        P(),
        P(("dp", "head"), None),
        P(("dp", "head"), None),
        P(("dp", "head"), None),
        P(("dp", "head"), None),
        P(("dp", "head"), None),
        P(("dp", "head"), None),
        P(("dp", "head"), None),
        P(("dp", "head"), None),
        P(("dp", "head"), None),
        P(("dp", "head"), None),
        P(("dp", "head"), None),
        P(("dp", "head"), None),
        P(("dp", "head"), None),
        P(("dp", "head"), None),
        P(("dp", "head"), None),
    )
    return jax.shard_map(body, mesh=mesh, in_specs=in_specs, out_specs=out_specs, check_vma=False)
```

```python
import math

import jax
import jax.numpy as jnp
import numpy as np
from jax import lax
from jax.experimental import pallas as pl
from jax.experimental.pallas import tpu as pltpu
from jax.sharding import PartitionSpec as P

HEADS = 4
GROUPS = 32
STEP = 10
TSTEPS = 4000


EPS_NORM = 1e-05
VLB_WEIGHT = 0.001
BETA_ONE = 0.9
BETA_TWO = 0.999
ADAM_EPS = 1e-08
DECAY = 0.01
RATE_MATRIX = 0.05
RATE_GAIN = 0.4
THRESHOLD = 0.002
OFFSET = 0.008
LOG2E = math.log2(math.e)
VMEM_LIMIT = 56 << 20


def plan(step_ids):
    moment = step_ids.astype(jnp.float32)

    def angle(values):
        return (values / TSTEPS + OFFSET) / (1.0 + OFFSET) * (0.5 * math.pi)

    start = angle(jnp.zeros_like(moment))
    before = angle(moment - 1.0)
    later_angle = angle(moment)
    beta_now = jnp.sin(later_angle - before) * jnp.sin(later_angle + before) / jnp.cos(before) ** 2
    fade_now = jnp.sin(later_angle - start) * jnp.sin(later_angle + start) / jnp.cos(start) ** 2
    fade_prev = jnp.sin(before - start) * jnp.sin(before + start) / jnp.cos(start) ** 2
    log_beta = jnp.log(beta_now)
    log_tilde = jnp.log(beta_now * fade_prev / fade_now)
    factor = beta_now * beta_now / ((1.0 - beta_now) * fade_now)
    return (log_beta, log_tilde, factor)


def embed(step_ids, width):
    half_width = width // 2
    frequency = jnp.exp(-math.log(10000.0) * jnp.arange(half_width, dtype=jnp.float32) / half_width)
    phases = step_ids.astype(jnp.float32)[:, None] * frequency[None, :]
    return jnp.concatenate([jnp.cos(phases), jnp.sin(phases)], axis=1)


def bit_count(axis):
    size = lax.axis_size(axis)
    count = size.bit_length() - 1
    assert size == 1 << count
    return count


def flip(values, axis, bit):
    size = lax.axis_size(axis)
    return lax.ppermute(values, axis, [(i, i ^ (1 << bit)) for i in range(size)])


def my_bit(axis, bit):
    return (lax.axis_index(axis) >> bit) & 1


def all_bits():
    return [(axis, bit) for axis in ("dp", "head") for bit in reversed(range(bit_count(axis)))]


def paths():
    bits = all_bits()
    top, near = bits[0], ("head", 0)
    far = [("dp", bit) for bit in reversed(range(1, bit_count("dp") - 1))]
    across = [("head", bit) for bit in reversed(range(1, bit_count("head")))]
    side_bit = [("dp", 0)]
    return top, far + across + side_bit, side_bit + across + far[::-1], near


def pair_up(block, other, name, place):
    low = my_bit(*name) == 0
    return jnp.stack([jnp.where(low, block, other), jnp.where(low, other, block)], axis=place)


def gather_bits(block, order):
    rank = {name: place for place, name in enumerate(all_bits())}
    shape = block.shape
    held = []
    for name in order:
        place = sum(rank[have] < rank[name] for have in held)
        block = pair_up(block, flip(block, *name), name, place)
        held.append(name)
    return block.reshape((-1,) + shape)


def gather_two(block, cut):
    _, path_a, path_b, near = paths()
    halves = [gather_bits(block[:cut], path_a), gather_bits(block[cut:], path_b)]
    both = jnp.concatenate(halves, axis=1)
    both = pair_up(both, flip(both, *near), near, 1)
    return both.reshape((-1,) + both.shape[2:])


def scatter_bits(blocks, order):
    names = sorted(order, key=all_bits().index)
    total = blocks.reshape((2,) * len(names) + blocks.shape[1:])
    for name in order:
        place = names.index(name)
        bit = my_bit(*name)
        keep = lax.dynamic_index_in_dim(total, bit, place, keepdims=False)
        send = lax.dynamic_index_in_dim(total, 1 - bit, place, keepdims=False)
        got = flip(send.astype(jnp.bfloat16), *name)
        total = keep.astype(jnp.float32) + got.astype(jnp.float32)
        names.remove(name)
    return total


def scatter_two(blocks, cut):
    _, path_a, path_b, near = paths()
    halved = blocks.reshape((-1, 2) + blocks.shape[1:])
    bit = my_bit(*near)
    keep = lax.dynamic_index_in_dim(halved, bit, 1, keepdims=False)
    got = flip(lax.dynamic_index_in_dim(halved, 1 - bit, 1, keepdims=False), *near)
    total = keep.astype(jnp.float32) + got.astype(jnp.float32)
    first = scatter_bits(total[:, :cut], path_a[::-1])
    second = scatter_bits(total[:, cut:], path_b[::-1])
    return jnp.concatenate([first, second], axis=0)


def sum_bits(values, order):
    for name in order:
        values = values + flip(values, *name)
    return values


def strips_of(values):
    parts = lax.axis_size("head")
    count = values.shape[0] // parts
    mine = lax.axis_index("head")
    strips = []
    for far in range(parts):
        strip = lax.dynamic_slice_in_dim(values, (mine ^ far) * count, count, axis=0)
        if far:
            strip = lax.ppermute(strip, "head", [(i, i ^ far) for i in range(parts)])
        strips.append(strip)
    return strips


def join_strips(strips):
    mine = lax.axis_index("head")
    shape = strips[0].shape
    whole_shape = (shape[0], len(strips)) + shape[1:]
    joined = jnp.zeros(whole_shape, strips[0].dtype)
    for far, strip in enumerate(strips):
        joined = lax.dynamic_update_slice_in_dim(joined, strip[:, None], mine ^ far, axis=1)
    return joined.reshape((shape[0], len(strips) * shape[1]) + shape[2:])


NN = (((1,), (0,)), ((), ()))
NT = (((1,), (1,)), ((), ()))
TN = (((0,), (0,)), ((), ()))


def mm(left, right, form=NN):
    return lax.dot_general(left, right, form, preferred_element_type=jnp.float32)


def group_total(rows, member):
    high = rows.astype(jnp.bfloat16).astype(jnp.float32)
    rest = rows - high
    mid = rest.astype(jnp.bfloat16).astype(jnp.float32)
    parts = jnp.concatenate([high, mid, rest - mid, jnp.zeros_like(rows)], axis=0)
    sums = mm(parts.astype(jnp.bfloat16), member)
    return sums[0:8] + sums[8:16] + sums[16:24]


def fold(values):
    rows, width = values.shape
    return jnp.sum(values.reshape(rows // 8, 8, width), axis=0)


def two_rows(first, second):
    first = jnp.sum(first, axis=0, keepdims=True)
    second = jnp.sum(second, axis=0, keepdims=True)
    row = lax.broadcasted_iota(jnp.int32, (8, first.shape[1]), 0)
    return jnp.where(row == 0, first, jnp.where(row == 1, second, 0.0))


def chunks(total, size, step, init):
    return lax.fori_loop(0, total // size, lambda m, c: step(pl.multiple_of(m * size, size), c), init)


def norm_sums(load, pixels, channels, member):
    def step(at, carry):
        values = load(at)
        return (carry[0] + fold(values), carry[1] + fold(values * values))

    zero = jnp.zeros((8, channels), jnp.float32)
    first, second = chunks(pixels, CHUNK, step, (zero, zero))
    count = pixels * (channels // GROUPS)
    sums = group_total(two_rows(first, second), member) / count
    mean = sums[0:1]
    inverse = lax.rsqrt(sums[1:2] - mean * mean + EPS_NORM)
    return mean, inverse


CHUNK = 128


def attention_kernel(
    scalars,
    middle,
    noise,
    gains,
    member,
    qkv_w,
    out_w,
    down_out,
    qkv_grad,
    out_grad,
    sums_out,
    loss_out,
    qkv_wt,
    normed,
    qkv_t,
    probs,
    totals,
    mixed_t,
    attn_t,
    result,
    grad_b,
    back_t,
    dqkv_t,
    gn_t,
    qkv_acc,
    out_acc,
):
    sample = pl.program_id(0)
    _, pixels, channels = middle.shape
    half = channels // 2
    size = channels // HEADS
    factor = size ** (-0.5)
    width = int(round(pixels**0.5))

    @pl.when(sample == 0)
    def _():
        qkv_wt[...] = qkv_w[...].T
        qkv_acc[...] = jnp.zeros_like(qkv_acc)
        out_acc[...] = jnp.zeros_like(out_acc)

    load = lambda at: middle[0, pl.ds(at, CHUNK), :]
    mean, inverse = norm_sums(load, pixels, channels, member[...])
    gain, shift = gains[4:5], gains[5:6]

    def normalize(at, carry):
        hat = (load(at) - mean) * inverse
        normed[pl.ds(at, CHUNK), :] = (hat * gain + shift).astype(jnp.bfloat16)
        return carry

    chunks(pixels, CHUNK, normalize, 0)

    block = 256

    def attend(head, carry):
        base = pl.multiple_of(head * 3 * size, 32)
        qkv_t[pl.ds(base, 3 * size), :] = mm(
            qkv_wt[pl.ds(base, 3 * size), :], normed[...], NT
        ).astype(jnp.bfloat16)
        keys = qkv_t[pl.ds(base + size, size), :].T
        values_t = qkv_t[pl.ds(base + 2 * size, size), :]
        for q in range(0, pixels, block):
            queries_t = qkv_t[pl.ds(base, size), q : q + block]
            scores = mm(keys, queries_t) * (factor * LOG2E)
            top = jnp.max(scores, axis=0, keepdims=True)
            powers = jnp.exp2(scores - top)
            inv = 1.0 / jnp.sum(powers, axis=0, keepdims=True)
            powers_b = powers.astype(jnp.bfloat16)
            probs[head, :, q : q + block] = powers_b
            totals[head, :, q : q + block] = jnp.broadcast_to(inv, (8, block))
            mixed = mm(values_t, powers_b) * inv
            at = pl.multiple_of(head * size, 32)
            mixed_t[pl.ds(at, size), q : q + block] = mixed
            attn_t[pl.ds(at, size), q : q + block] = mixed.astype(jnp.bfloat16)
        return carry

    lax.fori_loop(0, HEADS, attend, 0)

    result[...] = mm(attn_t[...].T, out_w[...])
    beta_log, tilde_log, coef = scalars[sample, 0], scalars[sample, 1], scalars[sample, 2]
    divisor, high, wide = scalars[sample, 3], scalars[sample, 4], scalars[sample, 5]

    def losses(at, carry):
        total = load(at) + result[pl.ds(at, CHUNK), :]
        pixel = at + lax.broadcasted_iota(jnp.int32, (CHUNK, half), 0)
        row = (pixel // width).astype(jnp.float32)
        col = (pixel % width).astype(jnp.float32)
        valid = jnp.where((row >= width - high) & (col < wide), 1.0, 0.0)
        residue = total[:, :half] - noise[0, pl.ds(at, CHUNK), :].astype(jnp.float32)
        weight = jax.nn.sigmoid(total[:, half:])
        blended = weight * beta_log + (1.0 - weight) * tilde_log
        spread = jnp.exp(tilde_log - blended)
        damped = coef * residue * residue * jnp.exp(-blended)
        diverge = 0.5 * (-1.0 + blended - tilde_log + spread + damped)
        pixel_loss = valid * (residue * residue + VLB_WEIGHT * diverge)
        scale = valid / (half * divisor)
        grad_guess = 2.0 * residue * scale
        grad_raw = (
            scale * (0.5 * VLB_WEIGHT) * (1.0 - spread - damped)
            * (beta_log - tilde_log) * weight * (1.0 - weight)
        )
        grad = jnp.concatenate([grad_guess, grad_raw], axis=-1)
        result[pl.ds(at, CHUNK), :] = grad
        grad_b[pl.ds(at, CHUNK), :] = grad.astype(jnp.bfloat16)
        return carry + fold(pixel_loss)

    loss = chunks(pixels, CHUNK, losses, jnp.zeros((8, half), jnp.float32))
    loss_out[0] = loss * (1.0 / half)

    out_acc[...] += mm(attn_t[...], grad_b[...])
    back_t[...] = mm(out_w[...], grad_b[...], NT).astype(jnp.bfloat16)

    def attend_back(head, carry):
        base = pl.multiple_of(head * 3 * size, 32)
        at = pl.multiple_of(head * size, 32)
        keys_t = qkv_t[pl.ds(base + size, size), :]
        values = qkv_t[pl.ds(base + 2 * size, size), :].T
        grad_key = jnp.zeros((size, pixels), jnp.float32)
        grad_value = jnp.zeros((size, pixels), jnp.float32)
        for q in range(0, pixels, block):
            queries_t = qkv_t[pl.ds(base, size), q : q + block]
            upstream = back_t[pl.ds(at, size), q : q + block]
            inner = jnp.sum(
                upstream.astype(jnp.float32) * mixed_t[pl.ds(at, size), q : q + block],
                axis=0,
                keepdims=True,
            )
            soft = probs[head, :, q : q + block].astype(jnp.float32) * totals[head, 0:1, q : q + block]
            grad_soft = mm(values, upstream)
            grad_scores = (soft * (grad_soft - inner)).astype(jnp.bfloat16)
            dqkv_t[pl.ds(base, size), q : q + block] = (mm(keys_t, grad_scores) * factor).astype(jnp.bfloat16)
            grad_key += mm(queries_t, grad_scores, NT)
            grad_value += mm(upstream, soft.astype(jnp.bfloat16), NT)
        dqkv_t[pl.ds(base + size, size), :] = (grad_key * factor).astype(jnp.bfloat16)
        dqkv_t[pl.ds(base + 2 * size, size), :] = grad_value.astype(jnp.bfloat16)
        return carry

    lax.fori_loop(0, HEADS, attend_back, 0)

    qkv_acc[...] += mm(normed[...].T, dqkv_t[...], NT)
    gn_t[...] = mm(qkv_w[...], dqkv_t[...])

    def back_sums(at, carry):
        hat = (load(at) - mean) * inverse
        grad = gn_t[:, pl.ds(at, CHUNK)].T
        return (carry[0] + fold(grad * hat), carry[1] + fold(grad))

    zero = jnp.zeros((8, channels), jnp.float32)
    both = chunks(pixels, CHUNK, back_sums, (zero, zero))
    rows = two_rows(*both)
    sums_out[0] = rows
    means = group_total(rows * gain, member[...]) / (pixels * (channels // GROUPS))

    def back_norm(at, carry):
        hat = (load(at) - mean) * inverse
        grad = gn_t[:, pl.ds(at, CHUNK)].T * gain
        back = (grad - means[1:2] - hat * means[0:1]) * inverse
        down_out[0, pl.ds(at, CHUNK), :] = (result[pl.ds(at, CHUNK), :] + back).astype(jnp.bfloat16)
        return carry

    chunks(pixels, CHUNK, back_norm, 0)

    @pl.when(sample == pl.num_programs(0) - 1)
    def _():
        qkv_grad[...] = qkv_acc[...].astype(jnp.bfloat16)
        out_grad[...] = out_acc[...].astype(jnp.bfloat16)


def attention_block(scalars, middle, noise, gains, member, qkv_w, out_w):
    samples, pixels, channels = middle.shape
    half = channels // 2
    bf, f32 = jnp.bfloat16, jnp.float32
    whole = lambda *shape: pl.BlockSpec(shape, lambda s: (0,) * len(shape))
    each = lambda *shape: pl.BlockSpec((1,) + shape, lambda s: (s, 0, 0))
    return pl.pallas_call(
        attention_kernel,
        grid=(samples,),
        in_specs=[
            pl.BlockSpec(memory_space=pltpu.SMEM),
            each(pixels, channels),
            each(pixels, half),
            whole(8, channels),
            whole(channels, channels),
            whole(channels, 3 * channels),
            whole(channels, channels),
        ],
        out_specs=[
            each(pixels, channels),
            whole(channels, 3 * channels),
            whole(channels, channels),
            each(8, channels),
            each(8, half),
        ],
        out_shape=[
            jax.ShapeDtypeStruct((samples, pixels, channels), bf),
            jax.ShapeDtypeStruct((channels, 3 * channels), bf),
            jax.ShapeDtypeStruct((channels, channels), bf),
            jax.ShapeDtypeStruct((samples, 8, channels), f32),
            jax.ShapeDtypeStruct((samples, 8, half), f32),
        ],
        scratch_shapes=[
            pltpu.VMEM((3 * channels, channels), bf),
            pltpu.VMEM((pixels, channels), bf),
            pltpu.VMEM((3 * channels, pixels), bf),
            pltpu.VMEM((HEADS, pixels, pixels), bf),
            pltpu.VMEM((HEADS, 8, pixels), f32),
            pltpu.VMEM((channels, pixels), f32),
            pltpu.VMEM((channels, pixels), bf),
            pltpu.VMEM((pixels, channels), f32),
            pltpu.VMEM((pixels, channels), bf),
            pltpu.VMEM((channels, pixels), bf),
            pltpu.VMEM((3 * channels, pixels), bf),
            pltpu.VMEM((channels, pixels), f32),
            pltpu.VMEM((channels, 3 * channels), f32),
            pltpu.VMEM((channels, channels), f32),
        ],
        compiler_params=pltpu.CompilerParams(vmem_limit_bytes=VMEM_LIMIT),
        cost_estimate=pl.CostEstimate(
            flops=30 * samples * pixels * pixels * channels,
            bytes_accessed=8 * samples * pixels * channels,
            transcendentals=samples * HEADS * pixels * pixels,
        ),
    )(scalars, middle, noise, gains, member, qkv_w, out_w)


def fill(padded, at, values, width):
    rows, channels = values.shape
    col = lax.broadcasted_iota(jnp.int32, values.shape, 0) % width
    there = pl.ds(at + width, rows)
    left = jnp.where(col == 0, 0.0, pltpu.roll(values, 1, 0))
    right = jnp.where(col == width - 1, 0.0, pltpu.roll(values, rows - 1, 0))
    padded[there, 0:channels] = left.astype(jnp.bfloat16)
    padded[there, channels : 2 * channels] = values.astype(jnp.bfloat16)
    padded[there, 2 * channels :] = right.astype(jnp.bfloat16)


def clear_edges(padded, width):
    rows, wide = padded.shape
    padded[0:width, :] = jnp.zeros((width, wide), jnp.bfloat16)
    padded[rows - width :, :] = jnp.zeros((width, wide), jnp.bfloat16)


def side(pixels):
    return int(round(pixels**0.5))


def taps_product(padded, weight, pixels, width):
    wide = padded.shape[1]
    total = mm(padded[0:pixels, :], weight(0))
    for i in (1, 2):
        total += mm(padded[i * width : i * width + pixels, :], weight(i))
    return total


def rows_of(*rows):
    index = lax.broadcasted_iota(jnp.int32, (8, rows[0].shape[1]), 0)
    total = jnp.zeros(index.shape, jnp.float32)
    for place, row in enumerate(rows):
        total = jnp.where(index == place, row, total)
    return total


def first_kernel(images, gains, member, weight, inner, hidden, stats, padded):
    _, pixels, channels = images.shape
    width = side(pixels)
    wide = 3 * channels
    load = lambda at: images[0, pl.ds(at, CHUNK), :].astype(jnp.float32)
    mean, inverse = norm_sums(load, pixels, channels, member[...])
    gain, shift = gains[0:1], gains[1:2]
    clear_edges(padded, width)

    def activate(at, carry):
        out = (load(at) - mean) * inverse * gain + shift
        value = out * jax.nn.sigmoid(out)
        hidden[0, pl.ds(at, CHUNK), :] = value.astype(jnp.bfloat16)
        fill(padded, at, value, width)
        return carry

    chunks(pixels, CHUNK, activate, 0)
    inner[0] = taps_product(padded, lambda i: weight[i * wide : (i + 1) * wide, :], pixels, width)
    mean_two, inverse_two = norm_sums(
        lambda at: inner[0, pl.ds(at, CHUNK), :], pixels, channels, member[...]
    )
    stats[0] = rows_of(mean, inverse, mean_two, inverse_two)


def second_kernel(inner, images, stats, film, gains, weight, middle, hidden, padded):
    _, pixels, channels = inner.shape
    width = side(pixels)
    wide = 3 * channels
    mean, inverse = stats[0, 2:3], stats[0, 3:4]
    scale, lift = 1.0 + film[0, 0:1], film[0, 1:2]
    gain, shift = gains[2:3], gains[3:4]
    clear_edges(padded, width)

    def activate(at, carry):
        out = (inner[0, pl.ds(at, CHUNK), :] - mean) * inverse * gain + shift
        lifted = out * scale + lift
        value = lifted * jax.nn.sigmoid(lifted)
        hidden[0, pl.ds(at, CHUNK), :] = value.astype(jnp.bfloat16)
        fill(padded, at, value, width)
        return carry

    chunks(pixels, CHUNK, activate, 0)
    middle[0] = images[0].astype(jnp.float32) + taps_product(
        padded, lambda i: weight[i * wide : (i + 1) * wide, :], pixels, width
    )


def weights_kernel(hidden, grad, out, padded, total):
    sample = pl.program_id(0)
    _, pixels, channels = hidden.shape
    width = side(pixels)
    wide = 3 * channels
    clear_edges(padded, width)

    def spread(at, carry):
        fill(padded, at, hidden[0, pl.ds(at, CHUNK), :].astype(jnp.float32), width)
        return carry

    chunks(pixels, CHUNK, spread, 0)

    @pl.when(sample == 0)
    def _():
        total[...] = jnp.zeros_like(total)

    for i in range(3):
        total[i * wide : (i + 1) * wide, :] += mm(
            padded[i * width : i * width + pixels, :], grad[0], TN
        )

    @pl.when(sample == pl.num_programs(0) - 1)
    def _():
        out[...] = total[...].astype(jnp.bfloat16)


def turn_taps(weight, turned):
    channels = weight.shape[1]
    for i in range(3):
        for j in range(3):
            tap = 3 * (2 - i) + 2 - j
            turned[i, :, j * channels : (j + 1) * channels] = weight[
                tap * channels : (tap + 1) * channels, :
            ]


def input_grad(grad, weight, padded, turned, down):
    _, pixels, channels = grad.shape
    width = side(pixels)

    @pl.when(pl.program_id(0) == 0)
    def _():
        turn_taps(weight, turned)

    clear_edges(padded, width)

    def spread(at, carry):
        fill(padded, at, grad[0, pl.ds(at, CHUNK), :].astype(jnp.float32), width)
        return carry

    chunks(pixels, CHUNK, spread, 0)
    total = mm(padded[0:pixels, :], turned[0], NT)
    for i in (1, 2):
        total += mm(padded[i * width : i * width + pixels, :], turned[i], NT)
    down[...] = total


def slope_of(values):
    sig = jax.nn.sigmoid(values)
    return sig * (1.0 + values * (1.0 - sig))


def second_back_kernel(
    grad, inner, stats, film, gains, member, weight, grad_out, sums_out, padded, turned, down
):
    _, pixels, channels = grad.shape
    input_grad(grad, weight, padded, turned, down)
    mean, inverse = stats[0, 2:3], stats[0, 3:4]
    scale, lift = 1.0 + film[0, 0:1], film[0, 1:2]
    gain, shift = gains[2:3], gains[3:4]

    def slopes(at, carry):
        hat = (inner[0, pl.ds(at, CHUNK), :] - mean) * inverse
        lifted = (hat * gain + shift) * scale + lift
        lifted_grad = down[pl.ds(at, CHUNK), :] * slope_of(lifted)
        down[pl.ds(at, CHUNK), :] = lifted_grad
        return (carry[0] + fold(lifted_grad * hat), carry[1] + fold(lifted_grad))

    zero = jnp.zeros((8, channels), jnp.float32)
    rows = two_rows(*chunks(pixels, CHUNK, slopes, (zero, zero)))
    sums_out[0] = rows
    factor = scale * gain
    means = group_total(rows * factor, member[...]) / (pixels * (channels // GROUPS))

    def back_norm(at, carry):
        hat = (inner[0, pl.ds(at, CHUNK), :] - mean) * inverse
        back = (down[pl.ds(at, CHUNK), :] * factor - means[1:2] - hat * means[0:1]) * inverse
        grad_out[0, pl.ds(at, CHUNK), :] = back.astype(jnp.bfloat16)
        return carry

    chunks(pixels, CHUNK, back_norm, 0)


def first_back_kernel(grad, images, stats, gains, weight, sums_out, padded, turned, down):
    _, pixels, channels = grad.shape
    input_grad(grad, weight, padded, turned, down)
    mean, inverse = stats[0, 0:1], stats[0, 1:2]
    gain, shift = gains[0:1], gains[1:2]

    def slopes(at, carry):
        hat = (images[0, pl.ds(at, CHUNK), :].astype(jnp.float32) - mean) * inverse
        grad_first = down[pl.ds(at, CHUNK), :] * slope_of(hat * gain + shift)
        return (carry[0] + fold(grad_first * hat), carry[1] + fold(grad_first))

    zero = jnp.zeros((8, channels), jnp.float32)
    sums_out[0] = two_rows(*chunks(pixels, CHUNK, slopes, (zero, zero)))


def whole(*shape):
    return pl.BlockSpec(shape, lambda s: (0,) * len(shape))


def each(*shape):
    return pl.BlockSpec((1,) + shape, lambda s: (s,) + (0,) * len(shape))


def per_sample(kernel, samples, in_specs, outs, scratch, flops, *operands):
    return pl.pallas_call(
        kernel,
        grid=(samples,),
        in_specs=in_specs,
        out_specs=[spec for spec, _ in outs],
        out_shape=[shape for _, shape in outs],
        scratch_shapes=scratch,
        compiler_params=pltpu.CompilerParams(vmem_limit_bytes=VMEM_LIMIT),
        cost_estimate=pl.CostEstimate(flops=flops, bytes_accessed=flops // 1000, transcendentals=0),
    )(*operands)


def sized(dtype, *shape):
    return jax.ShapeDtypeStruct(shape, dtype)


def block_calls(samples, pixels, channels):
    width = side(pixels)
    act = each(pixels, channels)
    few = each(8, channels)
    gain_spec, member_spec = whole(8, channels), whole(channels, channels)
    weight_spec = whole(9 * channels, channels)
    bf, f32 = jnp.bfloat16, jnp.float32
    padded = pltpu.VMEM((pixels + 2 * width, 3 * channels), bf)
    turned = pltpu.VMEM((3, channels, 3 * channels), bf)
    down = pltpu.VMEM((pixels, channels), f32)
    act_b = sized(bf, samples, pixels, channels)
    act_f = sized(f32, samples, pixels, channels)
    few_f = sized(f32, samples, 8, channels)
    flops = 18 * samples * pixels * channels * channels

    def first(images, gains, member, weight):
        return per_sample(
            first_kernel, samples, [act, gain_spec, member_spec, weight_spec],
            [(act, act_f), (act, act_b), (few, few_f)], [padded], flops,
            images, gains, member, weight,
        )

    def second(inner, images, stats, film, gains, weight):
        return per_sample(
            second_kernel, samples, [act, act, few, few, gain_spec, weight_spec],
            [(act, act_f), (act, act_b)], [padded], flops,
            inner, images, stats, film, gains, weight,
        )

    def weights(hidden, grad):
        return per_sample(
            weights_kernel, samples, [act, act],
            [(weight_spec, sized(bf, 9 * channels, channels))],
            [padded, pltpu.VMEM((9 * channels, channels), f32)], flops, hidden, grad,
        )[0]

    def second_back(grad, inner, stats, film, gains, member, weight):
        return per_sample(
            second_back_kernel, samples,
            [act, act, few, few, gain_spec, member_spec, weight_spec],
            [(act, act_b), (few, few_f)], [padded, turned, down], flops,
            grad, inner, stats, film, gains, member, weight,
        )

    def first_back(grad, images, stats, gains, weight):
        return per_sample(
            first_back_kernel, samples, [act, act, few, gain_spec, weight_spec],
            [(few, few_f)], [padded, turned, down], flops,
            grad, images, stats, gains, weight,
        )[0]

    return first, second, weights, second_back, first_back


def adamw(master, gradient, first, second, step_rate, decay_rate, clip_factor):
    gradient = gradient * clip_factor
    first_new = BETA_ONE * first + (1.0 - BETA_ONE) * gradient
    second_new = BETA_TWO * second + (1.0 - BETA_TWO) * gradient * gradient
    ratio = (
        first_new
        / (1.0 - BETA_ONE**STEP)
        / (jnp.sqrt(second_new / (1.0 - BETA_TWO**STEP)) + ADAM_EPS)
    )
    return (master - step_rate * (ratio + decay_rate * master), first_new, second_new)


def body(
    images,
    noise,
    timesteps,
    extents,
    film_master,
    conv_master,
    qkv_master,
    out_master,
    gains,
    film_first,
    film_second,
    conv_first,
    conv_second,
    qkv_first,
    qkv_second,
    out_first,
    out_second,
    gain_first,
    gain_second,
):
    devices = lax.axis_size("dp") * lax.axis_size("head")
    device = lax.axis_index("dp") * lax.axis_size("head") + lax.axis_index("head")
    bits = all_bits()
    channels = images.shape[-1]
    wide = film_master.shape[1]
    half_width = channels // 2
    conv_rows = conv_master.shape[0]
    film_rows = film_master.shape[0]
    out_rows = out_master.shape[0]

    local_samples = timesteps.shape[0]
    small = jnp.concatenate(
        [
            gains.reshape(-1),
            extents.astype(jnp.float32).reshape(-1),
            (timesteps // 64).astype(jnp.float32),
            (timesteps % 64).astype(jnp.float32),
        ]
    )
    small = jnp.pad(small, (0, 8 * channels - small.shape[0])).reshape(8, channels)
    top, _, _, _ = paths()
    is_top = my_bit(*top) == 1
    ours = jnp.concatenate([conv_master, small]).astype(jnp.bfloat16)
    theirs = flip(ours, *top)
    rest = jnp.concatenate(
        [film_master.reshape(-1, channels), qkv_master.reshape(-1, channels), out_master]
    ).astype(jnp.bfloat16)
    rest_two = pair_up(rest, flip(rest, *top), top, 0)
    one = jnp.where(is_top, theirs, ours)
    two = jnp.where(is_top, ours, theirs)
    small_two = jnp.stack([one[conv_rows:], two[conv_rows:]]).reshape(-1, channels)
    cut = conv_rows // 16 * 8
    group_one = gather_two(jnp.concatenate([one[:conv_rows], small_two]), cut)
    strips = strips_of(images)
    held_rows = rest.shape[0]
    group_two = gather_two(
        jnp.concatenate([two[:conv_rows], rest_two.reshape(-1, channels)]),
        (conv_rows + 2 * held_rows) // 16 * 8,
    )
    taps_one = group_one[:, :conv_rows].reshape(-1, channels)
    taps_two = group_two[:, :conv_rows].reshape(-1, channels)
    smalls = jnp.moveaxis(group_one[:, conv_rows:].reshape(-1, 2, 8 * channels), 0, 1)
    others = jnp.moveaxis(group_two[:, conv_rows:].reshape(-1, 2, held_rows, channels), 0, 1)
    others = others.reshape(devices, held_rows, channels)
    film_own_rows = film_rows * wide // channels
    film_w = others[:, :film_own_rows].reshape(-1, wide)
    qkv_w = others[:, film_own_rows : film_own_rows + 3 * out_rows].reshape(channels, 3 * channels)
    out_w = others[:, film_own_rows + 3 * out_rows :].reshape(channels, channels)
    smalls = smalls.reshape(devices, -1).astype(jnp.float32)
    gain_f = smalls[:, : gains.size].reshape(channels, 6)
    dp_smalls = smalls.reshape(lax.axis_size("dp"), lax.axis_size("head"), -1)[:, 0, gains.size :]
    extents_all = dp_smalls[:, : 2 * local_samples].reshape(-1, 2)
    times = dp_smalls[:, 2 * local_samples : 4 * local_samples].reshape(-1, 2, local_samples)
    times_all = (times[:, 0] * 64.0 + times[:, 1]).reshape(-1).astype(jnp.int32)
    divisor = jnp.sum(extents_all[:, 0] * extents_all[:, 1])

    pictures = join_strips(strips)
    target = join_strips(strips_of(noise))
    samples, rows, width_px, _ = pictures.shape
    pixels = rows * width_px
    first = lax.axis_index("head") * samples
    own_times = lax.dynamic_slice_in_dim(timesteps, first, samples)
    own_extents = lax.dynamic_slice_in_dim(extents, first, samples)

    log_beta, log_tilde, factor = plan(own_times)
    embedded_all = jax.nn.silu(embed(times_all, wide)).astype(jnp.bfloat16)
    embedded = jax.nn.silu(embed(own_times, wide)).astype(jnp.bfloat16)
    film_out = lax.dot_general(
        embedded, film_w, (((1,), (1,)), ((), ())), preferred_element_type=jnp.float32
    )
    film = jnp.pad(film_out.reshape(samples, 2, channels), ((0, 0), (0, 6), (0, 0)))
    scale = 1.0 + film_out[:, :channels]
    source = pictures.reshape(samples, pixels, channels)
    gains_t = jnp.pad(gain_f.T, ((0, 2), (0, 0)))
    member = jnp.asarray(np.kron(np.eye(GROUPS), np.ones((channels // GROUPS,) * 2)), jnp.bfloat16)
    scalars = jnp.stack(
        [log_beta, log_tilde, factor, jnp.broadcast_to(divisor, factor.shape)]
        + [own_extents[:, 0].astype(jnp.float32), own_extents[:, 1].astype(jnp.float32)],
        axis=1,
    )
    first_call, second_call, weights, second_back, first_back = block_calls(samples, pixels, channels)
    inner, hidden_one, stats = first_call(source, gains_t, member, taps_one)
    middle, hidden_two = second_call(inner, source, stats, film, gains_t, taps_two)
    grad_two_b, qkv_grad, out_grad, sums_three, losses = attention_block(
        scalars, middle, target.reshape(samples, pixels, half_width), gains_t, member, qkv_w, out_w
    )
    loss_local = jnp.sum(losses)
    conv_two_grad = weights(hidden_two, grad_two_b)
    grad_one_b, sums_two = second_back(grad_two_b, inner, stats, film, gains_t, member, taps_two)
    conv_one_grad = weights(hidden_one, grad_one_b)
    sums_one = first_back(grad_one_b, source, stats, gains_t, taps_one)
    gain_one, bias_one = jnp.sum(sums_one[:, 0], axis=0), jnp.sum(sums_one[:, 1], axis=0)
    gain_two, bias_two = jnp.sum(sums_two[:, 0] * scale, axis=0), jnp.sum(sums_two[:, 1] * scale, axis=0)
    gain_three, bias_three = jnp.sum(sums_three[:, 0], axis=0), jnp.sum(sums_three[:, 1], axis=0)
    grad_scale = sums_two[:, 0] * gains_t[2] + sums_two[:, 1] * gains_t[3]
    film_grad_b = jnp.concatenate([grad_scale, sums_two[:, 1]], axis=1).astype(jnp.bfloat16)

    both_grads = jnp.concatenate(
        [qkv_grad.reshape(2, -1, 3 * out_rows, channels), out_grad.reshape(2, -1, out_rows, channels)],
        axis=2,
    )
    both_grads = jnp.moveaxis(both_grads, 0, 1).reshape(devices // 2, 8 * out_rows, channels)
    two_grads = jnp.concatenate(
        [conv_two_grad.reshape(-1, conv_rows, channels), both_grads], axis=1
    )
    share_two = scatter_two(two_grads, (conv_rows + 8 * out_rows) // 16 * 8)
    share_one = scatter_two(conv_one_grad.reshape(-1, conv_rows, channels), cut)
    small_shares = share_two[conv_rows:].reshape(2, 4 * out_rows, channels)
    mine = jnp.concatenate(
        [
            jnp.where(is_top, share_two[:conv_rows], share_one),
            jnp.where(is_top, small_shares[1], small_shares[0]),
        ]
    )
    sent = jnp.concatenate(
        [
            jnp.where(is_top, share_one, share_two[:conv_rows]),
            jnp.where(is_top, small_shares[0], small_shares[1]),
        ]
    )
    summed = mine + flip(sent.astype(jnp.bfloat16), *top).astype(jnp.float32)
    conv_g = summed[:conv_rows]
    qkv_g = summed[conv_rows : conv_rows + 3 * out_rows].reshape(qkv_master.shape)
    out_g = summed[conv_rows + 3 * out_rows :]

    film_all = gather_bits(film_grad_b, bits).reshape(-1, film_grad_b.shape[1])
    film_own = lax.dynamic_slice_in_dim(film_all, device * film_rows, film_rows, axis=1)
    film_g = jnp.einsum("sf,se->fe", film_own, embedded_all, preferred_element_type=jnp.float32)
    gain_grad = jnp.stack([gain_one, bias_one, gain_two, bias_two, gain_three, bias_three], axis=1)
    gain_g = sum_bits(gain_grad, bits).reshape(devices, -1, 6)
    gain_g = lax.dynamic_index_in_dim(gain_g, device, 0, keepdims=False)
    reduced = (film_g, conv_g, qkv_g, out_g, gain_g)
    squares = jnp.zeros((), jnp.float32)
    for gradient in reduced:
        squares = squares + jnp.sum(gradient * gradient)
    totals = sum_bits(jnp.stack([squares, loss_local]), bits)
    grad_norm = jnp.sqrt(totals[0])
    clip_factor = jnp.minimum(1.0, THRESHOLD / (grad_norm + 1e-06))
    film_res = adamw(film_master, film_g, film_first, film_second, RATE_MATRIX, DECAY, clip_factor)
    conv_res = adamw(conv_master, conv_g, conv_first, conv_second, RATE_MATRIX, DECAY, clip_factor)
    qkv_res = adamw(qkv_master, qkv_g, qkv_first, qkv_second, RATE_MATRIX, DECAY, clip_factor)
    out_res = adamw(out_master, out_g, out_first, out_second, RATE_MATRIX, DECAY, clip_factor)
    gain_res = adamw(gains, gain_g, gain_first, gain_second, RATE_GAIN, 0.0, clip_factor)
    loss_parts = jnp.stack([totals[1], divisor])
    return (
        loss_parts,
        grad_norm,
        film_res[0],
        film_res[1],
        film_res[2],
        conv_res[0],
        conv_res[1],
        conv_res[2],
        qkv_res[0],
        qkv_res[1],
        qkv_res[2],
        out_res[0],
        out_res[1],
        out_res[2],
        gain_res[0],
        gain_res[1],
        gain_res[2],
    )


def solution(mesh):
    in_specs = (
        P("dp", "head", None, None),
        P("dp", "head", None, None),
        P("dp"),
        P("dp", None),
        P(("dp", "head"), None),
        P(("dp", "head"), None),
        P(("dp", "head"), None),
        P(("dp", "head"), None),
        P(("dp", "head"), None),
        P(("dp", "head"), None),
        P(("dp", "head"), None),
        P(("dp", "head"), None),
        P(("dp", "head"), None),
        P(("dp", "head"), None),
        P(("dp", "head"), None),
        P(("dp", "head"), None),
        P(("dp", "head"), None),
        P(("dp", "head"), None),
        P(("dp", "head"), None),
    )
    out_specs = (
        P(),
        P(),
        P(("dp", "head"), None),
        P(("dp", "head"), None),
        P(("dp", "head"), None),
        P(("dp", "head"), None),
        P(("dp", "head"), None),
        P(("dp", "head"), None),
        P(("dp", "head"), None),
        P(("dp", "head"), None),
        P(("dp", "head"), None),
        P(("dp", "head"), None),
        P(("dp", "head"), None),
        P(("dp", "head"), None),
        P(("dp", "head"), None),
        P(("dp", "head"), None),
        P(("dp", "head"), None),
    )
    return jax.shard_map(body, mesh=mesh, in_specs=in_specs, out_specs=out_specs, check_vma=False)
```

```python
import functools
import math

import jax
import jax.numpy as jnp
import numpy as np
from jax import lax
from jax.experimental import pallas as pl
from jax.experimental.pallas import tpu as pltpu
from jax.sharding import PartitionSpec as P

HEADS = 4
GROUPS = 32
STEP = 10
TSTEPS = 4000


EPS_NORM = 1e-05
VLB_WEIGHT = 0.001
BETA_ONE = 0.9
BETA_TWO = 0.999
ADAM_EPS = 1e-08
DECAY = 0.01
RATE_MATRIX = 0.05
RATE_GAIN = 0.4
THRESHOLD = 0.002
OFFSET = 0.008
LOG2E = math.log2(math.e)
VMEM_LIMIT = 56 << 20


def plan(step_ids):
    moment = step_ids.astype(jnp.float32)

    def angle(values):
        return (values / TSTEPS + OFFSET) / (1.0 + OFFSET) * (0.5 * math.pi)

    start = angle(jnp.zeros_like(moment))
    before = angle(moment - 1.0)
    later_angle = angle(moment)
    beta_now = jnp.sin(later_angle - before) * jnp.sin(later_angle + before) / jnp.cos(before) ** 2
    fade_now = jnp.sin(later_angle - start) * jnp.sin(later_angle + start) / jnp.cos(start) ** 2
    fade_prev = jnp.sin(before - start) * jnp.sin(before + start) / jnp.cos(start) ** 2
    log_beta = jnp.log(beta_now)
    log_tilde = jnp.log(beta_now * fade_prev / fade_now)
    factor = beta_now * beta_now / ((1.0 - beta_now) * fade_now)
    return (log_beta, log_tilde, factor)


def embed(step_ids, width):
    half_width = width // 2
    frequency = jnp.exp(-math.log(10000.0) * jnp.arange(half_width, dtype=jnp.float32) / half_width)
    phases = step_ids.astype(jnp.float32)[:, None] * frequency[None, :]
    return jnp.concatenate([jnp.cos(phases), jnp.sin(phases)], axis=1)


def behind(values, *others):
    return lax.optimization_barrier((values,) + others)[0]


def pair_up(block, other, low, place):
    return jnp.stack([jnp.where(low, block, other), jnp.where(low, other, block)], axis=place)


def class_count():
    return lax.axis_size("dp") * lax.axis_size("head") // 4


def last_bit():
    return lax.axis_index("head") % 2


def exchange(values, mask):
    size = lax.axis_size("dp") * lax.axis_size("head")
    return lax.ppermute(values, ("dp", "head"), [(i, i ^ mask) for i in range(size)])


def across_classes(blocks):
    count = class_count()
    groups = [
        [(high * count + k) * 2 + last for k in range(count)] for high in range(2) for last in range(2)
    ]
    return lax.all_to_all(
        blocks, ("dp", "head"), split_axis=0, concat_axis=0, axis_index_groups=groups, tiled=True
    )


def gather_classes(block):
    return across_classes(jnp.broadcast_to(block[None], (class_count(),) + block.shape))


def finish_gather(both, parts):
    other = exchange(both, 1)
    low = last_bit() == 0
    joined, at = [], 0
    for rows in parts:
        piece = pair_up(both[:, at : at + rows], other[:, at : at + rows], low, 1)
        joined.append(piece.reshape((-1,) + piece.shape[2:]))
        at += rows
    return joined


def to_all(blocks):
    return lax.all_to_all(blocks, ("dp", "head"), split_axis=0, concat_axis=0, tiled=True)


def strips_of(values):
    parts = lax.axis_size("head")
    count = values.shape[0] // parts
    mine = lax.axis_index("head")
    strips = []
    for far in range(parts):
        strip = lax.dynamic_slice_in_dim(values, (mine ^ far) * count, count, axis=0)
        if far:
            strip = lax.ppermute(strip, "head", [(i, i ^ far) for i in range(parts)])
        strips.append(strip)
    return strips


NN = (((1,), (0,)), ((), ()))
NT = (((1,), (1,)), ((), ()))
TN = (((0,), (0,)), ((), ()))


def mm(left, right, form=NN):
    return lax.dot_general(left, right, form, preferred_element_type=jnp.float32)


def group_total(rows, member):
    high = rows.astype(jnp.bfloat16).astype(jnp.float32)
    rest = rows - high
    mid = rest.astype(jnp.bfloat16).astype(jnp.float32)
    parts = jnp.concatenate([high, mid, rest - mid, jnp.zeros_like(rows)], axis=0)
    sums = mm(parts.astype(jnp.bfloat16), member)
    return sums[0:8] + sums[8:16] + sums[16:24]


def fold(values):
    rows, width = values.shape
    return jnp.sum(values.reshape(rows // 8, 8, width), axis=0)


def two_rows(first, second):
    first = jnp.sum(first, axis=0, keepdims=True)
    second = jnp.sum(second, axis=0, keepdims=True)
    row = lax.broadcasted_iota(jnp.int32, (8, first.shape[1]), 0)
    return jnp.where(row == 0, first, jnp.where(row == 1, second, 0.0))


def chunks(total, size, step, init):
    return lax.fori_loop(0, total // size, lambda m, c: step(pl.multiple_of(m * size, size), c), init)


def norm_sums(load, pixels, channels, member):
    def step(at, carry):
        values = load(at)
        return (carry[0] + fold(values), carry[1] + fold(values * values))

    zero = jnp.zeros((8, channels), jnp.float32)
    first, second = chunks(pixels, CHUNK, step, (zero, zero))
    count = pixels * (channels // GROUPS)
    sums = group_total(two_rows(first, second), member) / count
    mean = sums[0:1]
    inverse = lax.rsqrt(sums[1:2] - mean * mean + EPS_NORM)
    return mean, inverse


CHUNK = 128


def attention_kernel(parts, places, scalars, middle, *refs):
    attention_body(places, scalars, middle, refs[:parts], *refs[parts:])


def attention_body(
    places,
    scalars,
    middle,
    strips,
    gains,
    member,
    qkv_w,
    out_w,
    order,
    down_out,
    shares,
    sums_out,
    loss_out,
    noise,
    qkv_wt,
    normed,
    qkv_t,
    probs,
    totals,
    mixed_t,
    attn_t,
    result,
    grad_b,
    back_t,
    dqkv_t,
    gn_t,
    qkv_acc,
    out_acc,
):
    sample = pl.program_id(0)
    _, pixels, channels = middle.shape
    half = channels // 2
    size = channels // HEADS
    factor = size ** (-0.5)
    width = int(round(pixels**0.5))

    @pl.when(sample == 0)
    def _():
        qkv_wt[...] = qkv_w[...].T
        qkv_acc[...] = jnp.zeros_like(qkv_acc)
        out_acc[...] = jnp.zeros_like(out_acc)

    join_strips(places, strips, noise)
    load = lambda at: middle[0, pl.ds(at, CHUNK), :]
    mean, inverse = norm_sums(load, pixels, channels, member[...])
    gain, shift = gains[4:5], gains[5:6]

    def normalize(at, carry):
        hat = (load(at) - mean) * inverse
        normed[pl.ds(at, CHUNK), :] = (hat * gain + shift).astype(jnp.bfloat16)
        return carry

    chunks(pixels, CHUNK, normalize, 0)

    block = 256

    def attend(head, carry):
        base = pl.multiple_of(head * 3 * size, 32)
        qkv_t[pl.ds(base, 3 * size), :] = mm(
            qkv_wt[pl.ds(base, 3 * size), :], normed[...], NT
        ).astype(jnp.bfloat16)
        keys = qkv_t[pl.ds(base + size, size), :].T
        values_t = qkv_t[pl.ds(base + 2 * size, size), :]
        for q in range(0, pixels, block):
            queries_t = qkv_t[pl.ds(base, size), q : q + block]
            scores = mm(keys, queries_t) * (factor * LOG2E)
            top = jnp.max(scores, axis=0, keepdims=True)
            powers = jnp.exp2(scores - top)
            inv = 1.0 / jnp.sum(powers, axis=0, keepdims=True)
            powers_b = powers.astype(jnp.bfloat16)
            probs[head, :, q : q + block] = powers_b
            totals[head, :, q : q + block] = jnp.broadcast_to(inv, (8, block))
            mixed = mm(values_t, powers_b) * inv
            at = pl.multiple_of(head * size, 32)
            mixed_t[pl.ds(at, size), q : q + block] = mixed
            attn_t[pl.ds(at, size), q : q + block] = mixed.astype(jnp.bfloat16)
        return carry

    lax.fori_loop(0, HEADS, attend, 0)

    result[...] = mm(attn_t[...].T, out_w[...])
    beta_log, tilde_log, coef = scalars[sample, 0], scalars[sample, 1], scalars[sample, 2]
    divisor, high, wide = scalars[sample, 3], scalars[sample, 4], scalars[sample, 5]

    def losses(at, carry):
        total = load(at) + result[pl.ds(at, CHUNK), :]
        pixel = at + lax.broadcasted_iota(jnp.int32, (CHUNK, half), 0)
        row = (pixel // width).astype(jnp.float32)
        col = (pixel % width).astype(jnp.float32)
        valid = jnp.where((row >= width - high) & (col < wide), 1.0, 0.0)
        residue = total[:, :half] - noise[pl.ds(at, CHUNK), :].astype(jnp.float32)
        weight = jax.nn.sigmoid(total[:, half:])
        blended = weight * beta_log + (1.0 - weight) * tilde_log
        spread = jnp.exp(tilde_log - blended)
        damped = coef * residue * residue * jnp.exp(-blended)
        diverge = 0.5 * (-1.0 + blended - tilde_log + spread + damped)
        pixel_loss = valid * (residue * residue + VLB_WEIGHT * diverge)
        scale = valid / (half * divisor)
        grad_guess = 2.0 * residue * scale
        grad_raw = (
            scale * (0.5 * VLB_WEIGHT) * (1.0 - spread - damped)
            * (beta_log - tilde_log) * weight * (1.0 - weight)
        )
        grad = jnp.concatenate([grad_guess, grad_raw], axis=-1)
        result[pl.ds(at, CHUNK), :] = grad
        grad_b[pl.ds(at, CHUNK), :] = grad.astype(jnp.bfloat16)
        return carry + fold(pixel_loss)

    loss = chunks(pixels, CHUNK, losses, jnp.zeros((8, half), jnp.float32))
    loss_out[0] = loss * (1.0 / half)

    out_acc[...] += mm(attn_t[...], grad_b[...])
    back_t[...] = mm(out_w[...], grad_b[...], NT).astype(jnp.bfloat16)

    def attend_back(head, carry):
        base = pl.multiple_of(head * 3 * size, 32)
        at = pl.multiple_of(head * size, 32)
        keys_t = qkv_t[pl.ds(base + size, size), :]
        values = qkv_t[pl.ds(base + 2 * size, size), :].T
        grad_key = jnp.zeros((size, pixels), jnp.float32)
        grad_value = jnp.zeros((size, pixels), jnp.float32)
        for q in range(0, pixels, block):
            queries_t = qkv_t[pl.ds(base, size), q : q + block]
            upstream = back_t[pl.ds(at, size), q : q + block]
            inner = jnp.sum(
                upstream.astype(jnp.float32) * mixed_t[pl.ds(at, size), q : q + block],
                axis=0,
                keepdims=True,
            )
            soft = probs[head, :, q : q + block].astype(jnp.float32) * totals[head, 0:1, q : q + block]
            grad_soft = mm(values, upstream)
            grad_scores = (soft * (grad_soft - inner)).astype(jnp.bfloat16)
            dqkv_t[pl.ds(base, size), q : q + block] = (mm(keys_t, grad_scores) * factor).astype(jnp.bfloat16)
            grad_key += mm(queries_t, grad_scores, NT)
            grad_value += mm(upstream, soft.astype(jnp.bfloat16), NT)
        dqkv_t[pl.ds(base + size, size), :] = (grad_key * factor).astype(jnp.bfloat16)
        dqkv_t[pl.ds(base + 2 * size, size), :] = grad_value.astype(jnp.bfloat16)
        return carry

    lax.fori_loop(0, HEADS, attend_back, 0)

    qkv_acc[...] += mm(normed[...].T, dqkv_t[...], NT)
    gn_t[...] = mm(qkv_w[...], dqkv_t[...])

    def back_sums(at, carry):
        hat = (load(at) - mean) * inverse
        grad = gn_t[:, pl.ds(at, CHUNK)].T
        return (carry[0] + fold(grad * hat), carry[1] + fold(grad))

    zero = jnp.zeros((8, channels), jnp.float32)
    both = chunks(pixels, CHUNK, back_sums, (zero, zero))
    rows = two_rows(*both)
    sums_out[0] = rows
    means = group_total(rows * gain, member[...]) / (pixels * (channels // GROUPS))

    def back_norm(at, carry):
        hat = (load(at) - mean) * inverse
        grad = gn_t[:, pl.ds(at, CHUNK)].T * gain
        back = (grad - means[1:2] - hat * means[0:1]) * inverse
        down_out[0, pl.ds(at, CHUNK), :] = (result[pl.ds(at, CHUNK), :] + back).astype(jnp.bfloat16)
        return carry

    chunks(pixels, CHUNK, back_norm, 0)

    @pl.when(sample == pl.num_programs(0) - 1)
    def _():
        wide = 3 * channels
        shares[:, 0:wide] = mm(order[...], qkv_acc[...].astype(jnp.bfloat16)).astype(jnp.bfloat16)
        shares[:, wide:] = mm(order[...], out_acc[...].astype(jnp.bfloat16)).astype(jnp.bfloat16)


def attention_block(places, scalars, middle, strips, gains, member, qkv_w, out_w, order):
    parts = len(strips)
    samples, pixels, channels = middle.shape
    half = channels // 2
    bf, f32 = jnp.bfloat16, jnp.float32
    return pl.pallas_call(
        functools.partial(attention_kernel, parts),
        grid=(samples,),
        in_specs=[
            pl.BlockSpec(memory_space=pltpu.SMEM),
            pl.BlockSpec(memory_space=pltpu.SMEM),
            each(pixels, channels),
            *[each(pixels // parts, half)] * parts,
            whole(8, channels),
            whole(channels, channels),
            whole(channels, 3 * channels),
            whole(channels, channels),
            whole(channels, channels),
        ],
        out_specs=[
            each(pixels, channels),
            whole(channels, 4 * channels),
            each(8, channels),
            each(8, half),
        ],
        out_shape=[
            jax.ShapeDtypeStruct((samples, pixels, channels), bf),
            jax.ShapeDtypeStruct((channels, 4 * channels), bf),
            jax.ShapeDtypeStruct((samples, 8, channels), f32),
            jax.ShapeDtypeStruct((samples, 8, half), f32),
        ],
        scratch_shapes=[
            pltpu.VMEM((pixels, half), bf),
            pltpu.VMEM((3 * channels, channels), bf),
            pltpu.VMEM((pixels, channels), bf),
            pltpu.VMEM((3 * channels, pixels), bf),
            pltpu.VMEM((HEADS, pixels, pixels), bf),
            pltpu.VMEM((HEADS, 8, pixels), f32),
            pltpu.VMEM((channels, pixels), f32),
            pltpu.VMEM((channels, pixels), bf),
            pltpu.VMEM((pixels, channels), f32),
            pltpu.VMEM((pixels, channels), bf),
            pltpu.VMEM((channels, pixels), bf),
            pltpu.VMEM((3 * channels, pixels), bf),
            pltpu.VMEM((channels, pixels), f32),
            pltpu.VMEM((channels, 3 * channels), f32),
            pltpu.VMEM((channels, channels), f32),
        ],
        compiler_params=pltpu.CompilerParams(vmem_limit_bytes=VMEM_LIMIT),
        cost_estimate=pl.CostEstimate(
            flops=30 * samples * pixels * pixels * channels,
            bytes_accessed=8 * samples * pixels * channels,
            transcendentals=samples * HEADS * pixels * pixels,
        ),
    )(places, scalars, middle, *strips, gains, member, qkv_w, out_w, order)


def fill(padded, at, values, width):
    rows, channels = values.shape
    col = lax.broadcasted_iota(jnp.int32, values.shape, 0) % width
    there = pl.ds(at + width, rows)
    left = jnp.where(col == 0, 0.0, pltpu.roll(values, 1, 0))
    right = jnp.where(col == width - 1, 0.0, pltpu.roll(values, rows - 1, 0))
    padded[there, 0:channels] = left.astype(jnp.bfloat16)
    padded[there, channels : 2 * channels] = values.astype(jnp.bfloat16)
    padded[there, 2 * channels :] = right.astype(jnp.bfloat16)


def clear_edges(padded, width):
    rows, wide = padded.shape
    padded[0:width, :] = jnp.zeros((width, wide), jnp.bfloat16)
    padded[rows - width :, :] = jnp.zeros((width, wide), jnp.bfloat16)


def side(pixels):
    return int(round(pixels**0.5))


def taps_product(padded, weight, pixels, width):
    wide = padded.shape[1]
    total = mm(padded[0:pixels, :], weight(0))
    for i in (1, 2):
        total += mm(padded[i * width : i * width + pixels, :], weight(i))
    return total


def rows_of(*rows):
    index = lax.broadcasted_iota(jnp.int32, (8, rows[0].shape[1]), 0)
    total = jnp.zeros(index.shape, jnp.float32)
    for place, row in enumerate(rows):
        total = jnp.where(index == place, row, total)
    return total


def join_strips(places, strips, joined):
    rows = strips[0].shape[1]
    for far, strip in enumerate(strips):
        joined[pl.ds(pl.multiple_of(places[far] * rows, rows), rows), :] = strip[0]


def first_kernel(parts, places, *refs):
    strips, (gains, member, weight, inner, hidden, stats, images, padded) = refs[:parts], refs[parts:]
    _, pixels, channels = images.shape
    join_strips(places, strips, images.at[0])
    width = side(pixels)
    wide = 3 * channels
    load = lambda at: images[0, pl.ds(at, CHUNK), :].astype(jnp.float32)
    mean, inverse = norm_sums(load, pixels, channels, member[...])
    gain, shift = gains[0:1], gains[1:2]
    clear_edges(padded, width)

    def activate(at, carry):
        out = (load(at) - mean) * inverse * gain + shift
        value = out * jax.nn.sigmoid(out)
        hidden[0, pl.ds(at, CHUNK), :] = value.astype(jnp.bfloat16)
        fill(padded, at, value, width)
        return carry

    chunks(pixels, CHUNK, activate, 0)
    inner[0] = taps_product(padded, lambda i: weight[i * wide : (i + 1) * wide, :], pixels, width)
    mean_two, inverse_two = norm_sums(
        lambda at: inner[0, pl.ds(at, CHUNK), :], pixels, channels, member[...]
    )
    stats[0] = rows_of(mean, inverse, mean_two, inverse_two)


def second_kernel(inner, images, stats, film, gains, weight, middle, hidden, padded):
    _, pixels, channels = inner.shape
    width = side(pixels)
    wide = 3 * channels
    mean, inverse = stats[0, 2:3], stats[0, 3:4]
    scale, lift = 1.0 + film[0, 0:1], film[0, 1:2]
    gain, shift = gains[2:3], gains[3:4]
    clear_edges(padded, width)

    def activate(at, carry):
        out = (inner[0, pl.ds(at, CHUNK), :] - mean) * inverse * gain + shift
        lifted = out * scale + lift
        value = lifted * jax.nn.sigmoid(lifted)
        hidden[0, pl.ds(at, CHUNK), :] = value.astype(jnp.bfloat16)
        fill(padded, at, value, width)
        return carry

    chunks(pixels, CHUNK, activate, 0)
    middle[0] = images[0].astype(jnp.float32) + taps_product(
        padded, lambda i: weight[i * wide : (i + 1) * wide, :], pixels, width
    )


def weights_sums(hidden, grad, padded, total):
    _, pixels, channels = hidden.shape
    width = side(pixels)
    wide = 3 * channels
    clear_edges(padded, width)

    def spread(at, carry):
        fill(padded, at, hidden[0, pl.ds(at, CHUNK), :].astype(jnp.float32), width)
        return carry

    chunks(pixels, CHUNK, spread, 0)

    @pl.when(pl.program_id(0) == 0)
    def _():
        total[...] = jnp.zeros_like(total)

    for i in range(3):
        total[i * wide : (i + 1) * wide, :] += mm(
            padded[i * width : i * width + pixels, :], grad[0], TN
        )


def weights_kernel(hidden, grad, out, padded, total):
    weights_sums(hidden, grad, padded, total)

    @pl.when(pl.program_id(0) == pl.num_programs(0) - 1)
    def _():
        out[...] = total[...].astype(jnp.bfloat16)


def shares_kernel(extra, place, hidden, grad, *refs):
    others, (mine, theirs, padded, total) = refs[:extra], refs[extra:]
    weights_sums(hidden, grad, padded, total)
    classes = mine.shape[0]
    channels = total.shape[1]
    rows = total.shape[0] // (2 * classes)

    @pl.when(pl.program_id(0) == pl.num_programs(0) - 1)
    def _():
        for far in range(classes):
            for last, out in enumerate((mine, theirs)):
                owner = far * 2 + (place[0] ^ last)
                parts = [total[pl.ds(pl.multiple_of(owner * rows, 8), rows), :]]
                for other in others:
                    lines = other.shape[0] // (2 * classes)
                    at = (last * classes + far) * lines
                    for k in range(other.shape[1] // channels):
                        piece = other[at : at + lines, k * channels : (k + 1) * channels]
                        parts.append(piece.astype(jnp.float32))
                out[far] = jnp.concatenate(parts, axis=0).astype(jnp.bfloat16)


def turn_taps(weight, turned):
    channels = weight.shape[1]
    for i in range(3):
        for j in range(3):
            tap = 3 * (2 - i) + 2 - j
            turned[i, :, j * channels : (j + 1) * channels] = weight[
                tap * channels : (tap + 1) * channels, :
            ]


def input_grad(grad, weight, padded, turned, down):
    _, pixels, channels = grad.shape
    width = side(pixels)

    @pl.when(pl.program_id(0) == 0)
    def _():
        turn_taps(weight, turned)

    clear_edges(padded, width)

    def spread(at, carry):
        fill(padded, at, grad[0, pl.ds(at, CHUNK), :].astype(jnp.float32), width)
        return carry

    chunks(pixels, CHUNK, spread, 0)
    total = mm(padded[0:pixels, :], turned[0], NT)
    for i in (1, 2):
        total += mm(padded[i * width : i * width + pixels, :], turned[i], NT)
    down[...] = total


def slope_of(values):
    sig = jax.nn.sigmoid(values)
    return sig * (1.0 + values * (1.0 - sig))


def second_back_kernel(
    grad, inner, stats, film, gains, member, weight, grad_out, sums_out, padded, turned, down
):
    _, pixels, channels = grad.shape
    input_grad(grad, weight, padded, turned, down)
    mean, inverse = stats[0, 2:3], stats[0, 3:4]
    scale, lift = 1.0 + film[0, 0:1], film[0, 1:2]
    gain, shift = gains[2:3], gains[3:4]

    def slopes(at, carry):
        hat = (inner[0, pl.ds(at, CHUNK), :] - mean) * inverse
        lifted = (hat * gain + shift) * scale + lift
        lifted_grad = down[pl.ds(at, CHUNK), :] * slope_of(lifted)
        down[pl.ds(at, CHUNK), :] = lifted_grad
        return (carry[0] + fold(lifted_grad * hat), carry[1] + fold(lifted_grad))

    zero = jnp.zeros((8, channels), jnp.float32)
    rows = two_rows(*chunks(pixels, CHUNK, slopes, (zero, zero)))
    sums_out[0] = rows
    factor = scale * gain
    means = group_total(rows * factor, member[...]) / (pixels * (channels // GROUPS))

    def back_norm(at, carry):
        hat = (inner[0, pl.ds(at, CHUNK), :] - mean) * inverse
        back = (down[pl.ds(at, CHUNK), :] * factor - means[1:2] - hat * means[0:1]) * inverse
        grad_out[0, pl.ds(at, CHUNK), :] = back.astype(jnp.bfloat16)
        return carry

    chunks(pixels, CHUNK, back_norm, 0)


def first_back_kernel(grad, images, stats, gains, weight, sums_out, padded, turned, down):
    _, pixels, channels = grad.shape
    input_grad(grad, weight, padded, turned, down)
    mean, inverse = stats[0, 0:1], stats[0, 1:2]
    gain, shift = gains[0:1], gains[1:2]

    def slopes(at, carry):
        hat = (images[0, pl.ds(at, CHUNK), :].astype(jnp.float32) - mean) * inverse
        grad_first = down[pl.ds(at, CHUNK), :] * slope_of(hat * gain + shift)
        return (carry[0] + fold(grad_first * hat), carry[1] + fold(grad_first))

    zero = jnp.zeros((8, channels), jnp.float32)
    sums_out[0] = two_rows(*chunks(pixels, CHUNK, slopes, (zero, zero)))


def whole(*shape):
    return pl.BlockSpec(shape, lambda s: (0,) * len(shape))


def each(*shape):
    return pl.BlockSpec((1,) + shape, lambda s: (s,) + (0,) * len(shape))


def per_sample(kernel, samples, in_specs, outs, scratch, flops, *operands):
    return pl.pallas_call(
        kernel,
        grid=(samples,),
        in_specs=in_specs,
        out_specs=[spec for spec, _ in outs],
        out_shape=[shape for _, shape in outs],
        scratch_shapes=scratch,
        compiler_params=pltpu.CompilerParams(vmem_limit_bytes=VMEM_LIMIT),
        cost_estimate=pl.CostEstimate(flops=flops, bytes_accessed=flops // 1000, transcendentals=0),
    )(*operands)


def sized(dtype, *shape):
    return jax.ShapeDtypeStruct(shape, dtype)


def block_calls(samples, pixels, channels):
    width = side(pixels)
    act = each(pixels, channels)
    few = each(8, channels)
    gain_spec, member_spec = whole(8, channels), whole(channels, channels)
    weight_spec = whole(9 * channels, channels)
    bf, f32 = jnp.bfloat16, jnp.float32
    padded = pltpu.VMEM((pixels + 2 * width, 3 * channels), bf)
    turned = pltpu.VMEM((3, channels, 3 * channels), bf)
    down = pltpu.VMEM((pixels, channels), f32)
    act_b = sized(bf, samples, pixels, channels)
    act_f = sized(f32, samples, pixels, channels)
    few_f = sized(f32, samples, 8, channels)
    flops = 18 * samples * pixels * channels * channels

    def first(places, strips, gains, member, weight):
        parts = len(strips)
        return per_sample(
            functools.partial(first_kernel, parts), samples,
            [pl.BlockSpec(memory_space=pltpu.SMEM)] + [each(pixels // parts, channels)] * parts
            + [gain_spec, member_spec, weight_spec],
            [(act, act_f), (act, act_b), (few, few_f), (act, act_b)], [padded], flops,
            places, *strips, gains, member, weight,
        )

    def second(inner, images, stats, film, gains, weight):
        return per_sample(
            second_kernel, samples, [act, act, few, few, gain_spec, weight_spec],
            [(act, act_f), (act, act_b)], [padded], flops,
            inner, images, stats, film, gains, weight,
        )

    def weights(hidden, grad, place, classes, others=()):
        scratch = [padded, pltpu.VMEM((9 * channels, channels), f32)]
        conv_rows = 9 * channels // (2 * classes)
        more = [other.shape[0] * other.shape[1] // (2 * classes * channels) for other in others]
        if conv_rows % 8:
            (whole_grad,) = per_sample(
                weights_kernel, samples, [act, act],
                [(weight_spec, sized(bf, 9 * channels, channels))], scratch, flops, hidden, grad,
            )
            blocks = whole_grad.reshape(2 * classes, conv_rows, channels)
            both = []
            for last in range(2):
                owner = place[0] ^ last
                cut = blocks.reshape(classes, 2, conv_rows, channels)
                parts = [lax.dynamic_index_in_dim(cut, owner, 1, keepdims=False)]
                for other in others:
                    cut = other.reshape(2, classes, -1, other.shape[1] // channels, channels)[last]
                    parts.append(jnp.moveaxis(cut, 2, 1).reshape(classes, -1, channels))
                both.append(jnp.concatenate(parts, axis=1))
            return both
        shape = (classes, conv_rows + sum(more), channels)
        out = (whole(*shape), sized(bf, *shape))
        return per_sample(
            functools.partial(shares_kernel, len(others)), samples,
            [pl.BlockSpec(memory_space=pltpu.SMEM), act, act] + [whole(*o.shape) for o in others],
            [out, out], scratch, flops, place, hidden, grad, *others,
        )

    def second_back(grad, inner, stats, film, gains, member, weight):
        return per_sample(
            second_back_kernel, samples,
            [act, act, few, few, gain_spec, member_spec, weight_spec],
            [(act, act_b), (few, few_f)], [padded, turned, down], flops,
            grad, inner, stats, film, gains, member, weight,
        )

    def first_back(grad, images, stats, gains, weight):
        return per_sample(
            first_back_kernel, samples, [act, act, few, gain_spec, weight_spec],
            [(few, few_f)], [padded, turned, down], flops,
            grad, images, stats, gains, weight,
        )[0]

    return first, second, weights, second_back, first_back


def adamw(master, gradient, first, second, step_rate, decay_rate, clip_factor):
    gradient = gradient * clip_factor
    first_new = BETA_ONE * first + (1.0 - BETA_ONE) * gradient
    second_new = BETA_TWO * second + (1.0 - BETA_TWO) * gradient * gradient
    ratio = (
        first_new
        / (1.0 - BETA_ONE**STEP)
        / (jnp.sqrt(second_new / (1.0 - BETA_TWO**STEP)) + ADAM_EPS)
    )
    return (master - step_rate * (ratio + decay_rate * master), first_new, second_new)


def body(
    images,
    noise,
    timesteps,
    extents,
    film_master,
    conv_master,
    qkv_master,
    out_master,
    gains,
    film_first,
    film_second,
    conv_first,
    conv_second,
    qkv_first,
    qkv_second,
    out_first,
    out_second,
    gain_first,
    gain_second,
):
    devices = lax.axis_size("dp") * lax.axis_size("head")
    device = lax.axis_index("dp") * lax.axis_size("head") + lax.axis_index("head")
    channels = images.shape[-1]
    wide = film_master.shape[1]
    half_width = channels // 2
    conv_rows = conv_master.shape[0]
    film_rows = film_master.shape[0]
    out_rows = out_master.shape[0]

    local_samples = timesteps.shape[0]
    small = jnp.concatenate(
        [
            gains.reshape(-1),
            extents.astype(jnp.float32).reshape(-1),
            (timesteps // 64).astype(jnp.float32),
            (timesteps % 64).astype(jnp.float32),
        ]
    )
    small = jnp.pad(small, (0, 8 * channels - small.shape[0])).reshape(8, channels)
    classes = class_count()
    top_mask = devices // 2
    is_top = device >= top_mask
    film_cut = film_rows * wide // channels
    ours = jnp.concatenate([conv_master, small, film_master.reshape(-1, channels)])
    ours = ours.astype(jnp.bfloat16)
    theirs = exchange(ours, top_mask)
    strips = strips_of(images)
    low, high = jnp.where(is_top, theirs, ours), jnp.where(is_top, ours, theirs)
    small_two = [part[conv_rows : conv_rows + 8] for part in (low, high)]
    film_two = [part[conv_rows + 8 :] for part in (low, high)]
    every_one = gather_classes(jnp.concatenate([low[:conv_rows]] + small_two + film_two))
    rest = jnp.concatenate([qkv_master.reshape(-1, channels), out_master]).astype(jnp.bfloat16)
    rest = behind(rest, theirs)
    rest_two = pair_up(rest, exchange(rest, top_mask), jnp.logical_not(is_top), 0)
    every_two = gather_classes(
        behind(jnp.concatenate([high[:conv_rows], rest_two.reshape(-1, channels)]), every_one)
    )
    taps_one, smalls, film_w = finish_gather(
        behind(every_one, *strips), [conv_rows, 16, 2 * film_cut]
    )
    taps_one = taps_one.reshape(-1, channels)
    smalls = jnp.moveaxis(smalls.reshape(-1, 2, 8 * channels), 0, 1)
    smalls = smalls.reshape(devices, -1).astype(jnp.float32)
    gain_f = smalls[:, : gains.size].reshape(channels, 6)
    dp_smalls = smalls.reshape(lax.axis_size("dp"), lax.axis_size("head"), -1)[:, 0, gains.size :]
    extents_all = dp_smalls[:, : 2 * local_samples].reshape(-1, 2)
    times = dp_smalls[:, 2 * local_samples : 4 * local_samples].reshape(-1, 2, local_samples)
    times_all = (times[:, 0] * 64.0 + times[:, 1]).reshape(-1).astype(jnp.int32)
    divisor = jnp.sum(extents_all[:, 0] * extents_all[:, 1])

    parts = lax.axis_size("head")
    samples, strip_rows, width_px, _ = strips[0].shape
    places = lax.axis_index("head") ^ jnp.arange(parts, dtype=jnp.int32)
    rows = strip_rows * parts
    pixels = rows * width_px
    first = lax.axis_index("head") * samples
    own_times = lax.dynamic_slice_in_dim(timesteps, first, samples)
    own_extents = lax.dynamic_slice_in_dim(extents, first, samples)

    log_beta, log_tilde, factor = plan(own_times)
    embedded_all = jax.nn.silu(embed(times_all, wide)).astype(jnp.bfloat16)
    embedded = jax.nn.silu(embed(own_times, wide)).astype(jnp.bfloat16)
    gains_t = jnp.pad(gain_f.T, ((0, 2), (0, 0)))
    member = jnp.asarray(np.kron(np.eye(GROUPS), np.ones((channels // GROUPS,) * 2)), jnp.bfloat16)
    scalars = jnp.stack(
        [log_beta, log_tilde, factor, jnp.broadcast_to(divisor, factor.shape)]
        + [own_extents[:, 0].astype(jnp.float32), own_extents[:, 1].astype(jnp.float32)],
        axis=1,
    )
    first_call, second_call, weights, second_back, first_back = block_calls(samples, pixels, channels)
    flat = lambda values: [v.reshape(samples, strip_rows * width_px, -1) for v in values]
    inner, hidden_one, stats, source = first_call(places, flat(strips), gains_t, member, taps_one)
    taps_two, others = finish_gather(behind(every_two, inner), [conv_rows, 8 * out_rows])
    taps_two = taps_two.reshape(-1, channels)
    film_w = jnp.moveaxis(film_w.reshape(-1, 2, film_cut, channels), 0, 1).reshape(-1, wide)
    others = jnp.moveaxis(others.reshape(-1, 2, 4 * out_rows, channels), 0, 1)
    others = others.reshape(devices, 4 * out_rows, channels)
    qkv_w = others[:, : 3 * out_rows].reshape(channels, 3 * channels)
    out_w = others[:, 3 * out_rows :].reshape(channels, channels)
    noise_strips = strips_of(behind(noise, inner))
    film_out = lax.dot_general(
        embedded, film_w, (((1,), (1,)), ((), ())), preferred_element_type=jnp.float32
    )
    film = jnp.pad(film_out.reshape(samples, 2, channels), ((0, 0), (0, 6), (0, 0)))
    scale = 1.0 + film_out[:, :channels]
    middle, hidden_two = second_call(inner, source, stats, film, gains_t, taps_two)
    my_last = last_bit()
    place = my_last.reshape(1).astype(jnp.int32)
    line = jnp.arange(channels, dtype=jnp.int32)
    owner, spot = line // out_rows, line % out_rows
    source_device = (
        (owner % 2) * 2 * classes + (owner // 2 % classes) * 2 + (my_last ^ (owner // (2 * classes)))
    )
    order = (line[None, :] == (source_device * out_rows + spot)[:, None]).astype(jnp.bfloat16)
    grad_two_b, shares, sums_three, losses = attention_block(
        places, scalars, middle, flat(noise_strips), gains_t, member, qkv_w, out_w, order
    )
    loss_local = jnp.sum(losses)
    two_shares = weights(hidden_two, grad_two_b, place, classes, (shares,))
    grad_two_b = behind(grad_two_b, *two_shares)
    grad_one_b, sums_two = second_back(grad_two_b, inner, stats, film, gains_t, member, taps_two)
    two_sent = (two_shares[0].astype(jnp.float32) + exchange(two_shares[1], 1).astype(jnp.float32)).astype(jnp.bfloat16)
    share_two = jnp.sum(across_classes(two_sent).astype(jnp.float32), axis=0)
    one_shares = weights(behind(hidden_one, two_sent), grad_one_b, place, classes)
    one_sent = (one_shares[0].astype(jnp.float32) + exchange(one_shares[1], 1).astype(jnp.float32)).astype(jnp.bfloat16)
    share_one = jnp.sum(across_classes(one_sent).astype(jnp.float32), axis=0)
    grad_one_b = behind(grad_one_b, share_two, one_sent)
    sums_one = first_back(grad_one_b, source, stats, gains_t, taps_one)
    gain_one, bias_one = jnp.sum(sums_one[:, 0], axis=0), jnp.sum(sums_one[:, 1], axis=0)
    gain_two, bias_two = jnp.sum(sums_two[:, 0] * scale, axis=0), jnp.sum(sums_two[:, 1] * scale, axis=0)
    gain_three, bias_three = jnp.sum(sums_three[:, 0], axis=0), jnp.sum(sums_three[:, 1], axis=0)
    grad_scale = sums_two[:, 0] * gains_t[2] + sums_two[:, 1] * gains_t[3]
    film_grad_b = jnp.concatenate([grad_scale, sums_two[:, 1]], axis=1).astype(jnp.bfloat16)

    small_shares = share_two[conv_rows:].reshape(4, 2, out_rows, channels)
    keep_two = jnp.where(is_top, small_shares[:, 1], small_shares[:, 0])
    send_two = jnp.where(is_top, small_shares[:, 0], small_shares[:, 1])
    send_two = jnp.concatenate([share_two[:conv_rows], send_two.reshape(-1, channels)])
    got_two = exchange(send_two.astype(jnp.bfloat16), top_mask).astype(jnp.float32)
    got_one = exchange(share_one.astype(jnp.bfloat16), top_mask).astype(jnp.float32)
    conv_g = jnp.where(is_top, share_two[:conv_rows] + got_two[:conv_rows], share_one + got_one)
    small_g = keep_two + got_two[conv_rows:].reshape(keep_two.shape)
    qkv_g = jnp.concatenate([small_g[0], small_g[1], small_g[2]], axis=1)
    out_g = small_g[3]

    gain_grad = jnp.stack([gain_one, bias_one, gain_two, bias_two, gain_three, bias_three], axis=1)
    common = jnp.concatenate([film_grad_b.astype(jnp.float32).reshape(-1), loss_local[None]])
    parcel = jnp.concatenate(
        [
            behind(gain_grad, share_one).reshape(devices, -1),
            jnp.broadcast_to(common[None], (devices, common.shape[0])),
        ],
        axis=1,
    )
    length = parcel.shape[1]
    parcel = jnp.pad(parcel, ((0, 0), (0, -length % 1024))).reshape(devices, -1, 128)
    parcels = to_all(parcel).reshape(devices, -1)
    gain_g = jnp.sum(parcels[:, : gains.size], axis=0).reshape(gains.shape)
    film_all = parcels[:, gains.size : length - 1].reshape(-1, film_grad_b.shape[1])
    loss_total = jnp.sum(parcels[:, length - 1])
    film_own = lax.dynamic_slice_in_dim(film_all, device * film_rows, film_rows, axis=1)
    film_g = jnp.einsum(
        "sf,se->fe", film_own.astype(jnp.bfloat16), embedded_all, preferred_element_type=jnp.float32
    )
    reduced = (film_g, conv_g, qkv_g, out_g, gain_g)
    squares = jnp.zeros((), jnp.float32)
    for gradient in reduced:
        squares = squares + jnp.sum(gradient * gradient)
    grad_norm = jnp.sqrt(jnp.sum(to_all(jnp.broadcast_to(squares, (devices, 8, 128)))[:, 0, 0]))
    clip_factor = jnp.minimum(1.0, THRESHOLD / (grad_norm + 1e-06))
    film_res = adamw(film_master, film_g, film_first, film_second, RATE_MATRIX, DECAY, clip_factor)
    conv_res = adamw(conv_master, conv_g, conv_first, conv_second, RATE_MATRIX, DECAY, clip_factor)
    qkv_res = adamw(qkv_master, qkv_g, qkv_first, qkv_second, RATE_MATRIX, DECAY, clip_factor)
    out_res = adamw(out_master, out_g, out_first, out_second, RATE_MATRIX, DECAY, clip_factor)
    gain_res = adamw(gains, gain_g, gain_first, gain_second, RATE_GAIN, 0.0, clip_factor)
    loss_parts = jnp.stack([loss_total, divisor])
    return (
        loss_parts,
        grad_norm,
        film_res[0],
        film_res[1],
        film_res[2],
        conv_res[0],
        conv_res[1],
        conv_res[2],
        qkv_res[0],
        qkv_res[1],
        qkv_res[2],
        out_res[0],
        out_res[1],
        out_res[2],
        gain_res[0],
        gain_res[1],
        gain_res[2],
    )


def solution(mesh):
    in_specs = (
        P("dp", "head", None, None),
        P("dp", "head", None, None),
        P("dp"),
        P("dp", None),
        P(("dp", "head"), None),
        P(("dp", "head"), None),
        P(("dp", "head"), None),
        P(("dp", "head"), None),
        P(("dp", "head"), None),
        P(("dp", "head"), None),
        P(("dp", "head"), None),
        P(("dp", "head"), None),
        P(("dp", "head"), None),
        P(("dp", "head"), None),
        P(("dp", "head"), None),
        P(("dp", "head"), None),
        P(("dp", "head"), None),
        P(("dp", "head"), None),
        P(("dp", "head"), None),
    )
    out_specs = (
        P(),
        P(),
        P(("dp", "head"), None),
        P(("dp", "head"), None),
        P(("dp", "head"), None),
        P(("dp", "head"), None),
        P(("dp", "head"), None),
        P(("dp", "head"), None),
        P(("dp", "head"), None),
        P(("dp", "head"), None),
        P(("dp", "head"), None),
        P(("dp", "head"), None),
        P(("dp", "head"), None),
        P(("dp", "head"), None),
        P(("dp", "head"), None),
        P(("dp", "head"), None),
        P(("dp", "head"), None),
    )
    return jax.shard_map(body, mesh=mesh, in_specs=in_specs, out_specs=out_specs, check_vma=False)
```

```python
import functools
import math

import jax
import jax.numpy as jnp
import numpy as np
from jax import lax
from jax.experimental import pallas as pl
from jax.experimental.pallas import tpu as pltpu
from jax.sharding import PartitionSpec as P

HEADS = 4
GROUPS = 32
STEP = 10
TSTEPS = 4000


EPS_NORM = 1e-05
VLB_WEIGHT = 0.001
BETA_ONE = 0.9
BETA_TWO = 0.999
ADAM_EPS = 1e-08
DECAY = 0.01
RATE_MATRIX = 0.05
RATE_GAIN = 0.4
THRESHOLD = 0.002
OFFSET = 0.008
LOG2E = math.log2(math.e)
VMEM_LIMIT = 56 << 20


def plan(step_ids):
    moment = step_ids.astype(jnp.float32)

    def angle(values):
        return (values / TSTEPS + OFFSET) / (1.0 + OFFSET) * (0.5 * math.pi)

    start = angle(jnp.zeros_like(moment))
    before = angle(moment - 1.0)
    later_angle = angle(moment)
    beta_now = jnp.sin(later_angle - before) * jnp.sin(later_angle + before) / jnp.cos(before) ** 2
    fade_now = jnp.sin(later_angle - start) * jnp.sin(later_angle + start) / jnp.cos(start) ** 2
    fade_prev = jnp.sin(before - start) * jnp.sin(before + start) / jnp.cos(start) ** 2
    log_beta = jnp.log(beta_now)
    log_tilde = jnp.log(beta_now * fade_prev / fade_now)
    factor = beta_now * beta_now / ((1.0 - beta_now) * fade_now)
    return (log_beta, log_tilde, factor)


def embed(step_ids, width):
    half_width = width // 2
    frequency = jnp.exp(-math.log(10000.0) * jnp.arange(half_width, dtype=jnp.float32) / half_width)
    phases = step_ids.astype(jnp.float32)[:, None] * frequency[None, :]
    return jnp.concatenate([jnp.cos(phases), jnp.sin(phases)], axis=1)


def behind(values, *others):
    return lax.optimization_barrier((values,) + others)[0]


def pair_up(block, other, low, place):
    shape = [2 if dim == place else 1 for dim in range(block.ndim + 1)]
    first = jnp.arange(2, dtype=jnp.int32).reshape(shape) == 0
    return jnp.where(first == low, jnp.expand_dims(block, place), jnp.expand_dims(other, place))


def class_count():
    return lax.axis_size("dp") * lax.axis_size("head") // 4


def last_bit():
    return lax.axis_index("head") % 2


def exchange(values, mask):
    size = lax.axis_size("dp") * lax.axis_size("head")
    return lax.ppermute(values, ("dp", "head"), [(i, i ^ mask) for i in range(size)])


def across_classes(blocks):
    count = class_count()
    groups = [
        [(high * count + k) * 2 + last for k in range(count)] for high in range(2) for last in range(2)
    ]
    return lax.all_to_all(
        blocks, ("dp", "head"), split_axis=0, concat_axis=0, axis_index_groups=groups, tiled=True
    )


def gather_classes(block):
    return across_classes(jnp.broadcast_to(block[None], (class_count(),) + block.shape))


def finish_gather(both, parts):
    other = exchange(both, 1)
    low = last_bit() == 0
    joined, at = [], 0
    for rows in parts:
        piece = pair_up(both[:, at : at + rows], other[:, at : at + rows], low, 1)
        joined.append(piece.reshape((-1,) + piece.shape[2:]))
        at += rows
    return joined


def to_all(blocks):
    return lax.all_to_all(blocks, ("dp", "head"), split_axis=0, concat_axis=0, tiled=True)


def strips_of(values):
    parts = lax.axis_size("head")
    count = values.shape[0] // parts
    mine = lax.axis_index("head")
    strips = []
    for far in range(parts):
        strip = lax.dynamic_slice_in_dim(values, (mine ^ far) * count, count, axis=0)
        if far:
            strip = lax.ppermute(strip, "head", [(i, i ^ far) for i in range(parts)])
        strips.append(strip)
    return strips


NN = (((1,), (0,)), ((), ()))
NT = (((1,), (1,)), ((), ()))
TN = (((0,), (0,)), ((), ()))


def mm(left, right, form=NN):
    return lax.dot_general(left, right, form, preferred_element_type=jnp.float32)


def group_total(rows, member):
    high = rows.astype(jnp.bfloat16).astype(jnp.float32)
    rest = rows - high
    mid = rest.astype(jnp.bfloat16).astype(jnp.float32)
    parts = jnp.concatenate([high, mid, rest - mid, jnp.zeros_like(rows)], axis=0)
    sums = mm(parts.astype(jnp.bfloat16), member)
    return sums[0:8] + sums[8:16] + sums[16:24]


def fold(values):
    rows, width = values.shape
    return jnp.sum(values.reshape(rows // 8, 8, width), axis=0)


def two_rows(first, second):
    first = jnp.sum(first, axis=0, keepdims=True)
    second = jnp.sum(second, axis=0, keepdims=True)
    row = lax.broadcasted_iota(jnp.int32, (8, first.shape[1]), 0)
    return jnp.where(row == 0, first, jnp.where(row == 1, second, 0.0))


def chunks(total, size, step, init):
    return lax.fori_loop(0, total // size, lambda m, c: step(pl.multiple_of(m * size, size), c), init)


def norm_sums(load, pixels, channels, member):
    def step(at, carry):
        values = load(at)
        return (carry[0] + fold(values), carry[1] + fold(values * values))

    zero = jnp.zeros((8, channels), jnp.float32)
    first, second = chunks(pixels, CHUNK, step, (zero, zero))
    count = pixels * (channels // GROUPS)
    sums = group_total(two_rows(first, second), member) / count
    mean = sums[0:1]
    inverse = lax.rsqrt(sums[1:2] - mean * mean + EPS_NORM)
    return mean, inverse


CHUNK = 256


def attention_kernel(parts, places, scalars, middle, *refs):
    attention_body(places, scalars, middle, refs[:parts], *refs[parts:])


def attention_body(
    places,
    scalars,
    middle,
    strips,
    gains,
    member,
    qkv_w,
    out_w,
    order,
    down_out,
    shares,
    sums_out,
    loss_out,
    noise,
    qkv_wt,
    normed,
    qkv_t,
    probs,
    totals,
    mixed_t,
    attn_t,
    result,
    grad_b,
    back_t,
    dqkv_t,
    gn_t,
    qkv_acc,
    out_acc,
):
    sample = pl.program_id(0)
    _, pixels, channels = middle.shape
    half = channels // 2
    size = channels // HEADS
    factor = size ** (-0.5)
    width = int(round(pixels**0.5))

    @pl.when(sample == 0)
    def _():
        qkv_wt[...] = qkv_w[...].T
        qkv_acc[...] = jnp.zeros_like(qkv_acc)
        out_acc[...] = jnp.zeros_like(out_acc)

    join_strips(places, strips, noise)
    load = lambda at: middle[0, pl.ds(at, CHUNK), :]
    mean, inverse = norm_sums(load, pixels, channels, member[...])
    gain, shift = gains[4:5], gains[5:6]

    def normalize(at, carry):
        hat = (load(at) - mean) * inverse
        normed[pl.ds(at, CHUNK), :] = (hat * gain + shift).astype(jnp.bfloat16)
        return carry

    chunks(pixels, CHUNK, normalize, 0)

    block = 256

    qkv_t[...] = mm(qkv_wt[...], normed[...], NT).astype(jnp.bfloat16)

    def rows_of_head(head, part):
        at = (3 * head + part) * size
        return slice(at, at + size)

    def scores_of(head):
        return mm(qkv_t[rows_of_head(head, 1), :].T, qkv_t[rows_of_head(head, 0), :])

    following = scores_of(0)
    for head in range(HEADS):
        scores = following
        if head + 1 < HEADS:
            following = scores_of(head + 1)
        top = jnp.max(scores, axis=0, keepdims=True)
        powers = jnp.exp2((scores - top) * (factor * LOG2E))
        inv = 1.0 / jnp.sum(powers, axis=0, keepdims=True)
        powers_b = powers.astype(jnp.bfloat16)
        probs[head] = powers_b
        totals[head] = jnp.broadcast_to(inv, (8, pixels))
        mixed = mm(qkv_t[rows_of_head(head, 2), :], powers_b) * inv
        at = slice(head * size, (head + 1) * size)
        mixed_t[at, :] = mixed
        attn_t[at, :] = mixed.astype(jnp.bfloat16)

    result[...] = mm(attn_t[...].T, out_w[...])
    beta_log, tilde_log, coef = scalars[sample, 0], scalars[sample, 1], scalars[sample, 2]
    divisor, high, wide = scalars[sample, 3], scalars[sample, 4], scalars[sample, 5]

    def losses(at, carry):
        total = load(at) + result[pl.ds(at, CHUNK), :]
        pixel = at + lax.broadcasted_iota(jnp.int32, (CHUNK, half), 0)
        row = (pixel // width).astype(jnp.float32)
        col = (pixel % width).astype(jnp.float32)
        valid = jnp.where((row >= width - high) & (col < wide), 1.0, 0.0)
        residue = total[:, :half] - noise[pl.ds(at, CHUNK), :].astype(jnp.float32)
        weight = jax.nn.sigmoid(total[:, half:])
        blended = weight * beta_log + (1.0 - weight) * tilde_log
        spread = jnp.exp(tilde_log - blended)
        damped = coef * residue * residue * jnp.exp(-blended)
        diverge = 0.5 * (-1.0 + blended - tilde_log + spread + damped)
        pixel_loss = valid * (residue * residue + VLB_WEIGHT * diverge)
        scale = valid / (half * divisor)
        grad_guess = 2.0 * residue * scale
        grad_raw = (
            scale * (0.5 * VLB_WEIGHT) * (1.0 - spread - damped)
            * (beta_log - tilde_log) * weight * (1.0 - weight)
        )
        grad = jnp.concatenate([grad_guess, grad_raw], axis=-1)
        result[pl.ds(at, CHUNK), :] = grad
        grad_b[pl.ds(at, CHUNK), :] = grad.astype(jnp.bfloat16)
        return carry + fold(pixel_loss)

    loss = chunks(pixels, CHUNK, losses, jnp.zeros((8, half), jnp.float32))
    loss_out[0] = loss * (1.0 / half)

    out_acc[...] += mm(attn_t[...], grad_b[...])
    back_t[...] = mm(out_w[...], grad_b[...], NT).astype(jnp.bfloat16)

    def upstream_of(head):
        return back_t[head * size : (head + 1) * size, :]

    def soft_grad(head):
        return mm(qkv_t[rows_of_head(head, 2), :].T, upstream_of(head))

    following = soft_grad(0)
    for head in range(HEADS):
        grad_soft = following
        if head + 1 < HEADS:
            following = soft_grad(head + 1)
        upstream = upstream_of(head)
        inner = jnp.sum(
            upstream.astype(jnp.float32) * mixed_t[head * size : (head + 1) * size, :],
            axis=0,
            keepdims=True,
        )
        soft = probs[head].astype(jnp.float32) * totals[head, 0:1]
        grad_scores = (soft * (grad_soft - inner)).astype(jnp.bfloat16)
        queries_t, keys_t = qkv_t[rows_of_head(head, 0), :], qkv_t[rows_of_head(head, 1), :]
        dqkv_t[rows_of_head(head, 0), :] = (mm(keys_t, grad_scores) * factor).astype(jnp.bfloat16)
        dqkv_t[rows_of_head(head, 1), :] = (mm(queries_t, grad_scores, NT) * factor).astype(jnp.bfloat16)
        dqkv_t[rows_of_head(head, 2), :] = mm(upstream, soft.astype(jnp.bfloat16), NT).astype(jnp.bfloat16)

    qkv_acc[...] += mm(normed[...].T, dqkv_t[...], NT)
    gn_t[...] = mm(qkv_w[...], dqkv_t[...]).T

    def back_sums(at, carry):
        hat = (load(at) - mean) * inverse
        grad = gn_t[pl.ds(at, CHUNK), :]
        return (carry[0] + fold(grad * hat), carry[1] + fold(grad))

    zero = jnp.zeros((8, channels), jnp.float32)
    both = chunks(pixels, CHUNK, back_sums, (zero, zero))
    rows = two_rows(*both)
    sums_out[0] = rows
    means = group_total(rows * gain, member[...]) / (pixels * (channels // GROUPS))

    def back_norm(at, carry):
        hat = (load(at) - mean) * inverse
        grad = gn_t[pl.ds(at, CHUNK), :] * gain
        back = (grad - means[1:2] - hat * means[0:1]) * inverse
        down_out[0, pl.ds(at, CHUNK), :] = (result[pl.ds(at, CHUNK), :] + back).astype(jnp.bfloat16)
        return carry

    chunks(pixels, CHUNK, back_norm, 0)

    @pl.when(sample == pl.num_programs(0) - 1)
    def _():
        wide = 3 * channels
        shares[:, 0:wide] = mm(order[...], qkv_acc[...].astype(jnp.bfloat16)).astype(jnp.bfloat16)
        shares[:, wide:] = mm(order[...], out_acc[...].astype(jnp.bfloat16)).astype(jnp.bfloat16)


def attention_block(places, scalars, middle, strips, gains, member, qkv_w, out_w, order):
    parts = len(strips)
    samples, pixels, channels = middle.shape
    half = channels // 2
    bf, f32 = jnp.bfloat16, jnp.float32
    return pl.pallas_call(
        functools.partial(attention_kernel, parts),
        grid=(samples,),
        in_specs=[
            pl.BlockSpec(memory_space=pltpu.SMEM),
            pl.BlockSpec(memory_space=pltpu.SMEM),
            each(pixels, channels),
            *[each(pixels // parts, half)] * parts,
            whole(8, channels),
            whole(channels, channels),
            whole(channels, 3 * channels),
            whole(channels, channels),
            whole(channels, channels),
        ],
        out_specs=[
            each(pixels, channels),
            whole(channels, 4 * channels),
            each(8, channels),
            each(8, half),
        ],
        out_shape=[
            jax.ShapeDtypeStruct((samples, pixels, channels), bf),
            jax.ShapeDtypeStruct((channels, 4 * channels), bf),
            jax.ShapeDtypeStruct((samples, 8, channels), f32),
            jax.ShapeDtypeStruct((samples, 8, half), f32),
        ],
        scratch_shapes=[
            pltpu.VMEM((pixels, half), bf),
            pltpu.VMEM((3 * channels, channels), bf),
            pltpu.VMEM((pixels, channels), bf),
            pltpu.VMEM((3 * channels, pixels), bf),
            pltpu.VMEM((HEADS, pixels, pixels), bf),
            pltpu.VMEM((HEADS, 8, pixels), f32),
            pltpu.VMEM((channels, pixels), f32),
            pltpu.VMEM((channels, pixels), bf),
            pltpu.VMEM((pixels, channels), f32),
            pltpu.VMEM((pixels, channels), bf),
            pltpu.VMEM((channels, pixels), bf),
            pltpu.VMEM((3 * channels, pixels), bf),
            pltpu.VMEM((pixels, channels), f32),
            pltpu.VMEM((channels, 3 * channels), f32),
            pltpu.VMEM((channels, channels), f32),
        ],
        compiler_params=pltpu.CompilerParams(vmem_limit_bytes=VMEM_LIMIT),
        cost_estimate=pl.CostEstimate(
            flops=30 * samples * pixels * pixels * channels,
            bytes_accessed=8 * samples * pixels * channels,
            transcendentals=samples * HEADS * pixels * pixels,
        ),
    )(places, scalars, middle, *strips, gains, member, qkv_w, out_w, order)


def fill(padded, at, values, width):
    rows, channels = values.shape
    col = lax.broadcasted_iota(jnp.int32, values.shape, 0) % width
    there = pl.ds(at + width, rows)
    left = jnp.where(col == 0, 0.0, pltpu.roll(values, 1, 0))
    right = jnp.where(col == width - 1, 0.0, pltpu.roll(values, rows - 1, 0))
    padded[there, 0:channels] = left.astype(jnp.bfloat16)
    padded[there, channels : 2 * channels] = values.astype(jnp.bfloat16)
    padded[there, 2 * channels :] = right.astype(jnp.bfloat16)


def clear_edges(padded, width):
    rows, wide = padded.shape
    padded[0:width, :] = jnp.zeros((width, wide), jnp.bfloat16)
    padded[rows - width :, :] = jnp.zeros((width, wide), jnp.bfloat16)


def side(pixels):
    return int(round(pixels**0.5))


def taps_product(padded, weight, pixels, width):
    wide = padded.shape[1]
    total = mm(padded[0:pixels, :], weight(0))
    for i in (1, 2):
        total += mm(padded[i * width : i * width + pixels, :], weight(i))
    return total


def rows_of(*rows):
    index = lax.broadcasted_iota(jnp.int32, (8, rows[0].shape[1]), 0)
    total = jnp.zeros(index.shape, jnp.float32)
    for place, row in enumerate(rows):
        total = jnp.where(index == place, row, total)
    return total


def join_strips(places, strips, joined):
    rows = strips[0].shape[1]
    for far, strip in enumerate(strips):
        joined[pl.ds(pl.multiple_of(places[far] * rows, rows), rows), :] = strip[0]


def first_kernel(parts, places, *refs):
    strips, (gains, member, weight, inner, hidden, stats, images, padded) = refs[:parts], refs[parts:]
    _, pixels, channels = images.shape
    join_strips(places, strips, images.at[0])
    width = side(pixels)
    wide = 3 * channels
    load = lambda at: images[0, pl.ds(at, CHUNK), :].astype(jnp.float32)
    mean, inverse = norm_sums(load, pixels, channels, member[...])
    gain, shift = gains[0:1], gains[1:2]
    clear_edges(padded, width)

    def activate(at, carry):
        out = (load(at) - mean) * inverse * gain + shift
        value = out * jax.nn.sigmoid(out)
        hidden[0, pl.ds(at, CHUNK), :] = value.astype(jnp.bfloat16)
        fill(padded, at, value, width)
        return carry

    chunks(pixels, CHUNK, activate, 0)
    inner[0] = taps_product(padded, lambda i: weight[i * wide : (i + 1) * wide, :], pixels, width)
    mean_two, inverse_two = norm_sums(
        lambda at: inner[0, pl.ds(at, CHUNK), :], pixels, channels, member[...]
    )
    stats[0] = rows_of(mean, inverse, mean_two, inverse_two)


def second_kernel(inner, images, stats, film, gains, weight, middle, hidden, padded):
    _, pixels, channels = inner.shape
    width = side(pixels)
    wide = 3 * channels
    mean, inverse = stats[0, 2:3], stats[0, 3:4]
    scale, lift = 1.0 + film[0, 0:1], film[0, 1:2]
    gain, shift = gains[2:3], gains[3:4]
    clear_edges(padded, width)

    def activate(at, carry):
        out = (inner[0, pl.ds(at, CHUNK), :] - mean) * inverse * gain + shift
        lifted = out * scale + lift
        value = lifted * jax.nn.sigmoid(lifted)
        hidden[0, pl.ds(at, CHUNK), :] = value.astype(jnp.bfloat16)
        fill(padded, at, value, width)
        return carry

    chunks(pixels, CHUNK, activate, 0)
    middle[0] = images[0].astype(jnp.float32) + taps_product(
        padded, lambda i: weight[i * wide : (i + 1) * wide, :], pixels, width
    )


def weights_sums(hidden, grad, padded, total):
    _, pixels, channels = hidden.shape
    width = side(pixels)
    wide = 3 * channels
    clear_edges(padded, width)

    def spread(at, carry):
        fill(padded, at, hidden[0, pl.ds(at, CHUNK), :].astype(jnp.float32), width)
        return carry

    chunks(pixels, CHUNK, spread, 0)

    @pl.when(pl.program_id(0) == 0)
    def _():
        total[...] = jnp.zeros_like(total)

    for i in range(3):
        total[i * wide : (i + 1) * wide, :] += mm(
            padded[i * width : i * width + pixels, :], grad[0], TN
        )


def weights_kernel(hidden, grad, out, padded, total):
    weights_sums(hidden, grad, padded, total)

    @pl.when(pl.program_id(0) == pl.num_programs(0) - 1)
    def _():
        out[...] = total[...].astype(jnp.bfloat16)


def shares_kernel(extra, place, hidden, grad, *refs):
    others, (mine, theirs, padded, total) = refs[:extra], refs[extra:]
    weights_sums(hidden, grad, padded, total)
    classes = mine.shape[0]
    channels = total.shape[1]
    rows = total.shape[0] // (2 * classes)

    @pl.when(pl.program_id(0) == pl.num_programs(0) - 1)
    def _():
        for far in range(classes):
            for last, out in enumerate((mine, theirs)):
                owner = far * 2 + (place[0] ^ last)
                parts = [total[pl.ds(pl.multiple_of(owner * rows, 8), rows), :]]
                for other in others:
                    lines = other.shape[0] // (2 * classes)
                    at = (last * classes + far) * lines
                    for k in range(other.shape[1] // channels):
                        piece = other[at : at + lines, k * channels : (k + 1) * channels]
                        parts.append(piece.astype(jnp.float32))
                out[far] = jnp.concatenate(parts, axis=0).astype(jnp.bfloat16)


def turn_taps(weight, turned):
    channels = weight.shape[1]
    for i in range(3):
        for j in range(3):
            tap = 3 * (2 - i) + 2 - j
            turned[i, :, j * channels : (j + 1) * channels] = weight[
                tap * channels : (tap + 1) * channels, :
            ]


def input_grad(grad, weight, padded, turned, down):
    _, pixels, channels = grad.shape
    width = side(pixels)

    @pl.when(pl.program_id(0) == 0)
    def _():
        turn_taps(weight, turned)

    clear_edges(padded, width)

    def spread(at, carry):
        fill(padded, at, grad[0, pl.ds(at, CHUNK), :].astype(jnp.float32), width)
        return carry

    chunks(pixels, CHUNK, spread, 0)
    total = mm(padded[0:pixels, :], turned[0], NT)
    for i in (1, 2):
        total += mm(padded[i * width : i * width + pixels, :], turned[i], NT)
    down[...] = total


def slope_of(values):
    sig = jax.nn.sigmoid(values)
    return sig * (1.0 + values * (1.0 - sig))


def second_back_kernel(
    grad, inner, stats, film, gains, member, weight, grad_out, sums_out, padded, turned, down
):
    _, pixels, channels = grad.shape
    input_grad(grad, weight, padded, turned, down)
    mean, inverse = stats[0, 2:3], stats[0, 3:4]
    scale, lift = 1.0 + film[0, 0:1], film[0, 1:2]
    gain, shift = gains[2:3], gains[3:4]

    def slopes(at, carry):
        hat = (inner[0, pl.ds(at, CHUNK), :] - mean) * inverse
        lifted = (hat * gain + shift) * scale + lift
        lifted_grad = down[pl.ds(at, CHUNK), :] * slope_of(lifted)
        down[pl.ds(at, CHUNK), :] = lifted_grad
        return (carry[0] + fold(lifted_grad * hat), carry[1] + fold(lifted_grad))

    zero = jnp.zeros((8, channels), jnp.float32)
    rows = two_rows(*chunks(pixels, CHUNK, slopes, (zero, zero)))
    sums_out[0] = rows
    factor = scale * gain
    means = group_total(rows * factor, member[...]) / (pixels * (channels // GROUPS))

    def back_norm(at, carry):
        hat = (inner[0, pl.ds(at, CHUNK), :] - mean) * inverse
        back = (down[pl.ds(at, CHUNK), :] * factor - means[1:2] - hat * means[0:1]) * inverse
        grad_out[0, pl.ds(at, CHUNK), :] = back.astype(jnp.bfloat16)
        return carry

    chunks(pixels, CHUNK, back_norm, 0)


def first_back_kernel(grad, images, stats, gains, weight, sums_out, padded, turned, down):
    _, pixels, channels = grad.shape
    input_grad(grad, weight, padded, turned, down)
    mean, inverse = stats[0, 0:1], stats[0, 1:2]
    gain, shift = gains[0:1], gains[1:2]

    def slopes(at, carry):
        hat = (images[0, pl.ds(at, CHUNK), :].astype(jnp.float32) - mean) * inverse
        grad_first = down[pl.ds(at, CHUNK), :] * slope_of(hat * gain + shift)
        return (carry[0] + fold(grad_first * hat), carry[1] + fold(grad_first))

    zero = jnp.zeros((8, channels), jnp.float32)
    sums_out[0] = two_rows(*chunks(pixels, CHUNK, slopes, (zero, zero)))


def whole(*shape):
    return pl.BlockSpec(shape, lambda s: (0,) * len(shape))


def each(*shape):
    return pl.BlockSpec((1,) + shape, lambda s: (s,) + (0,) * len(shape))


def per_sample(kernel, samples, in_specs, outs, scratch, flops, *operands):
    return pl.pallas_call(
        kernel,
        grid=(samples,),
        in_specs=in_specs,
        out_specs=[spec for spec, _ in outs],
        out_shape=[shape for _, shape in outs],
        scratch_shapes=scratch,
        compiler_params=pltpu.CompilerParams(vmem_limit_bytes=VMEM_LIMIT),
        cost_estimate=pl.CostEstimate(flops=flops, bytes_accessed=flops // 1000, transcendentals=0),
    )(*operands)


def sized(dtype, *shape):
    return jax.ShapeDtypeStruct(shape, dtype)


def block_calls(samples, pixels, channels):
    width = side(pixels)
    act = each(pixels, channels)
    few = each(8, channels)
    gain_spec, member_spec = whole(8, channels), whole(channels, channels)
    weight_spec = whole(9 * channels, channels)
    bf, f32 = jnp.bfloat16, jnp.float32
    padded = pltpu.VMEM((pixels + 2 * width, 3 * channels), bf)
    turned = pltpu.VMEM((3, channels, 3 * channels), bf)
    down = pltpu.VMEM((pixels, channels), f32)
    act_b = sized(bf, samples, pixels, channels)
    act_f = sized(f32, samples, pixels, channels)
    few_f = sized(f32, samples, 8, channels)
    flops = 18 * samples * pixels * channels * channels

    def first(places, strips, gains, member, weight):
        parts = len(strips)
        return per_sample(
            functools.partial(first_kernel, parts), samples,
            [pl.BlockSpec(memory_space=pltpu.SMEM)] + [each(pixels // parts, channels)] * parts
            + [gain_spec, member_spec, weight_spec],
            [(act, act_f), (act, act_b), (few, few_f), (act, act_b)], [padded], flops,
            places, *strips, gains, member, weight,
        )

    def second(inner, images, stats, film, gains, weight):
        return per_sample(
            second_kernel, samples, [act, act, few, few, gain_spec, weight_spec],
            [(act, act_f), (act, act_b)], [padded], flops,
            inner, images, stats, film, gains, weight,
        )

    def weights(hidden, grad, place, classes, others=()):
        scratch = [padded, pltpu.VMEM((9 * channels, channels), f32)]
        conv_rows = 9 * channels // (2 * classes)
        more = [other.shape[0] * other.shape[1] // (2 * classes * channels) for other in others]
        if conv_rows % 8:
            (whole_grad,) = per_sample(
                weights_kernel, samples, [act, act],
                [(weight_spec, sized(bf, 9 * channels, channels))], scratch, flops, hidden, grad,
            )
            blocks = whole_grad.reshape(2 * classes, conv_rows, channels)
            both = []
            for last in range(2):
                owner = place[0] ^ last
                cut = blocks.reshape(classes, 2, conv_rows, channels)
                parts = [lax.dynamic_index_in_dim(cut, owner, 1, keepdims=False)]
                for other in others:
                    cut = other.reshape(2, classes, -1, other.shape[1] // channels, channels)[last]
                    parts.append(jnp.moveaxis(cut, 2, 1).reshape(classes, -1, channels))
                both.append(jnp.concatenate(parts, axis=1))
            return both
        shape = (classes, conv_rows + sum(more), channels)
        out = (whole(*shape), sized(bf, *shape))
        return per_sample(
            functools.partial(shares_kernel, len(others)), samples,
            [pl.BlockSpec(memory_space=pltpu.SMEM), act, act] + [whole(*o.shape) for o in others],
            [out, out], scratch, flops, place, hidden, grad, *others,
        )

    def second_back(grad, inner, stats, film, gains, member, weight):
        return per_sample(
            second_back_kernel, samples,
            [act, act, few, few, gain_spec, member_spec, weight_spec],
            [(act, act_b), (few, few_f)], [padded, turned, down], flops,
            grad, inner, stats, film, gains, member, weight,
        )

    def first_back(grad, images, stats, gains, weight):
        return per_sample(
            first_back_kernel, samples, [act, act, few, gain_spec, weight_spec],
            [(few, few_f)], [padded, turned, down], flops,
            grad, images, stats, gains, weight,
        )[0]

    return first, second, weights, second_back, first_back


def adamw(master, gradient, first, second, step_rate, decay_rate, clip_factor):
    gradient = gradient * clip_factor
    first_new = BETA_ONE * first + (1.0 - BETA_ONE) * gradient
    second_new = BETA_TWO * second + (1.0 - BETA_TWO) * gradient * gradient
    ratio = (
        first_new
        / (1.0 - BETA_ONE**STEP)
        / (jnp.sqrt(second_new / (1.0 - BETA_TWO**STEP)) + ADAM_EPS)
    )
    return (master - step_rate * (ratio + decay_rate * master), first_new, second_new)


def body(
    images,
    noise,
    timesteps,
    extents,
    film_master,
    conv_master,
    qkv_master,
    out_master,
    gains,
    film_first,
    film_second,
    conv_first,
    conv_second,
    qkv_first,
    qkv_second,
    out_first,
    out_second,
    gain_first,
    gain_second,
):
    devices = lax.axis_size("dp") * lax.axis_size("head")
    device = lax.axis_index("dp") * lax.axis_size("head") + lax.axis_index("head")
    channels = images.shape[-1]
    wide = film_master.shape[1]
    half_width = channels // 2
    conv_rows = conv_master.shape[0]
    film_rows = film_master.shape[0]
    out_rows = out_master.shape[0]

    local_samples = timesteps.shape[0]
    small = jnp.concatenate(
        [
            lax.reduce_precision(gains.reshape(-1), 8, 7),
            extents.astype(jnp.float32).reshape(-1),
            timesteps.astype(jnp.float32),
        ]
    )
    small = jnp.pad(small, (0, -small.shape[0] % 128))
    smalls = to_all(jnp.broadcast_to(small[None, None], (devices, 1, small.shape[0])))
    classes = class_count()
    top_mask = devices // 2
    is_top = device >= top_mask
    ours = conv_master.astype(jnp.bfloat16)
    theirs = exchange(ours, top_mask)
    strips = strips_of(images)
    low, high = jnp.where(is_top, theirs, ours), jnp.where(is_top, ours, theirs)
    smalls = smalls.reshape(devices, -1)
    gain_f = smalls[:, : gains.size].reshape(channels, 6)
    dp_smalls = smalls.reshape(lax.axis_size("dp"), lax.axis_size("head"), -1)[:, 0, gains.size :]
    extents_all = dp_smalls[:, : 2 * local_samples].reshape(-1, 2)
    times_all = dp_smalls[:, 2 * local_samples : 3 * local_samples].reshape(-1).astype(jnp.int32)
    divisor = jnp.sum(extents_all[:, 0] * extents_all[:, 1])

    parts = lax.axis_size("head")
    samples, strip_rows, width_px, _ = strips[0].shape
    places = lax.axis_index("head") ^ jnp.arange(parts, dtype=jnp.int32)
    rows = strip_rows * parts
    pixels = rows * width_px
    first = lax.axis_index("head") * samples
    own_times = lax.dynamic_slice_in_dim(timesteps, first, samples)
    own_extents = lax.dynamic_slice_in_dim(extents, first, samples)

    log_beta, log_tilde, factor = plan(own_times)
    embedded_all = jax.nn.silu(embed(times_all, wide)).astype(jnp.bfloat16)
    film_rows_out = lax.dot_general(
        film_master.astype(jnp.bfloat16),
        embedded_all,
        (((1,), (1,)), ((), ())),
        preferred_element_type=jnp.float32,
    )
    film_blocks = film_rows_out.T.reshape(devices, -1)
    film_blocks = jnp.pad(film_blocks, ((0, 0), (0, -film_blocks.shape[1] % 128)))
    film_blocks = to_all(film_blocks[:, None]).reshape(devices, -1)
    film_blocks = film_blocks[:, : samples * film_rows].reshape(devices, samples, film_rows)
    film_out = jnp.moveaxis(film_blocks, 1, 0).reshape(samples, devices * film_rows)
    every_one = gather_classes(behind(low, film_out, *strips))
    rest = jnp.concatenate([qkv_master.reshape(-1, channels), out_master]).astype(jnp.bfloat16)
    rest = behind(rest, theirs)
    rest_two = pair_up(rest, exchange(rest, top_mask), jnp.logical_not(is_top), 0)
    every_two = gather_classes(
        behind(jnp.concatenate([high, rest_two.reshape(-1, channels)]), every_one)
    )
    gains_t = jnp.pad(gain_f.T, ((0, 2), (0, 0)))
    member = jnp.asarray(np.kron(np.eye(GROUPS), np.ones((channels // GROUPS,) * 2)), jnp.bfloat16)
    scalars = jnp.stack(
        [log_beta, log_tilde, factor, jnp.broadcast_to(divisor, factor.shape)]
        + [own_extents[:, 0].astype(jnp.float32), own_extents[:, 1].astype(jnp.float32)],
        axis=1,
    )
    first_call, second_call, weights, second_back, first_back = block_calls(samples, pixels, channels)
    flat = lambda values: [v.reshape(samples, strip_rows * width_px, -1) for v in values]
    (taps_one,) = finish_gather(every_one, [conv_rows])
    taps_one = taps_one.reshape(-1, channels)
    inner, hidden_one, stats, source = first_call(places, flat(strips), gains_t, member, taps_one)
    taps_two, others = finish_gather(behind(every_two, inner), [conv_rows, 8 * out_rows])
    taps_two = taps_two.reshape(-1, channels)
    others = jnp.moveaxis(others.reshape(-1, 2, 4 * out_rows, channels), 0, 1)
    others = others.reshape(devices, 4 * out_rows, channels)
    qkv_w = others[:, : 3 * out_rows].reshape(channels, 3 * channels)
    out_w = others[:, 3 * out_rows :].reshape(channels, channels)
    noise_strips = strips_of(behind(noise, taps_two))
    film = jnp.pad(film_out.reshape(samples, 2, channels), ((0, 0), (0, 6), (0, 0)))
    scale = 1.0 + film_out[:, :channels]
    middle, hidden_two = second_call(inner, source, stats, film, gains_t, taps_two)
    my_last = last_bit()
    place = my_last.reshape(1).astype(jnp.int32)
    line = jnp.arange(channels, dtype=jnp.int32)
    owner, spot = line // out_rows, line % out_rows
    source_device = (
        (owner % 2) * 2 * classes + (owner // 2 % classes) * 2 + (my_last ^ (owner // (2 * classes)))
    )
    order = (line[None, :] == (source_device * out_rows + spot)[:, None]).astype(jnp.bfloat16)
    grad_two_b, shares, sums_three, losses = attention_block(
        places, scalars, middle, flat(noise_strips), gains_t, member, qkv_w, out_w, order
    )
    loss_local = jnp.sum(losses)
    two_shares = weights(hidden_two, grad_two_b, place, classes, (shares,))
    grad_two_b = behind(grad_two_b, *two_shares)
    grad_one_b, sums_two = second_back(grad_two_b, inner, stats, film, gains_t, member, taps_two)
    two_sent = (two_shares[0].astype(jnp.float32) + exchange(two_shares[1], 1).astype(jnp.float32)).astype(jnp.bfloat16)
    share_two = jnp.sum(across_classes(two_sent).astype(jnp.float32), axis=0)
    one_shares = weights(behind(hidden_one, two_sent), grad_one_b, place, classes)
    one_sent = (one_shares[0].astype(jnp.float32) + exchange(one_shares[1], 1).astype(jnp.float32)).astype(jnp.bfloat16)
    share_one = jnp.sum(across_classes(one_sent).astype(jnp.float32), axis=0)
    grad_one_b = behind(grad_one_b, share_two, one_sent)
    sums_one = first_back(grad_one_b, source, stats, gains_t, taps_one)
    gain_one, bias_one = jnp.sum(sums_one[:, 0], axis=0), jnp.sum(sums_one[:, 1], axis=0)
    gain_two, bias_two = jnp.sum(sums_two[:, 0] * scale, axis=0), jnp.sum(sums_two[:, 1] * scale, axis=0)
    gain_three, bias_three = jnp.sum(sums_three[:, 0], axis=0), jnp.sum(sums_three[:, 1], axis=0)
    grad_scale = sums_two[:, 0] * gains_t[2] + sums_two[:, 1] * gains_t[3]
    film_grad_b = jnp.concatenate([grad_scale, sums_two[:, 1]], axis=1).astype(jnp.bfloat16)

    small_shares = share_two[conv_rows:].reshape(4, 2, out_rows, channels)
    keep_two = jnp.where(is_top, small_shares[:, 1], small_shares[:, 0])
    send_two = jnp.where(is_top, small_shares[:, 0], small_shares[:, 1])
    send_two = jnp.concatenate([share_two[:conv_rows], send_two.reshape(-1, channels)])
    got_two = exchange(send_two.astype(jnp.bfloat16), top_mask).astype(jnp.float32)
    got_one = exchange(share_one.astype(jnp.bfloat16), top_mask).astype(jnp.float32)
    conv_g = jnp.where(is_top, share_two[:conv_rows] + got_two[:conv_rows], share_one + got_one)
    small_g = keep_two + got_two[conv_rows:].reshape(keep_two.shape)
    qkv_g = jnp.concatenate([small_g[0], small_g[1], small_g[2]], axis=1)
    out_g = small_g[3]

    gain_grad = jnp.stack([gain_one, bias_one, gain_two, bias_two, gain_three, bias_three], axis=1)
    common = jnp.concatenate([film_grad_b.astype(jnp.float32).reshape(-1), loss_local[None]])
    parcel = jnp.concatenate(
        [
            behind(gain_grad, share_one).reshape(devices, -1),
            jnp.broadcast_to(common[None], (devices, common.shape[0])),
        ],
        axis=1,
    )
    length = parcel.shape[1]
    parcel = jnp.pad(parcel, ((0, 0), (0, -length % 1024))).reshape(devices, -1, 128)
    parcels = to_all(parcel).reshape(devices, -1)
    gain_g = jnp.sum(parcels[:, : gains.size], axis=0).reshape(gains.shape)
    film_all = parcels[:, gains.size : length - 1].reshape(-1, film_grad_b.shape[1])
    loss_total = jnp.sum(parcels[:, length - 1])
    film_own = lax.dynamic_slice_in_dim(film_all, device * film_rows, film_rows, axis=1)
    film_g = jnp.einsum(
        "sf,se->fe", film_own.astype(jnp.bfloat16), embedded_all, preferred_element_type=jnp.float32
    )
    reduced = (film_g, conv_g, qkv_g, out_g, gain_g)
    squares = jnp.zeros((), jnp.float32)
    for gradient in reduced:
        squares = squares + jnp.sum(gradient * gradient)
    grad_norm = jnp.sqrt(jnp.sum(to_all(jnp.broadcast_to(squares, (devices, 8, 128)))[:, 0, 0]))
    clip_factor = jnp.minimum(1.0, THRESHOLD / (grad_norm + 1e-06))
    film_res = adamw(film_master, film_g, film_first, film_second, RATE_MATRIX, DECAY, clip_factor)
    conv_res = adamw(conv_master, conv_g, conv_first, conv_second, RATE_MATRIX, DECAY, clip_factor)
    qkv_res = adamw(qkv_master, qkv_g, qkv_first, qkv_second, RATE_MATRIX, DECAY, clip_factor)
    out_res = adamw(out_master, out_g, out_first, out_second, RATE_MATRIX, DECAY, clip_factor)
    gain_res = adamw(gains, gain_g, gain_first, gain_second, RATE_GAIN, 0.0, clip_factor)
    loss_parts = jnp.stack([loss_total, divisor])
    return (
        loss_parts,
        grad_norm,
        film_res[0],
        film_res[1],
        film_res[2],
        conv_res[0],
        conv_res[1],
        conv_res[2],
        qkv_res[0],
        qkv_res[1],
        qkv_res[2],
        out_res[0],
        out_res[1],
        out_res[2],
        gain_res[0],
        gain_res[1],
        gain_res[2],
    )


def solution(mesh):
    in_specs = (
        P("dp", "head", None, None),
        P("dp", "head", None, None),
        P("dp"),
        P("dp", None),
        P(("dp", "head"), None),
        P(("dp", "head"), None),
        P(("dp", "head"), None),
        P(("dp", "head"), None),
        P(("dp", "head"), None),
        P(("dp", "head"), None),
        P(("dp", "head"), None),
        P(("dp", "head"), None),
        P(("dp", "head"), None),
        P(("dp", "head"), None),
        P(("dp", "head"), None),
        P(("dp", "head"), None),
        P(("dp", "head"), None),
        P(("dp", "head"), None),
        P(("dp", "head"), None),
    )
    out_specs = (
        P(),
        P(),
        P(("dp", "head"), None),
        P(("dp", "head"), None),
        P(("dp", "head"), None),
        P(("dp", "head"), None),
        P(("dp", "head"), None),
        P(("dp", "head"), None),
        P(("dp", "head"), None),
        P(("dp", "head"), None),
        P(("dp", "head"), None),
        P(("dp", "head"), None),
        P(("dp", "head"), None),
        P(("dp", "head"), None),
        P(("dp", "head"), None),
        P(("dp", "head"), None),
        P(("dp", "head"), None),
    )
    return jax.shard_map(body, mesh=mesh, in_specs=in_specs, out_specs=out_specs, check_vma=False)
```

```python
import functools
import math

import jax
import jax.numpy as jnp
import numpy as np
from jax import lax
from jax.experimental import pallas as pl
from jax.experimental.pallas import tpu as pltpu
from jax.sharding import PartitionSpec as P

HEADS = 4
GROUPS = 32
STEP = 10
TSTEPS = 4000


EPS_NORM = 1e-05
VLB_WEIGHT = 0.001
BETA_ONE = 0.9
BETA_TWO = 0.999
ADAM_EPS = 1e-08
DECAY = 0.01
RATE_MATRIX = 0.05
RATE_GAIN = 0.4
THRESHOLD = 0.002
OFFSET = 0.008
LOG2E = math.log2(math.e)
VMEM_LIMIT = 56 << 20


def plan(step_ids):
    moment = step_ids.astype(jnp.float32)

    def angle(values):
        return (values / TSTEPS + OFFSET) / (1.0 + OFFSET) * (0.5 * math.pi)

    start = angle(jnp.zeros_like(moment))
    before = angle(moment - 1.0)
    later_angle = angle(moment)
    beta_now = jnp.sin(later_angle - before) * jnp.sin(later_angle + before) / jnp.cos(before) ** 2
    fade_now = jnp.sin(later_angle - start) * jnp.sin(later_angle + start) / jnp.cos(start) ** 2
    fade_prev = jnp.sin(before - start) * jnp.sin(before + start) / jnp.cos(start) ** 2
    log_beta = jnp.log(beta_now)
    log_tilde = jnp.log(beta_now * fade_prev / fade_now)
    factor = beta_now * beta_now / ((1.0 - beta_now) * fade_now)
    return (log_beta, log_tilde, factor)


def embed(step_ids, width):
    half_width = width // 2
    frequency = jnp.exp(-math.log(10000.0) * jnp.arange(half_width, dtype=jnp.float32) / half_width)
    phases = step_ids.astype(jnp.float32)[:, None] * frequency[None, :]
    return jnp.concatenate([jnp.cos(phases), jnp.sin(phases)], axis=1)


def behind(values, *others):
    return lax.optimization_barrier((values,) + others)[0]


def pair_up(block, other, low, place):
    shape = [2 if dim == place else 1 for dim in range(block.ndim + 1)]
    first = jnp.arange(2, dtype=jnp.int32).reshape(shape) == 0
    return jnp.where(first == low, jnp.expand_dims(block, place), jnp.expand_dims(other, place))


def class_count():
    return lax.axis_size("dp") * lax.axis_size("head") // 4


def last_bit():
    return lax.axis_index("head") % 2


def exchange(values, mask):
    size = lax.axis_size("dp") * lax.axis_size("head")
    return lax.ppermute(values, ("dp", "head"), [(i, i ^ mask) for i in range(size)])


def across_classes(blocks):
    count = class_count()
    groups = [
        [(high * count + k) * 2 + last for k in range(count)] for high in range(2) for last in range(2)
    ]
    return lax.all_to_all(
        blocks, ("dp", "head"), split_axis=0, concat_axis=0, axis_index_groups=groups, tiled=True
    )


def gather_classes(block):
    return across_classes(jnp.broadcast_to(block[None], (class_count(),) + block.shape))


def conv_pieces(both, other, rows):
    if rows % 8 == 0:
        return [both, other]
    joined = pair_up(both[:, :rows], other[:, :rows], last_bit() == 0, 1)
    return [joined.reshape(-1, both.shape[-1])]


def to_all(blocks):
    return lax.all_to_all(blocks, ("dp", "head"), split_axis=0, concat_axis=0, tiled=True)


def strips_of(values):
    parts = lax.axis_size("head")
    count = values.shape[0] // parts
    mine = lax.axis_index("head")
    strips = []
    for far in range(parts):
        strip = lax.dynamic_slice_in_dim(values, (mine ^ far) * count, count, axis=0)
        if far:
            strip = lax.ppermute(strip, "head", [(i, i ^ far) for i in range(parts)])
        strips.append(strip)
    return strips


NN = (((1,), (0,)), ((), ()))
NT = (((1,), (1,)), ((), ()))
TN = (((0,), (0,)), ((), ()))


def mm(left, right, form=NN):
    return lax.dot_general(left, right, form, preferred_element_type=jnp.float32)


def group_total(rows, member):
    high = rows.astype(jnp.bfloat16).astype(jnp.float32)
    rest = rows - high
    mid = rest.astype(jnp.bfloat16).astype(jnp.float32)
    parts = jnp.concatenate([high, mid, rest - mid, jnp.zeros_like(rows)], axis=0)
    sums = mm(parts.astype(jnp.bfloat16), member)
    return sums[0:8] + sums[8:16] + sums[16:24]


def fold(values):
    rows, width = values.shape
    return jnp.sum(values.reshape(rows // 8, 8, width), axis=0)


def two_rows(first, second):
    first = jnp.sum(first, axis=0, keepdims=True)
    second = jnp.sum(second, axis=0, keepdims=True)
    row = lax.broadcasted_iota(jnp.int32, (8, first.shape[1]), 0)
    return jnp.where(row == 0, first, jnp.where(row == 1, second, 0.0))


def chunks(total, size, step, init):
    return lax.fori_loop(0, total // size, lambda m, c: step(pl.multiple_of(m * size, size), c), init)


def norm_sums(load, pixels, channels, member, size):
    def step(at, carry):
        values = load(at)
        return (carry[0] + fold(values), carry[1] + fold(values * values))

    zero = jnp.zeros((8, channels), jnp.float32)
    first, second = chunks(pixels, size, step, (zero, zero))
    count = pixels * (channels // GROUPS)
    sums = group_total(two_rows(first, second), member) / count
    mean = sums[0:1]
    inverse = lax.rsqrt(sums[1:2] - mean * mean + EPS_NORM)
    return mean, inverse


CHUNK = 1024
PART = 256


def attention_kernel(parts, places, scalars, middle, *refs):
    attention_body(places, scalars, middle, refs[:parts], *refs[parts:])


def attention_body(
    places,
    scalars,
    middle,
    strips,
    gains,
    member,
    qkv_w,
    out_w,
    order,
    down_out,
    shares,
    sums_out,
    loss_out,
    noise,
    qkv_wt,
    normed,
    qkv_t,
    probs,
    totals,
    mixed_t,
    attn_t,
    result,
    grad_b,
    back_t,
    dqkv_t,
    gn_t,
    qkv_acc,
    out_acc,
):
    sample = pl.program_id(0)
    _, pixels, channels = middle.shape
    half = channels // 2
    size = channels // HEADS
    factor = size ** (-0.5)
    width = int(round(pixels**0.5))

    @pl.when(sample == 0)
    def _():
        qkv_wt[...] = qkv_w[...].T
        qkv_acc[...] = jnp.zeros_like(qkv_acc)
        out_acc[...] = jnp.zeros_like(out_acc)

    join_strips(places, strips, noise)
    load = lambda at: middle[0, pl.ds(at, PART), :]
    mean, inverse = norm_sums(load, pixels, channels, member[...], PART)
    gain, shift = gains[4:5], gains[5:6]

    def normalize(at, carry):
        hat = (load(at) - mean) * inverse
        normed[pl.ds(at, PART), :] = (hat * gain + shift).astype(jnp.bfloat16)
        return carry

    chunks(pixels, PART, normalize, 0)

    block = 256

    qkv_t[...] = mm(qkv_wt[...], normed[...], NT).astype(jnp.bfloat16)

    def rows_of_head(head, part):
        at = (3 * head + part) * size
        return slice(at, at + size)

    def scores_of(head):
        return mm(qkv_t[rows_of_head(head, 1), :].T, qkv_t[rows_of_head(head, 0), :])

    following = scores_of(0)
    for head in range(HEADS):
        scores = following
        if head + 1 < HEADS:
            following = scores_of(head + 1)
        top = jnp.max(scores, axis=0, keepdims=True)
        powers = jnp.exp2((scores - top) * (factor * LOG2E))
        inv = 1.0 / jnp.sum(powers, axis=0, keepdims=True)
        powers_b = powers.astype(jnp.bfloat16)
        probs[head] = powers_b
        totals[head] = jnp.broadcast_to(inv, (8, pixels))
        mixed = mm(qkv_t[rows_of_head(head, 2), :], powers_b) * inv
        at = slice(head * size, (head + 1) * size)
        mixed_t[at, :] = mixed
        attn_t[at, :] = mixed.astype(jnp.bfloat16)

    result[...] = mm(attn_t[...].T, out_w[...])
    beta_log, tilde_log, coef = scalars[sample, 0], scalars[sample, 1], scalars[sample, 2]
    divisor, high, wide = scalars[sample, 3], scalars[sample, 4], scalars[sample, 5]

    def losses(at, carry):
        total = load(at) + result[pl.ds(at, PART), :]
        pixel = at + lax.broadcasted_iota(jnp.int32, (PART, half), 0)
        row = (pixel // width).astype(jnp.float32)
        col = (pixel % width).astype(jnp.float32)
        valid = jnp.where((row >= width - high) & (col < wide), 1.0, 0.0)
        residue = total[:, :half] - noise[pl.ds(at, PART), :].astype(jnp.float32)
        weight = jax.nn.sigmoid(total[:, half:])
        blended = weight * beta_log + (1.0 - weight) * tilde_log
        spread = jnp.exp(tilde_log - blended)
        damped = coef * residue * residue * jnp.exp(-blended)
        diverge = 0.5 * (-1.0 + blended - tilde_log + spread + damped)
        pixel_loss = valid * (residue * residue + VLB_WEIGHT * diverge)
        scale = valid / (half * divisor)
        grad_guess = 2.0 * residue * scale
        grad_raw = (
            scale * (0.5 * VLB_WEIGHT) * (1.0 - spread - damped)
            * (beta_log - tilde_log) * weight * (1.0 - weight)
        )
        grad = jnp.concatenate([grad_guess, grad_raw], axis=-1)
        result[pl.ds(at, PART), :] = grad
        grad_b[pl.ds(at, PART), :] = grad.astype(jnp.bfloat16)
        return carry + fold(pixel_loss)

    loss = chunks(pixels, PART, losses, jnp.zeros((8, half), jnp.float32))
    loss_out[0] = loss * (1.0 / half)

    out_acc[...] += mm(attn_t[...], grad_b[...])
    back_t[...] = mm(out_w[...], grad_b[...], NT).astype(jnp.bfloat16)

    def upstream_of(head):
        return back_t[head * size : (head + 1) * size, :]

    def soft_grad(head):
        return mm(qkv_t[rows_of_head(head, 2), :].T, upstream_of(head))

    following = soft_grad(0)
    for head in range(HEADS):
        grad_soft = following
        if head + 1 < HEADS:
            following = soft_grad(head + 1)
        upstream = upstream_of(head)
        inner = jnp.sum(
            upstream.astype(jnp.float32) * mixed_t[head * size : (head + 1) * size, :],
            axis=0,
            keepdims=True,
        )
        soft = probs[head].astype(jnp.float32) * totals[head, 0:1]
        grad_scores = (soft * (grad_soft - inner)).astype(jnp.bfloat16)
        queries_t, keys_t = qkv_t[rows_of_head(head, 0), :], qkv_t[rows_of_head(head, 1), :]
        dqkv_t[rows_of_head(head, 0), :] = (mm(keys_t, grad_scores) * factor).astype(jnp.bfloat16)
        dqkv_t[rows_of_head(head, 1), :] = (mm(queries_t, grad_scores, NT) * factor).astype(jnp.bfloat16)
        dqkv_t[rows_of_head(head, 2), :] = mm(upstream, soft.astype(jnp.bfloat16), NT).astype(jnp.bfloat16)

    qkv_acc[...] += mm(normed[...].T, dqkv_t[...], NT)
    gn_t[...] = mm(qkv_w[...], dqkv_t[...]).T

    def back_sums(at, carry):
        hat = (load(at) - mean) * inverse
        grad = gn_t[pl.ds(at, PART), :]
        return (carry[0] + fold(grad * hat), carry[1] + fold(grad))

    zero = jnp.zeros((8, channels), jnp.float32)
    both = chunks(pixels, PART, back_sums, (zero, zero))
    rows = two_rows(*both)
    sums_out[0] = rows
    means = group_total(rows * gain, member[...]) / (pixels * (channels // GROUPS))

    def back_norm(at, carry):
        hat = (load(at) - mean) * inverse
        grad = gn_t[pl.ds(at, PART), :] * gain
        back = (grad - means[1:2] - hat * means[0:1]) * inverse
        down_out[0, pl.ds(at, PART), :] = (result[pl.ds(at, PART), :] + back).astype(jnp.bfloat16)
        return carry

    chunks(pixels, PART, back_norm, 0)

    @pl.when(sample == pl.num_programs(0) - 1)
    def _():
        wide = 3 * channels
        shares[:, 0:wide] = mm(order[...], qkv_acc[...].astype(jnp.bfloat16)).astype(jnp.bfloat16)
        shares[:, wide:] = mm(order[...], out_acc[...].astype(jnp.bfloat16)).astype(jnp.bfloat16)


def attention_block(places, scalars, middle, strips, gains, member, qkv_w, out_w, order):
    parts = len(strips)
    samples, pixels, channels = middle.shape
    half = channels // 2
    bf, f32 = jnp.bfloat16, jnp.float32
    return pl.pallas_call(
        functools.partial(attention_kernel, parts),
        grid=(samples,),
        in_specs=[
            pl.BlockSpec(memory_space=pltpu.SMEM),
            pl.BlockSpec(memory_space=pltpu.SMEM),
            each(pixels, channels),
            *[each(pixels // parts, half)] * parts,
            whole(8, channels),
            whole(channels, channels),
            whole(channels, 3 * channels),
            whole(channels, channels),
            whole(channels, channels),
        ],
        out_specs=[
            each(pixels, channels),
            whole(channels, 4 * channels),
            each(8, channels),
            each(8, half),
        ],
        out_shape=[
            jax.ShapeDtypeStruct((samples, pixels, channels), bf),
            jax.ShapeDtypeStruct((channels, 4 * channels), bf),
            jax.ShapeDtypeStruct((samples, 8, channels), f32),
            jax.ShapeDtypeStruct((samples, 8, half), f32),
        ],
        scratch_shapes=[
            pltpu.VMEM((pixels, half), bf),
            pltpu.VMEM((3 * channels, channels), bf),
            pltpu.VMEM((pixels, channels), bf),
            pltpu.VMEM((3 * channels, pixels), bf),
            pltpu.VMEM((HEADS, pixels, pixels), bf),
            pltpu.VMEM((HEADS, 8, pixels), f32),
            pltpu.VMEM((channels, pixels), f32),
            pltpu.VMEM((channels, pixels), bf),
            pltpu.VMEM((pixels, channels), f32),
            pltpu.VMEM((pixels, channels), bf),
            pltpu.VMEM((channels, pixels), bf),
            pltpu.VMEM((3 * channels, pixels), bf),
            pltpu.VMEM((pixels, channels), f32),
            pltpu.VMEM((channels, 3 * channels), f32),
            pltpu.VMEM((channels, channels), f32),
        ],
        compiler_params=pltpu.CompilerParams(vmem_limit_bytes=VMEM_LIMIT),
        cost_estimate=pl.CostEstimate(
            flops=30 * samples * pixels * pixels * channels,
            bytes_accessed=8 * samples * pixels * channels,
            transcendentals=samples * HEADS * pixels * pixels,
        ),
    )(places, scalars, middle, *strips, gains, member, qkv_w, out_w, order)


def fill(padded, at, values, width):
    rows, channels = values.shape
    col = lax.broadcasted_iota(jnp.int32, values.shape, 0) % width
    there = pl.ds(at + width, rows)
    left = jnp.where(col == 0, 0.0, pltpu.roll(values, 1, 0))
    right = jnp.where(col == width - 1, 0.0, pltpu.roll(values, rows - 1, 0))
    padded[there, 0:channels] = left.astype(jnp.bfloat16)
    padded[there, channels : 2 * channels] = values.astype(jnp.bfloat16)
    padded[there, 2 * channels :] = right.astype(jnp.bfloat16)


def clear_edges(padded, width):
    rows, wide = padded.shape
    padded[0:width, :] = jnp.zeros((width, wide), jnp.bfloat16)
    padded[rows - width :, :] = jnp.zeros((width, wide), jnp.bfloat16)


def side(pixels):
    return int(round(pixels**0.5))


def taps_product(padded, weight, pixels, width):
    wide = padded.shape[1]
    total = mm(padded[0:pixels, :], weight(0))
    for i in (1, 2):
        total += mm(padded[i * width : i * width + pixels, :], weight(i))
    return total


def rows_of(*rows):
    index = lax.broadcasted_iota(jnp.int32, (8, rows[0].shape[1]), 0)
    total = jnp.zeros(index.shape, jnp.float32)
    for place, row in enumerate(rows):
        total = jnp.where(index == place, row, total)
    return total


def join_strips(places, strips, joined):
    rows = strips[0].shape[1]
    for far, strip in enumerate(strips):
        joined[pl.ds(pl.multiple_of(places[far] * rows, rows), rows), :] = strip[0]


def join_weights(last, pieces, weight):
    if len(pieces) == 1:
        weight[...] = pieces[0][...]
        return
    rows = weight.shape[0] // (2 * pieces[0].shape[0])
    for low in range(2):

        @pl.when(last[0] == low)
        def _():
            for k in range(pieces[0].shape[0]):
                both = [pieces[low ^ half][k, 0:rows, :].astype(jnp.float32) for half in range(2)]
                pair = jnp.concatenate(both, axis=0).astype(jnp.bfloat16)
                weight[2 * rows * k : 2 * rows * (k + 1), :] = pair


def first_kernel(parts, count, places, last, *refs):
    strips, pieces, refs = refs[:parts], refs[parts : parts + count], refs[parts + count :]
    gains, member, inner, hidden, stats, images, weight, padded = refs
    _, pixels, channels = images.shape

    @pl.when(pl.program_id(0) == 0)
    def _():
        join_weights(last, pieces, weight)

    join_strips(places, strips, images.at[0])
    width = side(pixels)
    wide = 3 * channels
    load = lambda at: images[0, pl.ds(at, CHUNK), :].astype(jnp.float32)
    mean, inverse = norm_sums(load, pixels, channels, member[...], CHUNK)
    gain, shift = gains[0:1], gains[1:2]
    clear_edges(padded, width)

    def activate(at, carry):
        out = (load(at) - mean) * inverse * gain + shift
        value = out * jax.nn.sigmoid(out)
        hidden[0, pl.ds(at, CHUNK), :] = value.astype(jnp.bfloat16)
        fill(padded, at, value, width)
        return carry

    chunks(pixels, CHUNK, activate, 0)
    inner[0] = taps_product(padded, lambda i: weight[i * wide : (i + 1) * wide, :], pixels, width)
    mean_two, inverse_two = norm_sums(
        lambda at: inner[0, pl.ds(at, CHUNK), :], pixels, channels, member[...], CHUNK
    )
    stats[0] = rows_of(mean, inverse, mean_two, inverse_two)


def second_kernel(count, last, *refs):
    pieces, refs = refs[:count], refs[count:]
    inner, images, stats, film, gains, middle, hidden, weight, padded = refs
    _, pixels, channels = inner.shape

    @pl.when(pl.program_id(0) == 0)
    def _():
        join_weights(last, pieces, weight)

    width = side(pixels)
    wide = 3 * channels
    mean, inverse = stats[0, 2:3], stats[0, 3:4]
    scale, lift = 1.0 + film[0, 0:1], film[0, 1:2]
    gain, shift = gains[2:3], gains[3:4]
    clear_edges(padded, width)

    def activate(at, carry):
        out = (inner[0, pl.ds(at, CHUNK), :] - mean) * inverse * gain + shift
        lifted = out * scale + lift
        value = lifted * jax.nn.sigmoid(lifted)
        hidden[0, pl.ds(at, CHUNK), :] = value.astype(jnp.bfloat16)
        fill(padded, at, value, width)
        return carry

    chunks(pixels, CHUNK, activate, 0)
    middle[0] = images[0].astype(jnp.float32) + taps_product(
        padded, lambda i: weight[i * wide : (i + 1) * wide, :], pixels, width
    )


def weights_sums(hidden, grad, padded, total):
    _, pixels, channels = hidden.shape
    width = side(pixels)
    wide = 3 * channels
    clear_edges(padded, width)

    def spread(at, carry):
        fill(padded, at, hidden[0, pl.ds(at, CHUNK), :].astype(jnp.float32), width)
        return carry

    chunks(pixels, CHUNK, spread, 0)

    @pl.when(pl.program_id(0) == 0)
    def _():
        total[...] = jnp.zeros_like(total)

    for i in range(3):
        total[i * wide : (i + 1) * wide, :] += mm(
            padded[i * width : i * width + pixels, :], grad[0], TN
        )


def weights_kernel(hidden, grad, out, padded, total):
    weights_sums(hidden, grad, padded, total)

    @pl.when(pl.program_id(0) == pl.num_programs(0) - 1)
    def _():
        out[...] = total[...].astype(jnp.bfloat16)


def shares_kernel(extra, place, hidden, grad, *refs):
    others, (mine, theirs, padded, total) = refs[:extra], refs[extra:]
    weights_sums(hidden, grad, padded, total)
    classes = mine.shape[0]
    channels = total.shape[1]
    rows = total.shape[0] // (2 * classes)

    @pl.when(pl.program_id(0) == pl.num_programs(0) - 1)
    def _():
        for far in range(classes):
            for last, out in enumerate((mine, theirs)):
                owner = far * 2 + (place[0] ^ last)
                parts = [total[pl.ds(pl.multiple_of(owner * rows, 8), rows), :]]
                for other in others:
                    lines = other.shape[0] // (2 * classes)
                    at = (last * classes + far) * lines
                    for k in range(other.shape[1] // channels):
                        piece = other[at : at + lines, k * channels : (k + 1) * channels]
                        parts.append(piece.astype(jnp.float32))
                out[far] = jnp.concatenate(parts, axis=0).astype(jnp.bfloat16)


def turn_taps(weight, turned):
    channels = weight.shape[1]
    for i in range(3):
        for j in range(3):
            tap = 3 * (2 - i) + 2 - j
            turned[i, :, j * channels : (j + 1) * channels] = weight[
                tap * channels : (tap + 1) * channels, :
            ]


def input_grad(grad, weight, padded, turned, down):
    _, pixels, channels = grad.shape
    width = side(pixels)

    @pl.when(pl.program_id(0) == 0)
    def _():
        turn_taps(weight, turned)

    clear_edges(padded, width)

    def spread(at, carry):
        fill(padded, at, grad[0, pl.ds(at, CHUNK), :].astype(jnp.float32), width)
        return carry

    chunks(pixels, CHUNK, spread, 0)
    total = mm(padded[0:pixels, :], turned[0], NT)
    for i in (1, 2):
        total += mm(padded[i * width : i * width + pixels, :], turned[i], NT)
    down[...] = total


def slope_of(values):
    sig = jax.nn.sigmoid(values)
    return sig * (1.0 + values * (1.0 - sig))


def second_back_kernel(
    grad, inner, stats, film, gains, member, weight, grad_out, sums_out, padded, turned, down
):
    _, pixels, channels = grad.shape
    input_grad(grad, weight, padded, turned, down)
    mean, inverse = stats[0, 2:3], stats[0, 3:4]
    scale, lift = 1.0 + film[0, 0:1], film[0, 1:2]
    gain, shift = gains[2:3], gains[3:4]

    def slopes(at, carry):
        hat = (inner[0, pl.ds(at, CHUNK), :] - mean) * inverse
        lifted = (hat * gain + shift) * scale + lift
        lifted_grad = down[pl.ds(at, CHUNK), :] * slope_of(lifted)
        down[pl.ds(at, CHUNK), :] = lifted_grad
        return (carry[0] + fold(lifted_grad * hat), carry[1] + fold(lifted_grad))

    zero = jnp.zeros((8, channels), jnp.float32)
    rows = two_rows(*chunks(pixels, CHUNK, slopes, (zero, zero)))
    sums_out[0] = rows
    factor = scale * gain
    means = group_total(rows * factor, member[...]) / (pixels * (channels // GROUPS))

    def back_norm(at, carry):
        hat = (inner[0, pl.ds(at, CHUNK), :] - mean) * inverse
        back = (down[pl.ds(at, CHUNK), :] * factor - means[1:2] - hat * means[0:1]) * inverse
        grad_out[0, pl.ds(at, CHUNK), :] = back.astype(jnp.bfloat16)
        return carry

    chunks(pixels, CHUNK, back_norm, 0)


def first_back_kernel(grad, images, stats, gains, weight, sums_out, padded, turned, down):
    _, pixels, channels = grad.shape
    input_grad(grad, weight, padded, turned, down)
    mean, inverse = stats[0, 0:1], stats[0, 1:2]
    gain, shift = gains[0:1], gains[1:2]

    def slopes(at, carry):
        hat = (images[0, pl.ds(at, CHUNK), :].astype(jnp.float32) - mean) * inverse
        grad_first = down[pl.ds(at, CHUNK), :] * slope_of(hat * gain + shift)
        return (carry[0] + fold(grad_first * hat), carry[1] + fold(grad_first))

    zero = jnp.zeros((8, channels), jnp.float32)
    sums_out[0] = two_rows(*chunks(pixels, CHUNK, slopes, (zero, zero)))


def whole(*shape):
    return pl.BlockSpec(shape, lambda s: (0,) * len(shape))


def each(*shape):
    return pl.BlockSpec((1,) + shape, lambda s: (s,) + (0,) * len(shape))


def per_sample(kernel, samples, in_specs, outs, scratch, flops, *operands):
    return pl.pallas_call(
        kernel,
        grid=(samples,),
        in_specs=in_specs,
        out_specs=[spec for spec, _ in outs],
        out_shape=[shape for _, shape in outs],
        scratch_shapes=scratch,
        compiler_params=pltpu.CompilerParams(vmem_limit_bytes=VMEM_LIMIT),
        cost_estimate=pl.CostEstimate(flops=flops, bytes_accessed=flops // 1000, transcendentals=0),
    )(*operands)


def sized(dtype, *shape):
    return jax.ShapeDtypeStruct(shape, dtype)


def block_calls(samples, pixels, channels):
    width = side(pixels)
    act = each(pixels, channels)
    few = each(8, channels)
    gain_spec, member_spec = whole(8, channels), whole(channels, channels)
    weight_spec = whole(9 * channels, channels)
    bf, f32 = jnp.bfloat16, jnp.float32
    padded = pltpu.VMEM((pixels + 2 * width, 3 * channels), bf)
    turned = pltpu.VMEM((3, channels, 3 * channels), bf)
    down = pltpu.VMEM((pixels, channels), f32)
    act_b = sized(bf, samples, pixels, channels)
    act_f = sized(f32, samples, pixels, channels)
    few_f = sized(f32, samples, 8, channels)
    flops = 18 * samples * pixels * channels * channels

    weight_out = (weight_spec, sized(bf, 9 * channels, channels))
    smem = pl.BlockSpec(memory_space=pltpu.SMEM)

    def first(places, last, strips, pieces, gains, member):
        parts, count = len(strips), len(pieces)
        return per_sample(
            functools.partial(first_kernel, parts, count), samples,
            [smem, smem] + [each(pixels // parts, channels)] * parts
            + [whole(*piece.shape) for piece in pieces] + [gain_spec, member_spec],
            [(act, act_f), (act, act_b), (few, few_f), (act, act_b), weight_out], [padded], flops,
            places, last, *strips, *pieces, gains, member,
        )

    def second(last, pieces, inner, images, stats, film, gains):
        return per_sample(
            functools.partial(second_kernel, len(pieces)), samples,
            [smem] + [whole(*piece.shape) for piece in pieces] + [act, act, few, few, gain_spec],
            [(act, act_f), (act, act_b), weight_out], [padded], flops,
            last, *pieces, inner, images, stats, film, gains,
        )

    def weights(hidden, grad, place, classes, others=()):
        scratch = [padded, pltpu.VMEM((9 * channels, channels), f32)]
        conv_rows = 9 * channels // (2 * classes)
        more = [other.shape[0] * other.shape[1] // (2 * classes * channels) for other in others]
        if conv_rows % 8:
            (whole_grad,) = per_sample(
                weights_kernel, samples, [act, act],
                [(weight_spec, sized(bf, 9 * channels, channels))], scratch, flops, hidden, grad,
            )
            blocks = whole_grad.reshape(2 * classes, conv_rows, channels)
            both = []
            for last in range(2):
                owner = place[0] ^ last
                cut = blocks.reshape(classes, 2, conv_rows, channels)
                parts = [lax.dynamic_index_in_dim(cut, owner, 1, keepdims=False)]
                for other in others:
                    cut = other.reshape(2, classes, -1, other.shape[1] // channels, channels)[last]
                    parts.append(jnp.moveaxis(cut, 2, 1).reshape(classes, -1, channels))
                both.append(jnp.concatenate(parts, axis=1))
            return both
        shape = (classes, conv_rows + sum(more), channels)
        out = (whole(*shape), sized(bf, *shape))
        return per_sample(
            functools.partial(shares_kernel, len(others)), samples,
            [pl.BlockSpec(memory_space=pltpu.SMEM), act, act] + [whole(*o.shape) for o in others],
            [out, out], scratch, flops, place, hidden, grad, *others,
        )

    def second_back(grad, inner, stats, film, gains, member, weight):
        return per_sample(
            second_back_kernel, samples,
            [act, act, few, few, gain_spec, member_spec, weight_spec],
            [(act, act_b), (few, few_f)], [padded, turned, down], flops,
            grad, inner, stats, film, gains, member, weight,
        )

    def first_back(grad, images, stats, gains, weight):
        return per_sample(
            first_back_kernel, samples, [act, act, few, gain_spec, weight_spec],
            [(few, few_f)], [padded, turned, down], flops,
            grad, images, stats, gains, weight,
        )[0]

    return first, second, weights, second_back, first_back


def adamw(master, gradient, first, second, step_rate, decay_rate, clip_factor):
    gradient = gradient * clip_factor
    first_new = BETA_ONE * first + (1.0 - BETA_ONE) * gradient
    second_new = BETA_TWO * second + (1.0 - BETA_TWO) * gradient * gradient
    ratio = (
        first_new
        / (1.0 - BETA_ONE**STEP)
        / (jnp.sqrt(second_new / (1.0 - BETA_TWO**STEP)) + ADAM_EPS)
    )
    return (master - step_rate * (ratio + decay_rate * master), first_new, second_new)


def body(
    images,
    noise,
    timesteps,
    extents,
    film_master,
    conv_master,
    qkv_master,
    out_master,
    gains,
    film_first,
    film_second,
    conv_first,
    conv_second,
    qkv_first,
    qkv_second,
    out_first,
    out_second,
    gain_first,
    gain_second,
):
    devices = lax.axis_size("dp") * lax.axis_size("head")
    device = lax.axis_index("dp") * lax.axis_size("head") + lax.axis_index("head")
    channels = images.shape[-1]
    wide = film_master.shape[1]
    half_width = channels // 2
    conv_rows = conv_master.shape[0]
    film_rows = film_master.shape[0]
    out_rows = out_master.shape[0]

    local_samples = timesteps.shape[0]
    small = jnp.concatenate(
        [
            lax.reduce_precision(gains.reshape(-1), 8, 7),
            extents.astype(jnp.float32).reshape(-1),
            timesteps.astype(jnp.float32),
        ]
    )
    small = jnp.pad(small, (0, -small.shape[0] % 128))
    smalls = to_all(jnp.broadcast_to(small[None, None], (devices, 1, small.shape[0])))
    classes = class_count()
    top_mask = devices // 2
    is_top = device >= top_mask
    ours = conv_master.astype(jnp.bfloat16)
    theirs = exchange(ours, top_mask)
    strips = strips_of(images)
    low, high = jnp.where(is_top, theirs, ours), jnp.where(is_top, ours, theirs)
    every_one = gather_classes(behind(low, smalls, *strips))
    rest = jnp.concatenate([qkv_master.reshape(-1, channels), out_master]).astype(jnp.bfloat16)
    rest = behind(rest, theirs)
    rest_two = pair_up(rest, exchange(rest, top_mask), jnp.logical_not(is_top), 0)
    smalls = smalls.reshape(devices, -1)
    gain_f = smalls[:, : gains.size].reshape(channels, 6)
    dp_smalls = smalls.reshape(lax.axis_size("dp"), lax.axis_size("head"), -1)[:, 0, gains.size :]
    extents_all = dp_smalls[:, : 2 * local_samples].reshape(-1, 2)
    times_all = dp_smalls[:, 2 * local_samples : 3 * local_samples].reshape(-1).astype(jnp.int32)
    divisor = jnp.sum(extents_all[:, 0] * extents_all[:, 1])

    parts = lax.axis_size("head")
    samples, strip_rows, width_px, _ = strips[0].shape
    places = lax.axis_index("head") ^ jnp.arange(parts, dtype=jnp.int32)
    rows = strip_rows * parts
    pixels = rows * width_px
    first = lax.axis_index("head") * samples
    own_times = lax.dynamic_slice_in_dim(timesteps, first, samples)
    own_extents = lax.dynamic_slice_in_dim(extents, first, samples)

    log_beta, log_tilde, factor = plan(own_times)
    embedded_all = jax.nn.silu(embed(times_all, wide)).astype(jnp.bfloat16)
    film_rows_out = lax.dot_general(
        film_master.astype(jnp.bfloat16),
        embedded_all,
        (((1,), (1,)), ((), ())),
        preferred_element_type=jnp.float32,
    )
    film_flat = film_rows_out.T.reshape(-1, channels)
    film_high = lax.reduce_precision(film_flat, 8, 7)
    film_parts = jnp.concatenate([film_high, film_flat - film_high]).astype(jnp.bfloat16)
    film_lines = film_flat.shape[0]
    film_two = pair_up(film_parts, exchange(film_parts, top_mask), jnp.logical_not(is_top), 0)
    two_block = jnp.concatenate(
        [high, rest_two.reshape(-1, channels), film_two.reshape(-1, channels)]
    )
    every_two = gather_classes(behind(two_block, every_one))
    gain_gate = two_block
    gains_t = behind(jnp.pad(gain_f.T, ((0, 2), (0, 0))), gain_gate)
    member = jnp.asarray(np.kron(np.eye(GROUPS), np.ones((channels // GROUPS,) * 2)), jnp.bfloat16)
    scalars = jnp.stack(
        [log_beta, log_tilde, factor, jnp.broadcast_to(divisor, factor.shape)]
        + [own_extents[:, 0].astype(jnp.float32), own_extents[:, 1].astype(jnp.float32)],
        axis=1,
    )
    first_call, second_call, weights, second_back, first_back = block_calls(samples, pixels, channels)
    flat = lambda values: [v.reshape(samples, strip_rows * width_px, -1) for v in values]
    place = last_bit().reshape(1).astype(jnp.int32)
    pieces_one = conv_pieces(every_one, exchange(every_one, 1), conv_rows)
    inner, hidden_one, stats, source, taps_one = first_call(
        places, place, flat(strips), pieces_one, gains_t, member
    )
    every_two = behind(every_two, inner)
    other_two = exchange(every_two, 1)
    pieces_two = conv_pieces(every_two, other_two, conv_rows)
    film_at = conv_rows + 8 * out_rows
    first_own = lax.axis_index("dp") * local_samples + first
    line, spot = first_own * film_rows // channels, first_own * film_rows % channels
    film_got = pair_up(every_two[:, film_at:], other_two[:, film_at:], last_bit() == 0, 1)
    film_got = film_got.reshape(classes, 2, 2, 2, film_lines, channels)
    film_got = lax.dynamic_slice(
        film_got, (0, 0, 0, 0, line, spot), film_got.shape[:4] + (1, samples * film_rows)
    ).astype(jnp.float32)
    film_got = jnp.sum(film_got, axis=(3, 4)).reshape(classes, 2, 2, samples, film_rows)
    film_out = film_got.transpose(3, 2, 0, 1, 4).reshape(samples, devices * film_rows)
    noise_strips = strips_of(behind(noise, other_two))
    film = jnp.pad(film_out.reshape(samples, 2, channels), ((0, 0), (0, 6), (0, 0)))
    scale = 1.0 + film_out[:, :channels]
    middle, hidden_two, taps_two = second_call(
        place, pieces_two, inner, source, stats, film, gains_t
    )
    others = pair_up(every_two[:, conv_rows:film_at], other_two[:, conv_rows:film_at], last_bit() == 0, 1)
    others = jnp.moveaxis(others.reshape(-1, 2, 4 * out_rows, channels), 0, 1)
    others = others.reshape(devices, 4 * out_rows, channels)
    qkv_w = others[:, : 3 * out_rows].reshape(channels, 3 * channels)
    out_w = others[:, 3 * out_rows :].reshape(channels, channels)
    my_last = last_bit()
    line = jnp.arange(channels, dtype=jnp.int32)
    owner, spot = line // out_rows, line % out_rows
    source_device = (
        (owner % 2) * 2 * classes + (owner // 2 % classes) * 2 + (my_last ^ (owner // (2 * classes)))
    )
    order = (line[None, :] == (source_device * out_rows + spot)[:, None]).astype(jnp.bfloat16)
    grad_two_b, shares, sums_three, losses = attention_block(
        places, scalars, middle, flat(noise_strips), gains_t, member, qkv_w, out_w, order
    )
    loss_local = jnp.sum(losses)
    two_shares = weights(hidden_two, grad_two_b, place, classes, (shares,))
    grad_two_b = behind(grad_two_b, *two_shares)
    grad_one_b, sums_two = second_back(grad_two_b, inner, stats, film, gains_t, member, taps_two)
    two_sent = (two_shares[0].astype(jnp.float32) + exchange(two_shares[1], 1).astype(jnp.float32)).astype(jnp.bfloat16)
    share_two = jnp.sum(across_classes(two_sent).astype(jnp.float32), axis=0)
    one_shares = weights(behind(hidden_one, two_sent), grad_one_b, place, classes)
    one_sent = (one_shares[0].astype(jnp.float32) + exchange(one_shares[1], 1).astype(jnp.float32)).astype(jnp.bfloat16)
    share_one = jnp.sum(across_classes(one_sent).astype(jnp.float32), axis=0)
    grad_one_b = behind(grad_one_b, share_two, one_sent)
    sums_one = first_back(grad_one_b, source, stats, gains_t, taps_one)
    gain_one, bias_one = jnp.sum(sums_one[:, 0], axis=0), jnp.sum(sums_one[:, 1], axis=0)
    gain_two, bias_two = jnp.sum(sums_two[:, 0] * scale, axis=0), jnp.sum(sums_two[:, 1] * scale, axis=0)
    gain_three, bias_three = jnp.sum(sums_three[:, 0], axis=0), jnp.sum(sums_three[:, 1], axis=0)
    grad_scale = sums_two[:, 0] * gains_t[2] + sums_two[:, 1] * gains_t[3]
    film_grad_b = jnp.concatenate([grad_scale, sums_two[:, 1]], axis=1).astype(jnp.bfloat16)

    small_shares = share_two[conv_rows:].reshape(4, 2, out_rows, channels)
    keep_two = jnp.where(is_top, small_shares[:, 1], small_shares[:, 0])
    send_two = jnp.where(is_top, small_shares[:, 0], small_shares[:, 1])
    send_two = jnp.concatenate([share_two[:conv_rows], send_two.reshape(-1, channels)])
    got_two = exchange(send_two.astype(jnp.bfloat16), top_mask).astype(jnp.float32)
    got_one = exchange(share_one.astype(jnp.bfloat16), top_mask).astype(jnp.float32)
    conv_g = jnp.where(is_top, share_two[:conv_rows] + got_two[:conv_rows], share_one + got_one)
    small_g = keep_two + got_two[conv_rows:].reshape(keep_two.shape)
    qkv_g = jnp.concatenate([small_g[0], small_g[1], small_g[2]], axis=1)
    out_g = small_g[3]

    gain_grad = jnp.stack([gain_one, bias_one, gain_two, bias_two, gain_three, bias_three], axis=1)
    common = jnp.concatenate([film_grad_b.astype(jnp.float32).reshape(-1), loss_local[None]])
    parcel = jnp.concatenate(
        [
            behind(gain_grad, share_one).reshape(devices, -1),
            jnp.broadcast_to(common[None], (devices, common.shape[0])),
        ],
        axis=1,
    )
    length = parcel.shape[1]
    parcel = jnp.pad(parcel, ((0, 0), (0, -length % 1024))).reshape(devices, -1, 128)
    parcels = to_all(parcel).reshape(devices, -1)
    gain_g = jnp.sum(parcels[:, : gains.size], axis=0).reshape(gains.shape)
    film_all = parcels[:, gains.size : length - 1].reshape(-1, film_grad_b.shape[1])
    loss_total = jnp.sum(parcels[:, length - 1])
    film_own = lax.dynamic_slice_in_dim(film_all, device * film_rows, film_rows, axis=1)
    film_g = jnp.einsum(
        "sf,se->fe", film_own.astype(jnp.bfloat16), embedded_all, preferred_element_type=jnp.float32
    )
    reduced = (film_g, conv_g, qkv_g, out_g, gain_g)
    squares = jnp.zeros((), jnp.float32)
    for gradient in reduced:
        squares = squares + jnp.sum(gradient * gradient)
    grad_norm = jnp.sqrt(jnp.sum(to_all(jnp.broadcast_to(squares, (devices, 8, 128)))[:, 0, 0]))
    clip_factor = jnp.minimum(1.0, THRESHOLD / (grad_norm + 1e-06))
    film_res = adamw(film_master, film_g, film_first, film_second, RATE_MATRIX, DECAY, clip_factor)
    conv_res = adamw(conv_master, conv_g, conv_first, conv_second, RATE_MATRIX, DECAY, clip_factor)
    qkv_res = adamw(qkv_master, qkv_g, qkv_first, qkv_second, RATE_MATRIX, DECAY, clip_factor)
    out_res = adamw(out_master, out_g, out_first, out_second, RATE_MATRIX, DECAY, clip_factor)
    gain_res = adamw(gains, gain_g, gain_first, gain_second, RATE_GAIN, 0.0, clip_factor)
    loss_parts = jnp.stack([loss_total, divisor])
    return (
        loss_parts,
        grad_norm,
        film_res[0],
        film_res[1],
        film_res[2],
        conv_res[0],
        conv_res[1],
        conv_res[2],
        qkv_res[0],
        qkv_res[1],
        qkv_res[2],
        out_res[0],
        out_res[1],
        out_res[2],
        gain_res[0],
        gain_res[1],
        gain_res[2],
    )


def solution(mesh):
    in_specs = (
        P("dp", "head", None, None),
        P("dp", "head", None, None),
        P("dp"),
        P("dp", None),
        P(("dp", "head"), None),
        P(("dp", "head"), None),
        P(("dp", "head"), None),
        P(("dp", "head"), None),
        P(("dp", "head"), None),
        P(("dp", "head"), None),
        P(("dp", "head"), None),
        P(("dp", "head"), None),
        P(("dp", "head"), None),
        P(("dp", "head"), None),
        P(("dp", "head"), None),
        P(("dp", "head"), None),
        P(("dp", "head"), None),
        P(("dp", "head"), None),
        P(("dp", "head"), None),
    )
    out_specs = (
        P(),
        P(),
        P(("dp", "head"), None),
        P(("dp", "head"), None),
        P(("dp", "head"), None),
        P(("dp", "head"), None),
        P(("dp", "head"), None),
        P(("dp", "head"), None),
        P(("dp", "head"), None),
        P(("dp", "head"), None),
        P(("dp", "head"), None),
        P(("dp", "head"), None),
        P(("dp", "head"), None),
        P(("dp", "head"), None),
        P(("dp", "head"), None),
        P(("dp", "head"), None),
        P(("dp", "head"), None),
    )
    return jax.shard_map(body, mesh=mesh, in_specs=in_specs, out_specs=out_specs, check_vma=False)
```

```python
import functools
import math

import jax
import jax.numpy as jnp
import numpy as np
from jax import lax
from jax.experimental import pallas as pl
from jax.experimental.pallas import tpu as pltpu
from jax.sharding import PartitionSpec as P

HEADS = 4
GROUPS = 32
STEP = 10
TSTEPS = 4000


EPS_NORM = 1e-05
VLB_WEIGHT = 0.001
BETA_ONE = 0.9
BETA_TWO = 0.999
ADAM_EPS = 1e-08
DECAY = 0.01
RATE_MATRIX = 0.05
RATE_GAIN = 0.4
THRESHOLD = 0.002
OFFSET = 0.008
LOG2E = math.log2(math.e)
VMEM_LIMIT = 56 << 20


def plan(step_ids):
    moment = step_ids.astype(jnp.float32)

    def angle(values):
        return (values / TSTEPS + OFFSET) / (1.0 + OFFSET) * (0.5 * math.pi)

    start = angle(jnp.zeros_like(moment))
    before = angle(moment - 1.0)
    later_angle = angle(moment)
    beta_now = jnp.sin(later_angle - before) * jnp.sin(later_angle + before) / jnp.cos(before) ** 2
    fade_now = jnp.sin(later_angle - start) * jnp.sin(later_angle + start) / jnp.cos(start) ** 2
    fade_prev = jnp.sin(before - start) * jnp.sin(before + start) / jnp.cos(start) ** 2
    log_beta = jnp.log(beta_now)
    log_tilde = jnp.log(beta_now * fade_prev / fade_now)
    factor = beta_now * beta_now / ((1.0 - beta_now) * fade_now)
    return (log_beta, log_tilde, factor)


def embed(step_ids, width):
    half_width = width // 2
    frequency = jnp.exp(-math.log(10000.0) * jnp.arange(half_width, dtype=jnp.float32) / half_width)
    phases = step_ids.astype(jnp.float32)[:, None] * frequency[None, :]
    return jnp.concatenate([jnp.cos(phases), jnp.sin(phases)], axis=1)


def behind(values, *others):
    return lax.optimization_barrier((values,) + others)[0]


def pair_up(block, other, low, place):
    shape = [2 if dim == place else 1 for dim in range(block.ndim + 1)]
    first = jnp.arange(2, dtype=jnp.int32).reshape(shape) == 0
    return jnp.where(first == low, jnp.expand_dims(block, place), jnp.expand_dims(other, place))


def class_count():
    return lax.axis_size("dp") * lax.axis_size("head") // 4


def last_bit():
    return lax.axis_index("head") % 2


def exchange(values, mask):
    size = lax.axis_size("dp") * lax.axis_size("head")
    return lax.ppermute(values, ("dp", "head"), [(i, i ^ mask) for i in range(size)])


def across_classes(blocks):
    count = class_count()
    groups = [
        [(high * count + k) * 2 + last for k in range(count)] for high in range(2) for last in range(2)
    ]
    return lax.all_to_all(
        blocks, ("dp", "head"), split_axis=0, concat_axis=0, axis_index_groups=groups, tiled=True
    )


def gather_classes(block):
    return across_classes(jnp.broadcast_to(block[None], (class_count(),) + block.shape))


def conv_pieces(both, other, rows):
    if rows % 8 == 0:
        return [both, other]
    joined = pair_up(both[:, :rows], other[:, :rows], last_bit() == 0, 1)
    return [joined.reshape(-1, both.shape[-1])]


def to_all(blocks):
    return lax.all_to_all(blocks, ("dp", "head"), split_axis=0, concat_axis=0, tiled=True)


def strips_of(values, cuts=()):
    parts = lax.axis_size("head")
    count = values.shape[0] // parts
    mine = lax.axis_index("head")
    strips = []
    for far in range(parts):
        strip = cuts[far] if cuts else lax.dynamic_slice_in_dim(values, (mine ^ far) * count, count, axis=0)
        if far:
            strip = lax.ppermute(strip, "head", [(i, i ^ far) for i in range(parts)])
        strips.append(strip)
    return strips


NN = (((1,), (0,)), ((), ()))
NT = (((1,), (1,)), ((), ()))
TN = (((0,), (0,)), ((), ()))


def mm(left, right, form=NN):
    return lax.dot_general(left, right, form, preferred_element_type=jnp.float32)


def group_total(rows, member):
    high = rows.astype(jnp.bfloat16).astype(jnp.float32)
    rest = rows - high
    mid = rest.astype(jnp.bfloat16).astype(jnp.float32)
    parts = jnp.concatenate([high, mid, rest - mid, jnp.zeros_like(rows)], axis=0)
    sums = mm(parts.astype(jnp.bfloat16), member)
    return sums[0:8] + sums[8:16] + sums[16:24]


def fold(values):
    rows, width = values.shape
    return jnp.sum(values.reshape(rows // 8, 8, width), axis=0)


def two_rows(first, second):
    first = jnp.sum(first, axis=0, keepdims=True)
    second = jnp.sum(second, axis=0, keepdims=True)
    row = lax.broadcasted_iota(jnp.int32, (8, first.shape[1]), 0)
    return jnp.where(row == 0, first, jnp.where(row == 1, second, 0.0))


def chunks(total, size, step, init):
    return lax.fori_loop(0, total // size, lambda m, c: step(pl.multiple_of(m * size, size), c), init)


def norm_sums(load, pixels, channels, member, size):
    def step(at, carry):
        values = load(at)
        return (carry[0] + fold(values), carry[1] + fold(values * values))

    zero = jnp.zeros((8, channels), jnp.float32)
    first, second = chunks(pixels, size, step, (zero, zero))
    count = pixels * (channels // GROUPS)
    sums = group_total(two_rows(first, second), member) / count
    mean = sums[0:1]
    inverse = lax.rsqrt(sums[1:2] - mean * mean + EPS_NORM)
    return mean, inverse


CHUNK = 1024
PART = 256


def attention_kernel(parts, places, scalars, middle, *refs):
    attention_body(places, scalars, middle, refs[:parts], *refs[parts:])


def attention_body(
    places,
    scalars,
    middle,
    strips,
    gains,
    member,
    qkv_w,
    out_w,
    order,
    down_out,
    shares,
    sums_out,
    loss_out,
    noise,
    qkv_wt,
    normed,
    qkv_t,
    probs,
    totals,
    mixed_t,
    attn_t,
    result,
    grad_b,
    back_t,
    dqkv_t,
    gn_t,
    qkv_acc,
    out_acc,
):
    sample = pl.program_id(0)
    _, pixels, channels = middle.shape
    half = channels // 2
    size = channels // HEADS
    factor = size ** (-0.5)
    width = int(round(pixels**0.5))

    @pl.when(sample == 0)
    def _():
        qkv_wt[...] = qkv_w[...].T
        qkv_acc[...] = jnp.zeros_like(qkv_acc)
        out_acc[...] = jnp.zeros_like(out_acc)

    join_strips(places, strips, noise)
    load = lambda at: middle[0, pl.ds(at, PART), :]
    mean, inverse = norm_sums(load, pixels, channels, member[...], PART)
    gain, shift = gains[4:5], gains[5:6]

    def normalize(at, carry):
        hat = (load(at) - mean) * inverse
        normed[pl.ds(at, PART), :] = (hat * gain + shift).astype(jnp.bfloat16)
        return carry

    chunks(pixels, PART, normalize, 0)

    block = 256

    qkv_t[...] = mm(qkv_wt[...], normed[...], NT).astype(jnp.bfloat16)

    def rows_of_head(head, part):
        at = (3 * head + part) * size
        return slice(at, at + size)

    def scores_of(head):
        return mm(qkv_t[rows_of_head(head, 1), :].T, qkv_t[rows_of_head(head, 0), :])

    following = scores_of(0)
    for head in range(HEADS):
        scores = following
        if head + 1 < HEADS:
            following = scores_of(head + 1)
        top = jnp.max(scores, axis=0, keepdims=True)
        powers = jnp.exp2((scores - top) * (factor * LOG2E))
        inv = 1.0 / jnp.sum(powers, axis=0, keepdims=True)
        powers_b = powers.astype(jnp.bfloat16)
        probs[head] = powers_b
        totals[head] = jnp.broadcast_to(inv, (8, pixels))
        mixed = mm(qkv_t[rows_of_head(head, 2), :], powers_b) * inv
        at = slice(head * size, (head + 1) * size)
        mixed_t[at, :] = mixed
        attn_t[at, :] = mixed.astype(jnp.bfloat16)

    result[...] = mm(attn_t[...].T, out_w[...])
    beta_log, tilde_log, coef = scalars[sample, 0], scalars[sample, 1], scalars[sample, 2]
    divisor, high, wide = scalars[sample, 3], scalars[sample, 4], scalars[sample, 5]

    def losses(at, carry):
        total = load(at) + result[pl.ds(at, PART), :]
        pixel = at + lax.broadcasted_iota(jnp.int32, (PART, half), 0)
        row = (pixel // width).astype(jnp.float32)
        col = (pixel % width).astype(jnp.float32)
        valid = jnp.where((row >= width - high) & (col < wide), 1.0, 0.0)
        residue = total[:, :half] - noise[pl.ds(at, PART), :].astype(jnp.float32)
        weight = jax.nn.sigmoid(total[:, half:])
        blended = weight * beta_log + (1.0 - weight) * tilde_log
        spread = jnp.exp(tilde_log - blended)
        damped = coef * residue * residue * jnp.exp(-blended)
        diverge = 0.5 * (-1.0 + blended - tilde_log + spread + damped)
        pixel_loss = valid * (residue * residue + VLB_WEIGHT * diverge)
        scale = valid / (half * divisor)
        grad_guess = 2.0 * residue * scale
        grad_raw = (
            scale * (0.5 * VLB_WEIGHT) * (1.0 - spread - damped)
            * (beta_log - tilde_log) * weight * (1.0 - weight)
        )
        grad = jnp.concatenate([grad_guess, grad_raw], axis=-1)
        result[pl.ds(at, PART), :] = grad
        grad_b[pl.ds(at, PART), :] = grad.astype(jnp.bfloat16)
        return carry + fold(pixel_loss)

    loss = chunks(pixels, PART, losses, jnp.zeros((8, half), jnp.float32))
    loss_out[0] = loss * (1.0 / half)

    out_acc[...] += mm(attn_t[...], grad_b[...])
    back_t[...] = mm(out_w[...], grad_b[...], NT).astype(jnp.bfloat16)

    def upstream_of(head):
        return back_t[head * size : (head + 1) * size, :]

    def soft_grad(head):
        return mm(qkv_t[rows_of_head(head, 2), :].T, upstream_of(head))

    following = soft_grad(0)
    for head in range(HEADS):
        grad_soft = following
        if head + 1 < HEADS:
            following = soft_grad(head + 1)
        upstream = upstream_of(head)
        inner = jnp.sum(
            upstream.astype(jnp.float32) * mixed_t[head * size : (head + 1) * size, :],
            axis=0,
            keepdims=True,
        )
        soft = probs[head].astype(jnp.float32) * totals[head, 0:1]
        grad_scores = (soft * (grad_soft - inner)).astype(jnp.bfloat16)
        queries_t, keys_t = qkv_t[rows_of_head(head, 0), :], qkv_t[rows_of_head(head, 1), :]
        dqkv_t[rows_of_head(head, 0), :] = (mm(keys_t, grad_scores) * factor).astype(jnp.bfloat16)
        dqkv_t[rows_of_head(head, 1), :] = (mm(queries_t, grad_scores, NT) * factor).astype(jnp.bfloat16)
        dqkv_t[rows_of_head(head, 2), :] = mm(upstream, soft.astype(jnp.bfloat16), NT).astype(jnp.bfloat16)

    qkv_acc[...] += mm(normed[...].T, dqkv_t[...], NT)
    gn_t[...] = mm(qkv_w[...], dqkv_t[...]).T

    def back_sums(at, carry):
        hat = (load(at) - mean) * inverse
        grad = gn_t[pl.ds(at, PART), :]
        return (carry[0] + fold(grad * hat), carry[1] + fold(grad))

    zero = jnp.zeros((8, channels), jnp.float32)
    both = chunks(pixels, PART, back_sums, (zero, zero))
    rows = two_rows(*both)
    sums_out[0] = rows
    means = group_total(rows * gain, member[...]) / (pixels * (channels // GROUPS))

    def back_norm(at, carry):
        hat = (load(at) - mean) * inverse
        grad = gn_t[pl.ds(at, PART), :] * gain
        back = (grad - means[1:2] - hat * means[0:1]) * inverse
        down_out[0, pl.ds(at, PART), :] = (result[pl.ds(at, PART), :] + back).astype(jnp.bfloat16)
        return carry

    chunks(pixels, PART, back_norm, 0)

    @pl.when(sample == pl.num_programs(0) - 1)
    def _():
        wide = 3 * channels
        shares[:, 0:wide] = mm(order[...], qkv_acc[...].astype(jnp.bfloat16)).astype(jnp.bfloat16)
        shares[:, wide:] = mm(order[...], out_acc[...].astype(jnp.bfloat16)).astype(jnp.bfloat16)


def attention_block(places, scalars, middle, strips, gains, member, qkv_w, out_w, order):
    parts = len(strips)
    samples, pixels, channels = middle.shape
    half = channels // 2
    bf, f32 = jnp.bfloat16, jnp.float32
    return pl.pallas_call(
        functools.partial(attention_kernel, parts),
        grid=(samples,),
        in_specs=[
            pl.BlockSpec(memory_space=pltpu.SMEM),
            pl.BlockSpec(memory_space=pltpu.SMEM),
            each(pixels, channels),
            *[each(pixels // parts, half)] * parts,
            whole(8, channels),
            whole(channels, channels),
            whole(channels, 3 * channels),
            whole(channels, channels),
            whole(channels, channels),
        ],
        out_specs=[
            each(pixels, channels),
            whole(channels, 4 * channels),
            each(8, channels),
            each(8, half),
        ],
        out_shape=[
            jax.ShapeDtypeStruct((samples, pixels, channels), bf),
            jax.ShapeDtypeStruct((channels, 4 * channels), bf),
            jax.ShapeDtypeStruct((samples, 8, channels), f32),
            jax.ShapeDtypeStruct((samples, 8, half), f32),
        ],
        scratch_shapes=[
            pltpu.VMEM((pixels, half), bf),
            pltpu.VMEM((3 * channels, channels), bf),
            pltpu.VMEM((pixels, channels), bf),
            pltpu.VMEM((3 * channels, pixels), bf),
            pltpu.VMEM((HEADS, pixels, pixels), bf),
            pltpu.VMEM((HEADS, 8, pixels), f32),
            pltpu.VMEM((channels, pixels), f32),
            pltpu.VMEM((channels, pixels), bf),
            pltpu.VMEM((pixels, channels), f32),
            pltpu.VMEM((pixels, channels), bf),
            pltpu.VMEM((channels, pixels), bf),
            pltpu.VMEM((3 * channels, pixels), bf),
            pltpu.VMEM((pixels, channels), f32),
            pltpu.VMEM((channels, 3 * channels), f32),
            pltpu.VMEM((channels, channels), f32),
        ],
        compiler_params=pltpu.CompilerParams(vmem_limit_bytes=VMEM_LIMIT),
        cost_estimate=pl.CostEstimate(
            flops=30 * samples * pixels * pixels * channels,
            bytes_accessed=8 * samples * pixels * channels,
            transcendentals=samples * HEADS * pixels * pixels,
        ),
    )(places, scalars, middle, *strips, gains, member, qkv_w, out_w, order)


def fill(padded, at, values, width):
    rows, channels = values.shape
    col = lax.broadcasted_iota(jnp.int32, values.shape, 0) % width
    there = pl.ds(at + width, rows)
    left = jnp.where(col == 0, 0.0, pltpu.roll(values, 1, 0))
    right = jnp.where(col == width - 1, 0.0, pltpu.roll(values, rows - 1, 0))
    padded[there, 0:channels] = left.astype(jnp.bfloat16)
    padded[there, channels : 2 * channels] = values.astype(jnp.bfloat16)
    padded[there, 2 * channels :] = right.astype(jnp.bfloat16)


def clear_edges(padded, width):
    rows, wide = padded.shape
    padded[0:width, :] = jnp.zeros((width, wide), jnp.bfloat16)
    padded[rows - width :, :] = jnp.zeros((width, wide), jnp.bfloat16)


def side(pixels):
    return int(round(pixels**0.5))


def taps_product(padded, weight, pixels, width):
    wide = padded.shape[1]
    total = mm(padded[0:pixels, :], weight(0))
    for i in (1, 2):
        total += mm(padded[i * width : i * width + pixels, :], weight(i))
    return total


def rows_of(*rows):
    index = lax.broadcasted_iota(jnp.int32, (8, rows[0].shape[1]), 0)
    total = jnp.zeros(index.shape, jnp.float32)
    for place, row in enumerate(rows):
        total = jnp.where(index == place, row, total)
    return total


def join_strips(places, strips, joined):
    rows = strips[0].shape[1]
    for far, strip in enumerate(strips):
        joined[pl.ds(pl.multiple_of(places[far] * rows, rows), rows), :] = strip[0]


def join_weights(last, pieces, weight):
    if len(pieces) == 1:
        weight[...] = pieces[0][...]
        return
    rows = weight.shape[0] // (2 * pieces[0].shape[0])
    for low in range(2):

        @pl.when(last[0] == low)
        def _():
            for k in range(pieces[0].shape[0]):
                both = [pieces[low ^ half][k, 0:rows, :].astype(jnp.float32) for half in range(2)]
                pair = jnp.concatenate(both, axis=0).astype(jnp.bfloat16)
                weight[2 * rows * k : 2 * rows * (k + 1), :] = pair


def first_kernel(parts, count, places, last, *refs):
    strips, pieces, refs = refs[:parts], refs[parts : parts + count], refs[parts + count :]
    gains, member, inner, hidden, stats, images, weight, padded = refs
    _, pixels, channels = images.shape

    @pl.when(pl.program_id(0) == 0)
    def _():
        join_weights(last, pieces, weight)

    join_strips(places, strips, images.at[0])
    width = side(pixels)
    wide = 3 * channels
    load = lambda at: images[0, pl.ds(at, CHUNK), :].astype(jnp.float32)
    mean, inverse = norm_sums(load, pixels, channels, member[...], CHUNK)
    gain, shift = gains[0:1], gains[1:2]
    clear_edges(padded, width)

    def activate(at, carry):
        out = (load(at) - mean) * inverse * gain + shift
        value = out * jax.nn.sigmoid(out)
        hidden[0, pl.ds(at, CHUNK), :] = value.astype(jnp.bfloat16)
        fill(padded, at, value, width)
        return carry

    chunks(pixels, CHUNK, activate, 0)
    inner[0] = taps_product(padded, lambda i: weight[i * wide : (i + 1) * wide, :], pixels, width)
    mean_two, inverse_two = norm_sums(
        lambda at: inner[0, pl.ds(at, CHUNK), :], pixels, channels, member[...], CHUNK
    )
    stats[0] = rows_of(mean, inverse, mean_two, inverse_two)


def second_kernel(count, last, *refs):
    pieces, refs = refs[:count], refs[count:]
    inner, images, stats, film, gains, middle, hidden, weight, padded = refs
    _, pixels, channels = inner.shape

    @pl.when(pl.program_id(0) == 0)
    def _():
        join_weights(last, pieces, weight)

    width = side(pixels)
    wide = 3 * channels
    mean, inverse = stats[0, 2:3], stats[0, 3:4]
    scale, lift = 1.0 + film[0, 0:1], film[0, 1:2]
    gain, shift = gains[2:3], gains[3:4]
    clear_edges(padded, width)

    def activate(at, carry):
        out = (inner[0, pl.ds(at, CHUNK), :] - mean) * inverse * gain + shift
        lifted = out * scale + lift
        value = lifted * jax.nn.sigmoid(lifted)
        hidden[0, pl.ds(at, CHUNK), :] = value.astype(jnp.bfloat16)
        fill(padded, at, value, width)
        return carry

    chunks(pixels, CHUNK, activate, 0)
    middle[0] = images[0].astype(jnp.float32) + taps_product(
        padded, lambda i: weight[i * wide : (i + 1) * wide, :], pixels, width
    )


def weights_sums(hidden, grad, padded, total):
    _, pixels, channels = hidden.shape
    width = side(pixels)
    wide = 3 * channels
    clear_edges(padded, width)

    def spread(at, carry):
        fill(padded, at, hidden[0, pl.ds(at, CHUNK), :].astype(jnp.float32), width)
        return carry

    chunks(pixels, CHUNK, spread, 0)

    @pl.when(pl.program_id(0) == 0)
    def _():
        total[...] = jnp.zeros_like(total)

    for i in range(3):
        total[i * wide : (i + 1) * wide, :] += mm(
            padded[i * width : i * width + pixels, :], grad[0], TN
        )


def weights_kernel(hidden, grad, out, padded, total):
    weights_sums(hidden, grad, padded, total)

    @pl.when(pl.program_id(0) == pl.num_programs(0) - 1)
    def _():
        out[...] = total[...].astype(jnp.bfloat16)


def shares_kernel(extra, place, hidden, grad, *refs):
    others, (mine, theirs, padded, total) = refs[:extra], refs[extra:]
    weights_sums(hidden, grad, padded, total)
    classes = mine.shape[0]
    channels = total.shape[1]
    rows = total.shape[0] // (2 * classes)

    @pl.when(pl.program_id(0) == pl.num_programs(0) - 1)
    def _():
        for far in range(classes):
            for last, out in enumerate((mine, theirs)):
                owner = far * 2 + (place[0] ^ last)
                parts = [total[pl.ds(pl.multiple_of(owner * rows, 8), rows), :]]
                for other in others:
                    lines = other.shape[0] // (2 * classes)
                    at = (last * classes + far) * lines
                    for k in range(other.shape[1] // channels):
                        piece = other[at : at + lines, k * channels : (k + 1) * channels]
                        parts.append(piece.astype(jnp.float32))
                out[far] = jnp.concatenate(parts, axis=0).astype(jnp.bfloat16)


def turn_taps(weight, turned):
    channels = weight.shape[1]
    for i in range(3):
        for j in range(3):
            tap = 3 * (2 - i) + 2 - j
            turned[i, :, j * channels : (j + 1) * channels] = weight[
                tap * channels : (tap + 1) * channels, :
            ]


def input_grad(grad, weight, padded, turned, down):
    _, pixels, channels = grad.shape
    width = side(pixels)

    @pl.when(pl.program_id(0) == 0)
    def _():
        turn_taps(weight, turned)

    clear_edges(padded, width)

    def spread(at, carry):
        fill(padded, at, grad[0, pl.ds(at, CHUNK), :].astype(jnp.float32), width)
        return carry

    chunks(pixels, CHUNK, spread, 0)
    total = mm(padded[0:pixels, :], turned[0], NT)
    for i in (1, 2):
        total += mm(padded[i * width : i * width + pixels, :], turned[i], NT)
    down[...] = total


def slope_of(values):
    sig = jax.nn.sigmoid(values)
    return sig * (1.0 + values * (1.0 - sig))


def second_back_kernel(
    grad, inner, stats, film, gains, member, weight, grad_out, sums_out, padded, turned, down
):
    _, pixels, channels = grad.shape
    input_grad(grad, weight, padded, turned, down)
    mean, inverse = stats[0, 2:3], stats[0, 3:4]
    scale, lift = 1.0 + film[0, 0:1], film[0, 1:2]
    gain, shift = gains[2:3], gains[3:4]

    def slopes(at, carry):
        hat = (inner[0, pl.ds(at, CHUNK), :] - mean) * inverse
        lifted = (hat * gain + shift) * scale + lift
        lifted_grad = down[pl.ds(at, CHUNK), :] * slope_of(lifted)
        down[pl.ds(at, CHUNK), :] = lifted_grad
        return (carry[0] + fold(lifted_grad * hat), carry[1] + fold(lifted_grad))

    zero = jnp.zeros((8, channels), jnp.float32)
    rows = two_rows(*chunks(pixels, CHUNK, slopes, (zero, zero)))
    sums_out[0] = rows
    factor = scale * gain
    means = group_total(rows * factor, member[...]) / (pixels * (channels // GROUPS))

    def back_norm(at, carry):
        hat = (inner[0, pl.ds(at, CHUNK), :] - mean) * inverse
        back = (down[pl.ds(at, CHUNK), :] * factor - means[1:2] - hat * means[0:1]) * inverse
        grad_out[0, pl.ds(at, CHUNK), :] = back.astype(jnp.bfloat16)
        return carry

    chunks(pixels, CHUNK, back_norm, 0)


def first_back_kernel(grad, images, stats, gains, weight, sums_out, padded, turned, down):
    _, pixels, channels = grad.shape
    input_grad(grad, weight, padded, turned, down)
    mean, inverse = stats[0, 0:1], stats[0, 1:2]
    gain, shift = gains[0:1], gains[1:2]

    def slopes(at, carry):
        hat = (images[0, pl.ds(at, CHUNK), :].astype(jnp.float32) - mean) * inverse
        grad_first = down[pl.ds(at, CHUNK), :] * slope_of(hat * gain + shift)
        return (carry[0] + fold(grad_first * hat), carry[1] + fold(grad_first))

    zero = jnp.zeros((8, channels), jnp.float32)
    sums_out[0] = two_rows(*chunks(pixels, CHUNK, slopes, (zero, zero)))


def whole(*shape):
    return pl.BlockSpec(shape, lambda s: (0,) * len(shape))


def each(*shape):
    return pl.BlockSpec((1,) + shape, lambda s: (s,) + (0,) * len(shape))


def per_sample(kernel, samples, in_specs, outs, scratch, flops, *operands):
    return pl.pallas_call(
        kernel,
        grid=(samples,),
        in_specs=in_specs,
        out_specs=[spec for spec, _ in outs],
        out_shape=[shape for _, shape in outs],
        scratch_shapes=scratch,
        compiler_params=pltpu.CompilerParams(vmem_limit_bytes=VMEM_LIMIT),
        cost_estimate=pl.CostEstimate(flops=flops, bytes_accessed=flops // 1000, transcendentals=0),
    )(*operands)


def sized(dtype, *shape):
    return jax.ShapeDtypeStruct(shape, dtype)


def block_calls(samples, pixels, channels):
    width = side(pixels)
    act = each(pixels, channels)
    few = each(8, channels)
    gain_spec, member_spec = whole(8, channels), whole(channels, channels)
    weight_spec = whole(9 * channels, channels)
    bf, f32 = jnp.bfloat16, jnp.float32
    padded = pltpu.VMEM((pixels + 2 * width, 3 * channels), bf)
    turned = pltpu.VMEM((3, channels, 3 * channels), bf)
    down = pltpu.VMEM((pixels, channels), f32)
    act_b = sized(bf, samples, pixels, channels)
    act_f = sized(f32, samples, pixels, channels)
    few_f = sized(f32, samples, 8, channels)
    flops = 18 * samples * pixels * channels * channels

    weight_out = (weight_spec, sized(bf, 9 * channels, channels))
    smem = pl.BlockSpec(memory_space=pltpu.SMEM)

    def first(places, last, strips, pieces, gains, member):
        parts, count = len(strips), len(pieces)
        return per_sample(
            functools.partial(first_kernel, parts, count), samples,
            [smem, smem] + [each(pixels // parts, channels)] * parts
            + [whole(*piece.shape) for piece in pieces] + [gain_spec, member_spec],
            [(act, act_f), (act, act_b), (few, few_f), (act, act_b), weight_out], [padded], flops,
            places, last, *strips, *pieces, gains, member,
        )

    def second(last, pieces, inner, images, stats, film, gains):
        return per_sample(
            functools.partial(second_kernel, len(pieces)), samples,
            [smem] + [whole(*piece.shape) for piece in pieces] + [act, act, few, few, gain_spec],
            [(act, act_f), (act, act_b), weight_out], [padded], flops,
            last, *pieces, inner, images, stats, film, gains,
        )

    def weights(hidden, grad, place, classes, others=()):
        scratch = [padded, pltpu.VMEM((9 * channels, channels), f32)]
        conv_rows = 9 * channels // (2 * classes)
        more = [other.shape[0] * other.shape[1] // (2 * classes * channels) for other in others]
        if conv_rows % 8:
            (whole_grad,) = per_sample(
                weights_kernel, samples, [act, act],
                [(weight_spec, sized(bf, 9 * channels, channels))], scratch, flops, hidden, grad,
            )
            blocks = whole_grad.reshape(2 * classes, conv_rows, channels)
            both = []
            for last in range(2):
                owner = place[0] ^ last
                cut = blocks.reshape(classes, 2, conv_rows, channels)
                parts = [lax.dynamic_index_in_dim(cut, owner, 1, keepdims=False)]
                for other in others:
                    cut = other.reshape(2, classes, -1, other.shape[1] // channels, channels)[last]
                    parts.append(jnp.moveaxis(cut, 2, 1).reshape(classes, -1, channels))
                both.append(jnp.concatenate(parts, axis=1))
            return both
        shape = (classes, conv_rows + sum(more), channels)
        out = (whole(*shape), sized(bf, *shape))
        return per_sample(
            functools.partial(shares_kernel, len(others)), samples,
            [pl.BlockSpec(memory_space=pltpu.SMEM), act, act] + [whole(*o.shape) for o in others],
            [out, out], scratch, flops, place, hidden, grad, *others,
        )

    def second_back(grad, inner, stats, film, gains, member, weight):
        return per_sample(
            second_back_kernel, samples,
            [act, act, few, few, gain_spec, member_spec, weight_spec],
            [(act, act_b), (few, few_f)], [padded, turned, down], flops,
            grad, inner, stats, film, gains, member, weight,
        )

    def first_back(grad, images, stats, gains, weight):
        return per_sample(
            first_back_kernel, samples, [act, act, few, gain_spec, weight_spec],
            [(few, few_f)], [padded, turned, down], flops,
            grad, images, stats, gains, weight,
        )[0]

    return first, second, weights, second_back, first_back


def adamw(master, gradient, first, second, step_rate, decay_rate, clip_factor):
    gradient = gradient * clip_factor
    first_new = BETA_ONE * first + (1.0 - BETA_ONE) * gradient
    second_new = BETA_TWO * second + (1.0 - BETA_TWO) * gradient * gradient
    ratio = (
        first_new
        / (1.0 - BETA_ONE**STEP)
        / (jnp.sqrt(second_new / (1.0 - BETA_TWO**STEP)) + ADAM_EPS)
    )
    return (master - step_rate * (ratio + decay_rate * master), first_new, second_new)


def body(
    images,
    noise,
    timesteps,
    extents,
    film_master,
    conv_master,
    qkv_master,
    out_master,
    gains,
    film_first,
    film_second,
    conv_first,
    conv_second,
    qkv_first,
    qkv_second,
    out_first,
    out_second,
    gain_first,
    gain_second,
):
    devices = lax.axis_size("dp") * lax.axis_size("head")
    device = lax.axis_index("dp") * lax.axis_size("head") + lax.axis_index("head")
    channels = images.shape[-1]
    wide = film_master.shape[1]
    half_width = channels // 2
    conv_rows = conv_master.shape[0]
    film_rows = film_master.shape[0]
    out_rows = out_master.shape[0]

    local_samples = timesteps.shape[0]
    small = jnp.concatenate(
        [
            lax.reduce_precision(gains.reshape(-1), 8, 7),
            extents.astype(jnp.float32).reshape(-1),
            timesteps.astype(jnp.float32),
        ]
    )
    small = jnp.pad(small, (0, -small.shape[0] % 128))
    smalls = to_all(jnp.broadcast_to(small[None, None], (devices, 1, small.shape[0])))
    classes = class_count()
    top_mask = devices // 2
    is_top = device >= top_mask
    ours = conv_master.astype(jnp.bfloat16)
    theirs = exchange(ours, top_mask)
    strips = strips_of(images)
    low, high = jnp.where(is_top, theirs, ours), jnp.where(is_top, ours, theirs)
    every_one = gather_classes(behind(low, smalls, *strips))
    rest = jnp.concatenate([qkv_master.reshape(-1, channels), out_master]).astype(jnp.bfloat16)
    rest = behind(rest, theirs)
    rest_two = pair_up(rest, exchange(rest, top_mask), jnp.logical_not(is_top), 0)
    smalls = smalls.reshape(devices, -1)
    gain_f = smalls[:, : gains.size].reshape(channels, 6)
    dp_smalls = smalls.reshape(lax.axis_size("dp"), lax.axis_size("head"), -1)[:, 0, gains.size :]
    extents_all = dp_smalls[:, : 2 * local_samples].reshape(-1, 2)
    times_all = dp_smalls[:, 2 * local_samples : 3 * local_samples].reshape(-1).astype(jnp.int32)
    divisor = jnp.sum(extents_all[:, 0] * extents_all[:, 1])

    parts = lax.axis_size("head")
    samples, strip_rows, width_px, _ = strips[0].shape
    places = lax.axis_index("head") ^ jnp.arange(parts, dtype=jnp.int32)
    rows = strip_rows * parts
    pixels = rows * width_px
    first = lax.axis_index("head") * samples
    own_times = lax.dynamic_slice_in_dim(timesteps, first, samples)
    own_extents = lax.dynamic_slice_in_dim(extents, first, samples)

    log_beta, log_tilde, factor = plan(own_times)
    embedded_all = jax.nn.silu(embed(times_all, wide)).astype(jnp.bfloat16)
    film_rows_out = lax.dot_general(
        film_master.astype(jnp.bfloat16),
        embedded_all,
        (((1,), (1,)), ((), ())),
        preferred_element_type=jnp.float32,
    )
    film_flat = film_rows_out.T.reshape(-1, channels)
    film_high = lax.reduce_precision(film_flat, 8, 7)
    film_parts = jnp.concatenate([film_high, film_flat - film_high]).astype(jnp.bfloat16)
    film_lines = film_flat.shape[0]
    film_two = pair_up(film_parts, exchange(film_parts, top_mask), jnp.logical_not(is_top), 0)
    two_block = jnp.concatenate(
        [high, rest_two.reshape(-1, channels), film_two.reshape(-1, channels)]
    )
    mine = lax.axis_index("head")
    own_count = noise.shape[0] // lax.axis_size("head")
    noise_cuts = [
        lax.dynamic_slice_in_dim(noise, (mine ^ far) * own_count, own_count, axis=0)
        for far in range(lax.axis_size("head"))
    ]
    every_two = gather_classes(behind(two_block, every_one, *noise_cuts))
    gain_gate = two_block
    gains_t = behind(jnp.pad(gain_f.T, ((0, 2), (0, 0))), gain_gate)
    member = jnp.asarray(np.kron(np.eye(GROUPS), np.ones((channels // GROUPS,) * 2)), jnp.bfloat16)
    scalars = jnp.stack(
        [log_beta, log_tilde, factor, jnp.broadcast_to(divisor, factor.shape)]
        + [own_extents[:, 0].astype(jnp.float32), own_extents[:, 1].astype(jnp.float32)],
        axis=1,
    )
    first_call, second_call, weights, second_back, first_back = block_calls(samples, pixels, channels)
    flat = lambda values: [v.reshape(samples, strip_rows * width_px, -1) for v in values]
    place = last_bit().reshape(1).astype(jnp.int32)
    pieces_one = conv_pieces(every_one, exchange(every_one, 1), conv_rows)
    inner, hidden_one, stats, source, taps_one = first_call(
        places, place, flat(strips), pieces_one, gains_t, member
    )
    every_two = behind(every_two, inner)
    other_two = exchange(every_two, 1)
    pieces_two = conv_pieces(every_two, other_two, conv_rows)
    film_at = conv_rows + 8 * out_rows
    first_own = lax.axis_index("dp") * local_samples + first
    line, spot = first_own * film_rows // channels, first_own * film_rows % channels
    film_got = pair_up(every_two[:, film_at:], other_two[:, film_at:], last_bit() == 0, 1)
    film_got = film_got.reshape(classes, 2, 2, 2, film_lines, channels)
    film_got = lax.dynamic_slice(
        film_got, (0, 0, 0, 0, line, spot), film_got.shape[:4] + (1, samples * film_rows)
    ).astype(jnp.float32)
    film_got = jnp.sum(film_got, axis=(3, 4)).reshape(classes, 2, 2, samples, film_rows)
    film_out = film_got.transpose(3, 2, 0, 1, 4).reshape(samples, devices * film_rows)
    noise_strips = strips_of(noise, [behind(cut, other_two) for cut in noise_cuts])
    film = jnp.pad(film_out.reshape(samples, 2, channels), ((0, 0), (0, 6), (0, 0)))
    scale = 1.0 + film_out[:, :channels]
    middle, hidden_two, taps_two = second_call(
        place, pieces_two, inner, source, stats, film, gains_t
    )
    others = pair_up(every_two[:, conv_rows:film_at], other_two[:, conv_rows:film_at], last_bit() == 0, 1)
    others = jnp.moveaxis(others.reshape(-1, 2, 4 * out_rows, channels), 0, 1)
    others = others.reshape(devices, 4 * out_rows, channels)
    qkv_w = others[:, : 3 * out_rows].reshape(channels, 3 * channels)
    out_w = others[:, 3 * out_rows :].reshape(channels, channels)
    my_last = last_bit()
    line = jnp.arange(channels, dtype=jnp.int32)
    owner, spot = line // out_rows, line % out_rows
    source_device = (
        (owner % 2) * 2 * classes + (owner // 2 % classes) * 2 + (my_last ^ (owner // (2 * classes)))
    )
    order = (line[None, :] == (source_device * out_rows + spot)[:, None]).astype(jnp.bfloat16)
    grad_two_b, shares, sums_three, losses = attention_block(
        places, scalars, middle, flat(noise_strips), gains_t, member, qkv_w, out_w, order
    )
    loss_local = jnp.sum(losses)
    two_shares = weights(hidden_two, grad_two_b, place, classes, (shares,))
    grad_two_b = behind(grad_two_b, *two_shares)
    grad_one_b, sums_two = second_back(grad_two_b, inner, stats, film, gains_t, member, taps_two)
    two_sent = (two_shares[0].astype(jnp.float32) + exchange(two_shares[1], 1).astype(jnp.float32)).astype(jnp.bfloat16)
    share_two = jnp.sum(across_classes(two_sent).astype(jnp.float32), axis=0)
    one_shares = weights(behind(hidden_one, two_sent), grad_one_b, place, classes)
    one_sent = (one_shares[0].astype(jnp.float32) + exchange(one_shares[1], 1).astype(jnp.float32)).astype(jnp.bfloat16)
    share_one = jnp.sum(across_classes(one_sent).astype(jnp.float32), axis=0)
    grad_one_b = behind(grad_one_b, share_two, one_sent)
    sums_one = first_back(grad_one_b, source, stats, gains_t, taps_one)
    gain_one, bias_one = jnp.sum(sums_one[:, 0], axis=0), jnp.sum(sums_one[:, 1], axis=0)
    gain_two, bias_two = jnp.sum(sums_two[:, 0] * scale, axis=0), jnp.sum(sums_two[:, 1] * scale, axis=0)
    gain_three, bias_three = jnp.sum(sums_three[:, 0], axis=0), jnp.sum(sums_three[:, 1], axis=0)
    grad_scale = sums_two[:, 0] * gains_t[2] + sums_two[:, 1] * gains_t[3]
    film_grad_b = jnp.concatenate([grad_scale, sums_two[:, 1]], axis=1).astype(jnp.bfloat16)

    small_shares = share_two[conv_rows:].reshape(4, 2, out_rows, channels)
    keep_two = jnp.where(is_top, small_shares[:, 1], small_shares[:, 0])
    send_two = jnp.where(is_top, small_shares[:, 0], small_shares[:, 1])
    send_two = jnp.concatenate([share_two[:conv_rows], send_two.reshape(-1, channels)])
    got_two = exchange(send_two.astype(jnp.bfloat16), top_mask).astype(jnp.float32)
    one_low = share_one.astype(jnp.bfloat16)
    got_one = exchange(one_low, top_mask).astype(jnp.float32)
    conv_g = jnp.where(is_top, share_two[:conv_rows] + got_two[:conv_rows], share_one + got_one)
    small_g = keep_two + got_two[conv_rows:].reshape(keep_two.shape)
    qkv_g = jnp.concatenate([small_g[0], small_g[1], small_g[2]], axis=1)
    out_g = small_g[3]

    gain_grad = jnp.stack([gain_one, bias_one, gain_two, bias_two, gain_three, bias_three], axis=1)
    common = jnp.concatenate([film_grad_b.astype(jnp.float32).reshape(-1), loss_local[None]])
    parcel = jnp.concatenate(
        [
            behind(gain_grad, one_low).reshape(devices, -1),
            jnp.broadcast_to(common[None], (devices, common.shape[0])),
        ],
        axis=1,
    )
    length = parcel.shape[1]
    parcel = jnp.pad(parcel, ((0, 0), (0, -length % 1024))).reshape(devices, -1, 128)
    parcels = to_all(parcel).reshape(devices, -1)
    gain_g = jnp.sum(parcels[:, : gains.size], axis=0).reshape(gains.shape)
    film_all = parcels[:, gains.size : length - 1].reshape(-1, film_grad_b.shape[1])
    loss_total = jnp.sum(parcels[:, length - 1])
    film_own = lax.dynamic_slice_in_dim(film_all, device * film_rows, film_rows, axis=1)
    film_g = jnp.einsum(
        "sf,se->fe", film_own.astype(jnp.bfloat16), embedded_all, preferred_element_type=jnp.float32
    )
    reduced = (film_g, conv_g, qkv_g, out_g, gain_g)
    squares = jnp.zeros((), jnp.float32)
    for gradient in reduced:
        squares = squares + jnp.sum(gradient * gradient)
    grad_norm = jnp.sqrt(jnp.sum(to_all(jnp.broadcast_to(squares, (devices, 8, 128)))[:, 0, 0]))
    clip_factor = jnp.minimum(1.0, THRESHOLD / (grad_norm + 1e-06))
    film_res = adamw(film_master, film_g, film_first, film_second, RATE_MATRIX, DECAY, clip_factor)
    conv_res = adamw(conv_master, conv_g, conv_first, conv_second, RATE_MATRIX, DECAY, clip_factor)
    qkv_res = adamw(qkv_master, qkv_g, qkv_first, qkv_second, RATE_MATRIX, DECAY, clip_factor)
    out_res = adamw(out_master, out_g, out_first, out_second, RATE_MATRIX, DECAY, clip_factor)
    gain_res = adamw(gains, gain_g, gain_first, gain_second, RATE_GAIN, 0.0, clip_factor)
    loss_parts = jnp.stack([loss_total, divisor])
    return (
        loss_parts,
        grad_norm,
        film_res[0],
        film_res[1],
        film_res[2],
        conv_res[0],
        conv_res[1],
        conv_res[2],
        qkv_res[0],
        qkv_res[1],
        qkv_res[2],
        out_res[0],
        out_res[1],
        out_res[2],
        gain_res[0],
        gain_res[1],
        gain_res[2],
    )


def solution(mesh):
    in_specs = (
        P("dp", "head", None, None),
        P("dp", "head", None, None),
        P("dp"),
        P("dp", None),
        P(("dp", "head"), None),
        P(("dp", "head"), None),
        P(("dp", "head"), None),
        P(("dp", "head"), None),
        P(("dp", "head"), None),
        P(("dp", "head"), None),
        P(("dp", "head"), None),
        P(("dp", "head"), None),
        P(("dp", "head"), None),
        P(("dp", "head"), None),
        P(("dp", "head"), None),
        P(("dp", "head"), None),
        P(("dp", "head"), None),
        P(("dp", "head"), None),
        P(("dp", "head"), None),
    )
    out_specs = (
        P(),
        P(),
        P(("dp", "head"), None),
        P(("dp", "head"), None),
        P(("dp", "head"), None),
        P(("dp", "head"), None),
        P(("dp", "head"), None),
        P(("dp", "head"), None),
        P(("dp", "head"), None),
        P(("dp", "head"), None),
        P(("dp", "head"), None),
        P(("dp", "head"), None),
        P(("dp", "head"), None),
        P(("dp", "head"), None),
        P(("dp", "head"), None),
        P(("dp", "head"), None),
        P(("dp", "head"), None),
    )
    return jax.shard_map(body, mesh=mesh, in_specs=in_specs, out_specs=out_specs, check_vma=False)
```

```python
import functools
import math

import jax
import jax.numpy as jnp
import numpy as np
from jax import lax
from jax.experimental import pallas as pl
from jax.experimental.pallas import tpu as pltpu
from jax.sharding import PartitionSpec as P

HEADS = 4
GROUPS = 32
STEP = 10
TSTEPS = 4000


EPS_NORM = 1e-05
VLB_WEIGHT = 0.001
BETA_ONE = 0.9
BETA_TWO = 0.999
ADAM_EPS = 1e-08
DECAY = 0.01
RATE_MATRIX = 0.05
RATE_GAIN = 0.4
THRESHOLD = 0.002
OFFSET = 0.008
LOG2E = math.log2(math.e)
VMEM_LIMIT = 56 << 20


def plan(step_ids):
    moment = step_ids.astype(jnp.float32)

    def angle(values):
        return (values / TSTEPS + OFFSET) / (1.0 + OFFSET) * (0.5 * math.pi)

    start = angle(jnp.zeros_like(moment))
    before = angle(moment - 1.0)
    later_angle = angle(moment)
    beta_now = jnp.sin(later_angle - before) * jnp.sin(later_angle + before) / jnp.cos(before) ** 2
    fade_now = jnp.sin(later_angle - start) * jnp.sin(later_angle + start) / jnp.cos(start) ** 2
    fade_prev = jnp.sin(before - start) * jnp.sin(before + start) / jnp.cos(start) ** 2
    log_beta = jnp.log(beta_now)
    log_tilde = jnp.log(beta_now * fade_prev / fade_now)
    factor = beta_now * beta_now / ((1.0 - beta_now) * fade_now)
    return (log_beta, log_tilde, factor)


def embed(step_ids, width):
    half_width = width // 2
    frequency = jnp.exp(-math.log(10000.0) * jnp.arange(half_width, dtype=jnp.float32) / half_width)
    phases = step_ids.astype(jnp.float32)[:, None] * frequency[None, :]
    return jnp.concatenate([jnp.cos(phases), jnp.sin(phases)], axis=1)


def behind(values, *others):
    return lax.optimization_barrier((values,) + others)[0]


def pair_up(block, other, low, place):
    shape = [2 if dim == place else 1 for dim in range(block.ndim + 1)]
    first = jnp.arange(2, dtype=jnp.int32).reshape(shape) == 0
    return jnp.where(first == low, jnp.expand_dims(block, place), jnp.expand_dims(other, place))


def class_count():
    return lax.axis_size("dp") * lax.axis_size("head") // 4


def last_bit():
    return lax.axis_index("head") % 2


def exchange(values, mask):
    size = lax.axis_size("dp") * lax.axis_size("head")
    return lax.ppermute(values, ("dp", "head"), [(i, i ^ mask) for i in range(size)])


def across_classes(blocks):
    count = class_count()
    groups = [
        [(high * count + k) * 2 + last for k in range(count)] for high in range(2) for last in range(2)
    ]
    return lax.all_to_all(
        blocks, ("dp", "head"), split_axis=0, concat_axis=0, axis_index_groups=groups, tiled=True
    )


def gather_classes(block):
    return across_classes(jnp.broadcast_to(block[None], (class_count(),) + block.shape))


def conv_pieces(both, other, rows):
    if rows % 8 == 0:
        return [both, other]
    joined = pair_up(both[:, :rows], other[:, :rows], last_bit() == 0, 1)
    return [joined.reshape(-1, both.shape[-1])]


def to_all(blocks):
    return lax.all_to_all(blocks, ("dp", "head"), split_axis=0, concat_axis=0, tiled=True)


def strips_of(values, cuts=()):
    parts = lax.axis_size("head")
    count = values.shape[0] // parts
    mine = lax.axis_index("head")
    strips = []
    for far in range(parts):
        strip = cuts[far] if cuts else lax.dynamic_slice_in_dim(values, (mine ^ far) * count, count, axis=0)
        if far:
            strip = lax.ppermute(strip, "head", [(i, i ^ far) for i in range(parts)])
        strips.append(strip)
    return strips


NN = (((1,), (0,)), ((), ()))
NT = (((1,), (1,)), ((), ()))
TN = (((0,), (0,)), ((), ()))


def mm(left, right, form=NN):
    return lax.dot_general(left, right, form, preferred_element_type=jnp.float32)


def group_total(rows, member):
    high = rows.astype(jnp.bfloat16).astype(jnp.float32)
    rest = rows - high
    mid = rest.astype(jnp.bfloat16).astype(jnp.float32)
    parts = jnp.concatenate([high, mid, rest - mid, jnp.zeros_like(rows)], axis=0)
    sums = mm(parts.astype(jnp.bfloat16), member)
    return sums[0:8] + sums[8:16] + sums[16:24]


def fold(values):
    rows, width = values.shape
    return jnp.sum(values.reshape(rows // 8, 8, width), axis=0)


def two_rows(first, second):
    first = jnp.sum(first, axis=0, keepdims=True)
    second = jnp.sum(second, axis=0, keepdims=True)
    row = lax.broadcasted_iota(jnp.int32, (8, first.shape[1]), 0)
    return jnp.where(row == 0, first, jnp.where(row == 1, second, 0.0))


def chunks(total, size, step, init):
    return lax.fori_loop(0, total // size, lambda m, c: step(pl.multiple_of(m * size, size), c), init)


def norm_sums(load, pixels, channels, member, size):
    def step(at, carry):
        values = load(at)
        return (carry[0] + fold(values), carry[1] + fold(values * values))

    zero = jnp.zeros((8, channels), jnp.float32)
    first, second = chunks(pixels, size, step, (zero, zero))
    count = pixels * (channels // GROUPS)
    sums = group_total(two_rows(first, second), member) / count
    mean = sums[0:1]
    inverse = lax.rsqrt(sums[1:2] - mean * mean + EPS_NORM)
    return mean, inverse


CHUNK = 1024
PART = 256


def attention_kernel(parts, places, scalars, middle, *refs):
    attention_body(places, scalars, middle, refs[:parts], *refs[parts:])


def attention_body(
    places,
    scalars,
    middle,
    strips,
    gains,
    member,
    qkv_w,
    out_w,
    order,
    down_out,
    shares,
    sums_out,
    loss_out,
    noise,
    qkv_wt,
    normed,
    qkv_t,
    probs,
    totals,
    mixed_t,
    attn_t,
    result,
    grad_b,
    back_t,
    dqkv_t,
    gn_t,
    qkv_acc,
    out_acc,
):
    sample = pl.program_id(0)
    _, pixels, channels = middle.shape
    half = channels // 2
    size = channels // HEADS
    factor = size ** (-0.5)
    width = int(round(pixels**0.5))

    @pl.when(sample == 0)
    def _():
        qkv_wt[...] = qkv_w[...].T
        qkv_acc[...] = jnp.zeros_like(qkv_acc)
        out_acc[...] = jnp.zeros_like(out_acc)

    join_strips(places, strips, noise)
    load = lambda at: middle[0, pl.ds(at, PART), :]
    mean, inverse = norm_sums(load, pixels, channels, member[...], PART)
    gain, shift = gains[4:5], gains[5:6]

    def normalize(at, carry):
        hat = (load(at) - mean) * inverse
        normed[pl.ds(at, PART), :] = (hat * gain + shift).astype(jnp.bfloat16)
        return carry

    chunks(pixels, PART, normalize, 0)

    block = 256

    qkv_t[...] = mm(qkv_wt[...], normed[...], NT).astype(jnp.bfloat16)

    def rows_of_head(head, part):
        at = (3 * head + part) * size
        return slice(at, at + size)

    def scores_of(head):
        return mm(qkv_t[rows_of_head(head, 1), :].T, qkv_t[rows_of_head(head, 0), :])

    following = scores_of(0)
    for head in range(HEADS):
        scores = following
        if head + 1 < HEADS:
            following = scores_of(head + 1)
        top = jnp.max(scores, axis=0, keepdims=True)
        powers = jnp.exp2((scores - top) * (factor * LOG2E))
        inv = 1.0 / jnp.sum(powers, axis=0, keepdims=True)
        powers_b = powers.astype(jnp.bfloat16)
        probs[head] = powers_b
        totals[head] = jnp.broadcast_to(inv, (8, pixels))
        mixed = mm(qkv_t[rows_of_head(head, 2), :], powers_b) * inv
        at = slice(head * size, (head + 1) * size)
        mixed_t[at, :] = mixed
        attn_t[at, :] = mixed.astype(jnp.bfloat16)

    result[...] = mm(attn_t[...].T, out_w[...])
    beta_log, tilde_log, coef = scalars[sample, 0], scalars[sample, 1], scalars[sample, 2]
    divisor, high, wide = scalars[sample, 3], scalars[sample, 4], scalars[sample, 5]

    def losses(at, carry):
        total = load(at) + result[pl.ds(at, PART), :]
        pixel = at + lax.broadcasted_iota(jnp.int32, (PART, half), 0)
        row = (pixel // width).astype(jnp.float32)
        col = (pixel % width).astype(jnp.float32)
        valid = jnp.where((row >= width - high) & (col < wide), 1.0, 0.0)
        residue = total[:, :half] - noise[pl.ds(at, PART), :].astype(jnp.float32)
        weight = jax.nn.sigmoid(total[:, half:])
        blended = weight * beta_log + (1.0 - weight) * tilde_log
        spread = jnp.exp(tilde_log - blended)
        damped = coef * residue * residue * jnp.exp(-blended)
        diverge = 0.5 * (-1.0 + blended - tilde_log + spread + damped)
        pixel_loss = valid * (residue * residue + VLB_WEIGHT * diverge)
        scale = valid / (half * divisor)
        grad_guess = 2.0 * residue * scale
        grad_raw = (
            scale * (0.5 * VLB_WEIGHT) * (1.0 - spread - damped)
            * (beta_log - tilde_log) * weight * (1.0 - weight)
        )
        grad = jnp.concatenate([grad_guess, grad_raw], axis=-1)
        result[pl.ds(at, PART), :] = grad
        grad_b[pl.ds(at, PART), :] = grad.astype(jnp.bfloat16)
        return carry + fold(pixel_loss)

    loss = chunks(pixels, PART, losses, jnp.zeros((8, half), jnp.float32))
    loss_out[0] = loss * (1.0 / half)

    out_acc[...] += mm(attn_t[...], grad_b[...])
    back_t[...] = mm(out_w[...], grad_b[...], NT).astype(jnp.bfloat16)

    def upstream_of(head):
        return back_t[head * size : (head + 1) * size, :]

    def soft_grad(head):
        return mm(qkv_t[rows_of_head(head, 2), :].T, upstream_of(head))

    following = soft_grad(0)
    for head in range(HEADS):
        grad_soft = following
        if head + 1 < HEADS:
            following = soft_grad(head + 1)
        upstream = upstream_of(head)
        inner = jnp.sum(
            upstream.astype(jnp.float32) * mixed_t[head * size : (head + 1) * size, :],
            axis=0,
            keepdims=True,
        )
        soft = probs[head].astype(jnp.float32) * totals[head, 0:1]
        grad_scores = (soft * (grad_soft - inner)).astype(jnp.bfloat16)
        queries_t, keys_t = qkv_t[rows_of_head(head, 0), :], qkv_t[rows_of_head(head, 1), :]
        dqkv_t[rows_of_head(head, 0), :] = (mm(keys_t, grad_scores) * factor).astype(jnp.bfloat16)
        dqkv_t[rows_of_head(head, 1), :] = (mm(queries_t, grad_scores, NT) * factor).astype(jnp.bfloat16)
        dqkv_t[rows_of_head(head, 2), :] = mm(upstream, soft.astype(jnp.bfloat16), NT).astype(jnp.bfloat16)

    qkv_acc[...] += mm(normed[...].T, dqkv_t[...], NT)
    gn_t[...] = mm(qkv_w[...], dqkv_t[...]).T

    def back_sums(at, carry):
        hat = (load(at) - mean) * inverse
        grad = gn_t[pl.ds(at, PART), :]
        return (carry[0] + fold(grad * hat), carry[1] + fold(grad))

    zero = jnp.zeros((8, channels), jnp.float32)
    both = chunks(pixels, PART, back_sums, (zero, zero))
    rows = two_rows(*both)
    sums_out[0] = rows
    means = group_total(rows * gain, member[...]) / (pixels * (channels // GROUPS))

    def back_norm(at, carry):
        hat = (load(at) - mean) * inverse
        grad = gn_t[pl.ds(at, PART), :] * gain
        back = (grad - means[1:2] - hat * means[0:1]) * inverse
        down_out[0, pl.ds(at, PART), :] = (result[pl.ds(at, PART), :] + back).astype(jnp.bfloat16)
        return carry

    chunks(pixels, PART, back_norm, 0)

    @pl.when(sample == pl.num_programs(0) - 1)
    def _():
        wide = 3 * channels
        shares[:, 0:wide] = mm(order[...], qkv_acc[...].astype(jnp.bfloat16)).astype(jnp.bfloat16)
        shares[:, wide:] = mm(order[...], out_acc[...].astype(jnp.bfloat16)).astype(jnp.bfloat16)


def attention_block(places, scalars, middle, strips, gains, member, qkv_w, out_w, order):
    parts = len(strips)
    samples, pixels, channels = middle.shape
    half = channels // 2
    bf, f32 = jnp.bfloat16, jnp.float32
    return pl.pallas_call(
        functools.partial(attention_kernel, parts),
        grid=(samples,),
        in_specs=[
            pl.BlockSpec(memory_space=pltpu.SMEM),
            pl.BlockSpec(memory_space=pltpu.SMEM),
            each(pixels, channels),
            *[each(pixels // parts, half)] * parts,
            whole(8, channels),
            whole(channels, channels),
            whole(channels, 3 * channels),
            whole(channels, channels),
            whole(channels, channels),
        ],
        out_specs=[
            each(pixels, channels),
            whole(channels, 4 * channels),
            each(8, channels),
            each(8, half),
        ],
        out_shape=[
            jax.ShapeDtypeStruct((samples, pixels, channels), bf),
            jax.ShapeDtypeStruct((channels, 4 * channels), bf),
            jax.ShapeDtypeStruct((samples, 8, channels), f32),
            jax.ShapeDtypeStruct((samples, 8, half), f32),
        ],
        scratch_shapes=[
            pltpu.VMEM((pixels, half), bf),
            pltpu.VMEM((3 * channels, channels), bf),
            pltpu.VMEM((pixels, channels), bf),
            pltpu.VMEM((3 * channels, pixels), bf),
            pltpu.VMEM((HEADS, pixels, pixels), bf),
            pltpu.VMEM((HEADS, 8, pixels), f32),
            pltpu.VMEM((channels, pixels), f32),
            pltpu.VMEM((channels, pixels), bf),
            pltpu.VMEM((pixels, channels), f32),
            pltpu.VMEM((pixels, channels), bf),
            pltpu.VMEM((channels, pixels), bf),
            pltpu.VMEM((3 * channels, pixels), bf),
            pltpu.VMEM((pixels, channels), f32),
            pltpu.VMEM((channels, 3 * channels), f32),
            pltpu.VMEM((channels, channels), f32),
        ],
        compiler_params=pltpu.CompilerParams(vmem_limit_bytes=VMEM_LIMIT),
        cost_estimate=pl.CostEstimate(
            flops=30 * samples * pixels * pixels * channels,
            bytes_accessed=8 * samples * pixels * channels,
            transcendentals=samples * HEADS * pixels * pixels,
        ),
    )(places, scalars, middle, *strips, gains, member, qkv_w, out_w, order)


def fill(padded, at, values, width):
    rows, channels = values.shape
    col = lax.broadcasted_iota(jnp.int32, values.shape, 0) % width
    there = pl.ds(at + width, rows)
    left = jnp.where(col == 0, 0.0, pltpu.roll(values, 1, 0))
    right = jnp.where(col == width - 1, 0.0, pltpu.roll(values, rows - 1, 0))
    padded[there, 0:channels] = left.astype(jnp.bfloat16)
    padded[there, channels : 2 * channels] = values.astype(jnp.bfloat16)
    padded[there, 2 * channels :] = right.astype(jnp.bfloat16)


def clear_edges(padded, width):
    rows, wide = padded.shape
    padded[0:width, :] = jnp.zeros((width, wide), jnp.bfloat16)
    padded[rows - width :, :] = jnp.zeros((width, wide), jnp.bfloat16)


def side(pixels):
    return int(round(pixels**0.5))


def taps_product(padded, weight, pixels, width):
    wide = padded.shape[1]
    total = mm(padded[0:pixels, :], weight(0))
    for i in (1, 2):
        total += mm(padded[i * width : i * width + pixels, :], weight(i))
    return total


def rows_of(*rows):
    index = lax.broadcasted_iota(jnp.int32, (8, rows[0].shape[1]), 0)
    total = jnp.zeros(index.shape, jnp.float32)
    for place, row in enumerate(rows):
        total = jnp.where(index == place, row, total)
    return total


def join_strips(places, strips, joined):
    rows = strips[0].shape[1]
    for far, strip in enumerate(strips):
        joined[pl.ds(pl.multiple_of(places[far] * rows, rows), rows), :] = strip[0]


def join_weights(last, pieces, weight):
    if len(pieces) == 1:
        weight[...] = pieces[0][...]
        return
    rows = weight.shape[0] // (2 * pieces[0].shape[0])
    for low in range(2):

        @pl.when(last[0] == low)
        def _():
            for k in range(pieces[0].shape[0]):
                both = [pieces[low ^ half][k, 0:rows, :].astype(jnp.float32) for half in range(2)]
                pair = jnp.concatenate(both, axis=0).astype(jnp.bfloat16)
                weight[2 * rows * k : 2 * rows * (k + 1), :] = pair


def first_kernel(parts, count, places, last, *refs):
    strips, pieces, refs = refs[:parts], refs[parts : parts + count], refs[parts + count :]
    gains, member, inner, hidden, stats, images, weight, padded = refs
    _, pixels, channels = images.shape

    @pl.when(pl.program_id(0) == 0)
    def _():
        join_weights(last, pieces, weight)

    join_strips(places, strips, images.at[0])
    width = side(pixels)
    wide = 3 * channels
    load = lambda at: images[0, pl.ds(at, CHUNK), :].astype(jnp.float32)
    mean, inverse = norm_sums(load, pixels, channels, member[...], CHUNK)
    gain, shift = gains[0:1], gains[1:2]
    clear_edges(padded, width)

    def activate(at, carry):
        out = (load(at) - mean) * inverse * gain + shift
        value = out * jax.nn.sigmoid(out)
        hidden[0, pl.ds(at, CHUNK), :] = value.astype(jnp.bfloat16)
        fill(padded, at, value, width)
        return carry

    chunks(pixels, CHUNK, activate, 0)
    inner[0] = taps_product(padded, lambda i: weight[i * wide : (i + 1) * wide, :], pixels, width)
    mean_two, inverse_two = norm_sums(
        lambda at: inner[0, pl.ds(at, CHUNK), :], pixels, channels, member[...], CHUNK
    )
    stats[0] = rows_of(mean, inverse, mean_two, inverse_two)


def second_kernel(count, last, *refs):
    pieces, refs = refs[:count], refs[count:]
    inner, images, stats, film, gains, middle, hidden, weight, padded = refs
    _, pixels, channels = inner.shape

    @pl.when(pl.program_id(0) == 0)
    def _():
        join_weights(last, pieces, weight)

    width = side(pixels)
    wide = 3 * channels
    mean, inverse = stats[0, 2:3], stats[0, 3:4]
    scale, lift = 1.0 + film[0, 0:1], film[0, 1:2]
    gain, shift = gains[2:3], gains[3:4]
    clear_edges(padded, width)

    def activate(at, carry):
        out = (inner[0, pl.ds(at, CHUNK), :] - mean) * inverse * gain + shift
        lifted = out * scale + lift
        value = lifted * jax.nn.sigmoid(lifted)
        hidden[0, pl.ds(at, CHUNK), :] = value.astype(jnp.bfloat16)
        fill(padded, at, value, width)
        return carry

    chunks(pixels, CHUNK, activate, 0)
    middle[0] = images[0].astype(jnp.float32) + taps_product(
        padded, lambda i: weight[i * wide : (i + 1) * wide, :], pixels, width
    )


def weights_sums(hidden, grad, padded, total):
    _, pixels, channels = hidden.shape
    width = side(pixels)
    wide = 3 * channels
    clear_edges(padded, width)

    def spread(at, carry):
        fill(padded, at, hidden[0, pl.ds(at, CHUNK), :].astype(jnp.float32), width)
        return carry

    chunks(pixels, CHUNK, spread, 0)

    @pl.when(pl.program_id(0) == 0)
    def _():
        total[...] = jnp.zeros_like(total)

    for i in range(3):
        total[i * wide : (i + 1) * wide, :] += mm(
            padded[i * width : i * width + pixels, :], grad[0], TN
        )


def weights_kernel(hidden, grad, out, padded, total):
    weights_sums(hidden, grad, padded, total)

    @pl.when(pl.program_id(0) == pl.num_programs(0) - 1)
    def _():
        out[...] = total[...].astype(jnp.bfloat16)


def shares_kernel(extra, place, hidden, grad, *refs):
    others, (mine, theirs, padded, total) = refs[:extra], refs[extra:]
    weights_sums(hidden, grad, padded, total)
    classes = mine.shape[0]
    channels = total.shape[1]
    rows = total.shape[0] // (2 * classes)

    @pl.when(pl.program_id(0) == pl.num_programs(0) - 1)
    def _():
        for far in range(classes):
            for last, out in enumerate((mine, theirs)):
                owner = far * 2 + (place[0] ^ last)
                parts = [total[pl.ds(pl.multiple_of(owner * rows, 8), rows), :]]
                for other in others:
                    lines = other.shape[0] // (2 * classes)
                    at = (last * classes + far) * lines
                    for k in range(other.shape[1] // channels):
                        piece = other[at : at + lines, k * channels : (k + 1) * channels]
                        parts.append(piece.astype(jnp.float32))
                out[far] = jnp.concatenate(parts, axis=0).astype(jnp.bfloat16)


def turn_taps(weight, turned):
    channels = weight.shape[1]
    for i in range(3):
        for j in range(3):
            tap = 3 * (2 - i) + 2 - j
            turned[i, :, j * channels : (j + 1) * channels] = weight[
                tap * channels : (tap + 1) * channels, :
            ]


def input_grad(grad, weight, padded, turned, down):
    _, pixels, channels = grad.shape
    width = side(pixels)

    @pl.when(pl.program_id(0) == 0)
    def _():
        turn_taps(weight, turned)

    clear_edges(padded, width)

    def spread(at, carry):
        fill(padded, at, grad[0, pl.ds(at, CHUNK), :].astype(jnp.float32), width)
        return carry

    chunks(pixels, CHUNK, spread, 0)
    total = mm(padded[0:pixels, :], turned[0], NT)
    for i in (1, 2):
        total += mm(padded[i * width : i * width + pixels, :], turned[i], NT)
    down[...] = total


def slope_of(values):
    sig = jax.nn.sigmoid(values)
    return sig * (1.0 + values * (1.0 - sig))


def second_back_kernel(
    grad, inner, stats, film, gains, member, weight, grad_out, sums_out, padded, turned, down
):
    _, pixels, channels = grad.shape
    input_grad(grad, weight, padded, turned, down)
    mean, inverse = stats[0, 2:3], stats[0, 3:4]
    scale, lift = 1.0 + film[0, 0:1], film[0, 1:2]
    gain, shift = gains[2:3], gains[3:4]

    def slopes(at, carry):
        hat = (inner[0, pl.ds(at, CHUNK), :] - mean) * inverse
        lifted = (hat * gain + shift) * scale + lift
        lifted_grad = down[pl.ds(at, CHUNK), :] * slope_of(lifted)
        down[pl.ds(at, CHUNK), :] = lifted_grad
        return (carry[0] + fold(lifted_grad * hat), carry[1] + fold(lifted_grad))

    zero = jnp.zeros((8, channels), jnp.float32)
    rows = two_rows(*chunks(pixels, CHUNK, slopes, (zero, zero)))
    sums_out[0] = rows
    factor = scale * gain
    means = group_total(rows * factor, member[...]) / (pixels * (channels // GROUPS))

    def back_norm(at, carry):
        hat = (inner[0, pl.ds(at, CHUNK), :] - mean) * inverse
        back = (down[pl.ds(at, CHUNK), :] * factor - means[1:2] - hat * means[0:1]) * inverse
        grad_out[0, pl.ds(at, CHUNK), :] = back.astype(jnp.bfloat16)
        return carry

    chunks(pixels, CHUNK, back_norm, 0)


def first_back_kernel(grad, images, stats, gains, weight, sums_out, padded, turned, down):
    _, pixels, channels = grad.shape
    input_grad(grad, weight, padded, turned, down)
    mean, inverse = stats[0, 0:1], stats[0, 1:2]
    gain, shift = gains[0:1], gains[1:2]

    def slopes(at, carry):
        hat = (images[0, pl.ds(at, CHUNK), :].astype(jnp.float32) - mean) * inverse
        grad_first = down[pl.ds(at, CHUNK), :] * slope_of(hat * gain + shift)
        return (carry[0] + fold(grad_first * hat), carry[1] + fold(grad_first))

    zero = jnp.zeros((8, channels), jnp.float32)
    sums_out[0] = two_rows(*chunks(pixels, CHUNK, slopes, (zero, zero)))


def whole(*shape):
    return pl.BlockSpec(shape, lambda s: (0,) * len(shape))


def each(*shape):
    return pl.BlockSpec((1,) + shape, lambda s: (s,) + (0,) * len(shape))


def per_sample(kernel, samples, in_specs, outs, scratch, flops, *operands):
    return pl.pallas_call(
        kernel,
        grid=(samples,),
        in_specs=in_specs,
        out_specs=[spec for spec, _ in outs],
        out_shape=[shape for _, shape in outs],
        scratch_shapes=scratch,
        compiler_params=pltpu.CompilerParams(vmem_limit_bytes=VMEM_LIMIT),
        cost_estimate=pl.CostEstimate(flops=flops, bytes_accessed=flops // 1000, transcendentals=0),
    )(*operands)


def sized(dtype, *shape):
    return jax.ShapeDtypeStruct(shape, dtype)


def block_calls(samples, pixels, channels):
    width = side(pixels)
    act = each(pixels, channels)
    few = each(8, channels)
    gain_spec, member_spec = whole(8, channels), whole(channels, channels)
    weight_spec = whole(9 * channels, channels)
    bf, f32 = jnp.bfloat16, jnp.float32
    padded = pltpu.VMEM((pixels + 2 * width, 3 * channels), bf)
    turned = pltpu.VMEM((3, channels, 3 * channels), bf)
    down = pltpu.VMEM((pixels, channels), f32)
    act_b = sized(bf, samples, pixels, channels)
    act_f = sized(f32, samples, pixels, channels)
    few_f = sized(f32, samples, 8, channels)
    flops = 18 * samples * pixels * channels * channels

    weight_out = (weight_spec, sized(bf, 9 * channels, channels))
    smem = pl.BlockSpec(memory_space=pltpu.SMEM)

    def first(places, last, strips, pieces, gains, member):
        parts, count = len(strips), len(pieces)
        return per_sample(
            functools.partial(first_kernel, parts, count), samples,
            [smem, smem] + [each(pixels // parts, channels)] * parts
            + [whole(*piece.shape) for piece in pieces] + [gain_spec, member_spec],
            [(act, act_f), (act, act_b), (few, few_f), (act, act_b), weight_out], [padded], flops,
            places, last, *strips, *pieces, gains, member,
        )

    def second(last, pieces, inner, images, stats, film, gains):
        return per_sample(
            functools.partial(second_kernel, len(pieces)), samples,
            [smem] + [whole(*piece.shape) for piece in pieces] + [act, act, few, few, gain_spec],
            [(act, act_f), (act, act_b), weight_out], [padded], flops,
            last, *pieces, inner, images, stats, film, gains,
        )

    def weights(hidden, grad, place, classes, others=()):
        scratch = [padded, pltpu.VMEM((9 * channels, channels), f32)]
        conv_rows = 9 * channels // (2 * classes)
        more = [other.shape[0] * other.shape[1] // (2 * classes * channels) for other in others]
        if conv_rows % 8:
            (whole_grad,) = per_sample(
                weights_kernel, samples, [act, act],
                [(weight_spec, sized(bf, 9 * channels, channels))], scratch, flops, hidden, grad,
            )
            blocks = whole_grad.reshape(2 * classes, conv_rows, channels)
            both = []
            for last in range(2):
                owner = place[0] ^ last
                cut = blocks.reshape(classes, 2, conv_rows, channels)
                parts = [lax.dynamic_index_in_dim(cut, owner, 1, keepdims=False)]
                for other in others:
                    cut = other.reshape(2, classes, -1, other.shape[1] // channels, channels)[last]
                    parts.append(jnp.moveaxis(cut, 2, 1).reshape(classes, -1, channels))
                both.append(jnp.concatenate(parts, axis=1))
            return both
        shape = (classes, conv_rows + sum(more), channels)
        out = (whole(*shape), sized(bf, *shape))
        return per_sample(
            functools.partial(shares_kernel, len(others)), samples,
            [pl.BlockSpec(memory_space=pltpu.SMEM), act, act] + [whole(*o.shape) for o in others],
            [out, out], scratch, flops, place, hidden, grad, *others,
        )

    def second_back(grad, inner, stats, film, gains, member, weight):
        return per_sample(
            second_back_kernel, samples,
            [act, act, few, few, gain_spec, member_spec, weight_spec],
            [(act, act_b), (few, few_f)], [padded, turned, down], flops,
            grad, inner, stats, film, gains, member, weight,
        )

    def first_back(grad, images, stats, gains, weight):
        return per_sample(
            first_back_kernel, samples, [act, act, few, gain_spec, weight_spec],
            [(few, few_f)], [padded, turned, down], flops,
            grad, images, stats, gains, weight,
        )[0]

    return first, second, weights, second_back, first_back


def adamw(master, gradient, first, second, step_rate, decay_rate, clip_factor):
    gradient = gradient * clip_factor
    first_new = BETA_ONE * first + (1.0 - BETA_ONE) * gradient
    second_new = BETA_TWO * second + (1.0 - BETA_TWO) * gradient * gradient
    ratio = (
        first_new
        / (1.0 - BETA_ONE**STEP)
        / (jnp.sqrt(second_new / (1.0 - BETA_TWO**STEP)) + ADAM_EPS)
    )
    return (master - step_rate * (ratio + decay_rate * master), first_new, second_new)


def body(
    images,
    noise,
    timesteps,
    extents,
    film_master,
    conv_master,
    qkv_master,
    out_master,
    gains,
    film_first,
    film_second,
    conv_first,
    conv_second,
    qkv_first,
    qkv_second,
    out_first,
    out_second,
    gain_first,
    gain_second,
):
    devices = lax.axis_size("dp") * lax.axis_size("head")
    device = lax.axis_index("dp") * lax.axis_size("head") + lax.axis_index("head")
    channels = images.shape[-1]
    wide = film_master.shape[1]
    half_width = channels // 2
    conv_rows = conv_master.shape[0]
    film_rows = film_master.shape[0]
    out_rows = out_master.shape[0]

    local_samples = timesteps.shape[0]
    small = jnp.concatenate(
        [
            lax.reduce_precision(gains.reshape(-1), 8, 7),
            extents.astype(jnp.float32).reshape(-1),
            timesteps.astype(jnp.float32),
        ]
    )
    small = jnp.pad(small, (0, -small.shape[0] % 128))
    smalls = to_all(jnp.broadcast_to(small[None, None], (devices, 1, small.shape[0])))
    classes = class_count()
    top_mask = devices // 2
    is_top = device >= top_mask
    ours = conv_master.astype(jnp.bfloat16)
    theirs = exchange(ours, top_mask)
    strips = strips_of(images)
    low, high = jnp.where(is_top, theirs, ours), jnp.where(is_top, ours, theirs)
    every_one = gather_classes(behind(low, smalls, *strips))
    rest = jnp.concatenate([qkv_master.reshape(-1, channels), out_master]).astype(jnp.bfloat16)
    rest = behind(rest, theirs)
    rest_two = pair_up(rest, exchange(rest, top_mask), jnp.logical_not(is_top), 0)
    smalls = smalls.reshape(devices, -1)
    gain_f = smalls[:, : gains.size].reshape(channels, 6)
    dp_smalls = smalls.reshape(lax.axis_size("dp"), lax.axis_size("head"), -1)[:, 0, gains.size :]
    extents_all = dp_smalls[:, : 2 * local_samples].reshape(-1, 2)
    times_all = dp_smalls[:, 2 * local_samples : 3 * local_samples].reshape(-1).astype(jnp.int32)
    divisor = jnp.sum(extents_all[:, 0] * extents_all[:, 1])

    parts = lax.axis_size("head")
    samples, strip_rows, width_px, _ = strips[0].shape
    places = lax.axis_index("head") ^ jnp.arange(parts, dtype=jnp.int32)
    rows = strip_rows * parts
    pixels = rows * width_px
    first = lax.axis_index("head") * samples
    own_times = lax.dynamic_slice_in_dim(timesteps, first, samples)
    own_extents = lax.dynamic_slice_in_dim(extents, first, samples)

    log_beta, log_tilde, factor = plan(own_times)
    embedded_all = jax.nn.silu(embed(times_all, wide)).astype(jnp.bfloat16)
    film_rows_out = lax.dot_general(
        film_master.astype(jnp.bfloat16),
        embedded_all,
        (((1,), (1,)), ((), ())),
        preferred_element_type=jnp.float32,
    )
    film_flat = film_rows_out.T.reshape(-1, channels)
    film_high = lax.reduce_precision(film_flat, 8, 7)
    film_parts = jnp.concatenate([film_high, film_flat - film_high]).astype(jnp.bfloat16)
    film_lines = film_flat.shape[0]
    film_two = pair_up(film_parts, exchange(film_parts, top_mask), jnp.logical_not(is_top), 0)
    two_block = jnp.concatenate(
        [high, rest_two.reshape(-1, channels), film_two.reshape(-1, channels)]
    )
    mine = lax.axis_index("head")
    own_count = noise.shape[0] // lax.axis_size("head")
    noise_cuts = [
        lax.dynamic_slice_in_dim(noise, (mine ^ far) * own_count, own_count, axis=0)
        for far in range(lax.axis_size("head"))
    ]
    every_two = gather_classes(behind(two_block, every_one, *noise_cuts))
    gain_gate = two_block
    gains_t = behind(jnp.pad(gain_f.T, ((0, 2), (0, 0))), gain_gate)
    member = jnp.asarray(np.kron(np.eye(GROUPS), np.ones((channels // GROUPS,) * 2)), jnp.bfloat16)
    scalars = jnp.stack(
        [log_beta, log_tilde, factor, jnp.broadcast_to(divisor, factor.shape)]
        + [own_extents[:, 0].astype(jnp.float32), own_extents[:, 1].astype(jnp.float32)],
        axis=1,
    )
    first_call, second_call, weights, second_back, first_back = block_calls(samples, pixels, channels)
    flat = lambda values: [v.reshape(samples, strip_rows * width_px, -1) for v in values]
    place = last_bit().reshape(1).astype(jnp.int32)
    pieces_one = conv_pieces(every_one, exchange(every_one, 1), conv_rows)
    inner, hidden_one, stats, source, taps_one = first_call(
        places, place, flat(strips), pieces_one, gains_t, member
    )
    every_two = behind(every_two, inner)
    other_two = exchange(every_two, 1)
    pieces_two = conv_pieces(every_two, other_two, conv_rows)
    film_at = conv_rows + 8 * out_rows
    first_own = lax.axis_index("dp") * local_samples + first
    line, spot = first_own * film_rows // channels, first_own * film_rows % channels
    film_got = pair_up(every_two[:, film_at:], other_two[:, film_at:], last_bit() == 0, 1)
    film_got = film_got.reshape(classes, 2, 2, 2, film_lines, channels)
    film_got = lax.dynamic_slice(
        film_got, (0, 0, 0, 0, line, spot), film_got.shape[:4] + (1, samples * film_rows)
    ).astype(jnp.float32)
    film_got = jnp.sum(film_got, axis=(3, 4)).reshape(classes, 2, 2, samples, film_rows)
    film_out = film_got.transpose(3, 2, 0, 1, 4).reshape(samples, devices * film_rows)
    noise_strips = strips_of(noise, [behind(cut, other_two) for cut in noise_cuts])
    film = jnp.pad(film_out.reshape(samples, 2, channels), ((0, 0), (0, 6), (0, 0)))
    scale = 1.0 + film_out[:, :channels]
    middle, hidden_two, taps_two = second_call(
        place, pieces_two, inner, source, stats, film, gains_t
    )
    others = pair_up(every_two[:, conv_rows:film_at], other_two[:, conv_rows:film_at], last_bit() == 0, 1)
    others = jnp.moveaxis(others.reshape(-1, 2, 4 * out_rows, channels), 0, 1)
    others = others.reshape(devices, 4 * out_rows, channels)
    qkv_w = others[:, : 3 * out_rows].reshape(channels, 3 * channels)
    out_w = others[:, 3 * out_rows :].reshape(channels, channels)
    my_last = last_bit()
    line = jnp.arange(channels, dtype=jnp.int32)
    owner, spot = line // out_rows, line % out_rows
    source_device = (
        (owner % 2) * 2 * classes + (owner // 2 % classes) * 2 + (my_last ^ (owner // (2 * classes)))
    )
    order = (line[None, :] == (source_device * out_rows + spot)[:, None]).astype(jnp.bfloat16)
    grad_two_b, shares, sums_three, losses = attention_block(
        places, scalars, middle, flat(noise_strips), gains_t, member, qkv_w, out_w, order
    )
    loss_local = jnp.sum(losses)
    two_shares = weights(hidden_two, grad_two_b, place, classes, (shares,))
    grad_two_b = behind(grad_two_b, *two_shares)
    grad_one_b, sums_two = second_back(grad_two_b, inner, stats, film, gains_t, member, taps_two)
    two_sent = (two_shares[0].astype(jnp.float32) + exchange(two_shares[1], 1).astype(jnp.float32)).astype(jnp.bfloat16)
    share_two = jnp.sum(across_classes(two_sent).astype(jnp.float32), axis=0)
    one_shares = weights(behind(hidden_one, two_sent), grad_one_b, place, classes)
    one_sent = (one_shares[0].astype(jnp.float32) + exchange(one_shares[1], 1).astype(jnp.float32)).astype(jnp.bfloat16)
    share_one = jnp.sum(across_classes(one_sent).astype(jnp.float32), axis=0)
    grad_one_b = behind(grad_one_b, share_two, one_sent)
    sums_one = first_back(grad_one_b, source, stats, gains_t, taps_one)
    gain_one, bias_one = jnp.sum(sums_one[:, 0], axis=0), jnp.sum(sums_one[:, 1], axis=0)
    gain_two, bias_two = jnp.sum(sums_two[:, 0] * scale, axis=0), jnp.sum(sums_two[:, 1] * scale, axis=0)
    gain_three, bias_three = jnp.sum(sums_three[:, 0], axis=0), jnp.sum(sums_three[:, 1], axis=0)
    grad_scale = sums_two[:, 0] * gains_t[2] + sums_two[:, 1] * gains_t[3]
    film_grad_b = jnp.concatenate([grad_scale, sums_two[:, 1]], axis=1).astype(jnp.bfloat16)

    small_shares = share_two[conv_rows:].reshape(4, 2, out_rows, channels)
    keep_two = jnp.where(is_top, small_shares[:, 1], small_shares[:, 0])
    send_two = jnp.where(is_top, small_shares[:, 0], small_shares[:, 1])
    send_two = jnp.concatenate([share_two[:conv_rows], send_two.reshape(-1, channels)])
    got_two = exchange(send_two.astype(jnp.bfloat16), top_mask).astype(jnp.float32)
    one_low = share_one.astype(jnp.bfloat16)
    got_one = exchange(one_low, top_mask).astype(jnp.float32)
    conv_g = jnp.where(is_top, share_two[:conv_rows] + got_two[:conv_rows], share_one + got_one)
    small_g = keep_two + got_two[conv_rows:].reshape(keep_two.shape)
    qkv_g = jnp.concatenate([small_g[0], small_g[1], small_g[2]], axis=1)
    out_g = small_g[3]

    gain_grad = jnp.stack([gain_one, bias_one, gain_two, bias_two, gain_three, bias_three], axis=1)
    film_sent = jnp.moveaxis(film_grad_b.astype(jnp.float32).reshape(samples, devices, film_rows), 1, 0)
    parcel = jnp.concatenate(
        [
            film_sent.reshape(devices, -1),
            behind(gain_grad, one_low).reshape(devices, -1),
            jnp.broadcast_to(loss_local, (devices, 1)),
        ],
        axis=1,
    )
    length = parcel.shape[1]
    parcel = jnp.pad(parcel, ((0, 0), (0, -length % 128)))
    parcels = to_all(parcel[:, None]).reshape(devices, -1)
    film_size = samples * film_rows
    film_own = parcels[:, :film_size].reshape(-1, film_rows)
    gain_g = jnp.sum(parcels[:, film_size : length - 1], axis=0).reshape(gains.shape)
    loss_total = jnp.sum(parcels[:, length - 1])
    film_g = jnp.einsum(
        "sf,se->fe", film_own.astype(jnp.bfloat16), embedded_all, preferred_element_type=jnp.float32
    )
    reduced = (film_g, conv_g, qkv_g, out_g, gain_g)
    squares = jnp.zeros((), jnp.float32)
    for gradient in reduced:
        squares = squares + jnp.sum(gradient * gradient)
    grad_norm = jnp.sqrt(jnp.sum(to_all(jnp.broadcast_to(squares, (devices, 8, 128)))[:, 0, 0]))
    clip_factor = jnp.minimum(1.0, THRESHOLD / (grad_norm + 1e-06))
    film_res = adamw(film_master, film_g, film_first, film_second, RATE_MATRIX, DECAY, clip_factor)
    conv_res = adamw(conv_master, conv_g, conv_first, conv_second, RATE_MATRIX, DECAY, clip_factor)
    qkv_res = adamw(qkv_master, qkv_g, qkv_first, qkv_second, RATE_MATRIX, DECAY, clip_factor)
    out_res = adamw(out_master, out_g, out_first, out_second, RATE_MATRIX, DECAY, clip_factor)
    gain_res = adamw(gains, gain_g, gain_first, gain_second, RATE_GAIN, 0.0, clip_factor)
    loss_parts = jnp.stack([loss_total, divisor])
    return (
        loss_parts,
        grad_norm,
        film_res[0],
        film_res[1],
        film_res[2],
        conv_res[0],
        conv_res[1],
        conv_res[2],
        qkv_res[0],
        qkv_res[1],
        qkv_res[2],
        out_res[0],
        out_res[1],
        out_res[2],
        gain_res[0],
        gain_res[1],
        gain_res[2],
    )


def solution(mesh):
    in_specs = (
        P("dp", "head", None, None),
        P("dp", "head", None, None),
        P("dp"),
        P("dp", None),
        P(("dp", "head"), None),
        P(("dp", "head"), None),
        P(("dp", "head"), None),
        P(("dp", "head"), None),
        P(("dp", "head"), None),
        P(("dp", "head"), None),
        P(("dp", "head"), None),
        P(("dp", "head"), None),
        P(("dp", "head"), None),
        P(("dp", "head"), None),
        P(("dp", "head"), None),
        P(("dp", "head"), None),
        P(("dp", "head"), None),
        P(("dp", "head"), None),
        P(("dp", "head"), None),
    )
    out_specs = (
        P(),
        P(),
        P(("dp", "head"), None),
        P(("dp", "head"), None),
        P(("dp", "head"), None),
        P(("dp", "head"), None),
        P(("dp", "head"), None),
        P(("dp", "head"), None),
        P(("dp", "head"), None),
        P(("dp", "head"), None),
        P(("dp", "head"), None),
        P(("dp", "head"), None),
        P(("dp", "head"), None),
        P(("dp", "head"), None),
        P(("dp", "head"), None),
        P(("dp", "head"), None),
        P(("dp", "head"), None),
    )
    return jax.shard_map(body, mesh=mesh, in_specs=in_specs, out_specs=out_specs, check_vma=False)
```
